128 devices in a mesh: replica: 8 (over x, y_lo), tensor: 16 (over y_hi, z, core).
Axes of the slice: x: 4, y: 4 (y_hi: 2, y_lo: 2; y = y_hi * 2 + y_lo), z: 4, core: 2. Of those that a mesh axis runs over, the one named last changes fastest.
Arguments:
- tokens: bfloat16 [8192, 8192], P(('replica', 'tensor')), may hold values from -16 to 16
- norm_gain: float32 [8192], replicated, may hold values from 0.5 to 1.5
- query_weight: bfloat16 [8192, 8192], P(None, 'tensor'), may hold values from -0.5 to 0.5
- kv_weight: bfloat16 [8192, 2048], P(None, 'tensor'), may hold values from -0.5 to 0.5
- out_weight: bfloat16 [8192, 8192], P('tensor'), may hold values from -0.5 to 0.5
- pseudo_grad: bfloat16 [8, 8192, 1024], P('replica', 'tensor'), may hold values from -6 to 6
- grad_exps: int32 [8, 8192, 8], P('replica', 'tensor'), may hold values from -2 to 1
- params: bfloat16 [8192, 1024], P('tensor'), may hold values from -4 to 4
- momentum: float32 [8192, 1024], P('tensor', 'replica'), may hold values from -4 to 4
Outputs:
- attended: bfloat16 [8192, 8192], P(('replica', 'tensor'))
- new_params: bfloat16 [8192, 1024], P('tensor')
- new_momentum: float32 [8192, 1024], P('tensor', 'replica')
The draws below stay inside these ranges and needn't reach their ends.
All inputs are finite; a program needn't handle non-finite values. Where the reference program divides by a largest or mean magnitude, that divisor is 1e-20 or more.
Results may differ from the reference program's by a relative error of at most 0.019.
Values may be sent and summed in bfloat16 or wider, within the bound.
No kernel may reach another device: no remote copies, remote signals or barrier semaphores. Data moves between devices by JAX's collectives and lax.ppermute only.
A program may use at most 128 MiB of HBM per device.

```python
import math
import jax
import jax.numpy as jnp
from jax import lax

D = 8192
HEAD_DIM = 128
HEADS_DEV = 4
HEADS = 64
KV_HEADS = 8
FRAG = 1024
HBLOCK = 128
TOK = 1024
TOKENS = 8192
REPLICAS = 8
NBLOCKS = 8
N_REPLICA = 8
N_TENSOR = 16


def draw_tokens(key, part):
    key = jax.random.fold_in(key, 1)
    noise = jax.random.normal(jax.random.fold_in(key, 2), (TOKENS, D), jnp.float32)
    return jnp.clip(noise, -16.0, 16.0).astype(jnp.bfloat16)


def draw_query_weight(key, part):
    key = jax.random.fold_in(key, 4)
    base = jax.random.normal(key, (D, HEADS * HEAD_DIM), jnp.float32) / jnp.sqrt(float(D))
    return jnp.clip(base, -0.5, 0.5).astype(jnp.bfloat16)


def draw_kv_weight(key, part):
    key = jax.random.fold_in(key, 5)
    base = jax.random.normal(key, (D, 2 * KV_HEADS * HEAD_DIM), jnp.float32) / jnp.sqrt(float(D))
    return jnp.clip(base, -0.5, 0.5).astype(jnp.bfloat16)


def with_ends(result, key, smallest, high):
    shape = result.shape
    index_at = [jax.random.randint(jax.random.fold_in(key, axis), (), 0, shape[axis]) for axis in range(len(shape))]
    result = result.at[tuple(index_at)].set(smallest)
    longest = shape.index(max(shape))
    index_at[longest] = (index_at[longest] + 1) % shape[longest]
    return result.at[tuple(index_at)].set(high)


def with_spikes(entries, stream_key, source, target, blocks, factor):
    owner, partner = [(jnp.arange(entries.shape[dim]) // (entries.shape[dim] // blocks)).reshape([-1 if axis == dim else 1 for axis in range(entries.ndim)]) for dim in (source, target)]
    chosen = jax.random.permutation(stream_key, blocks)[partner]
    strong = (owner == chosen) | (owner == (partner + blocks // 2) % blocks)
    return jnp.where(strong, factor * entries, entries)


def block_levels(stream_key, dims, cuts, smallest, high):
    def one(dim, parts):
        heights = jax.random.uniform(jax.random.fold_in(jax.random.fold_in(stream_key, 6), dim), (parts,), jnp.float32, smallest / len(cuts), high / len(cuts))
        return jnp.repeat(jnp.exp(heights), dims[dim] // parts).reshape((-1,) + (1,) * (len(dims) - dim - 1))

    level = one(*cuts[0])
    for cut in cuts[1:]:
        level = level * one(*cut)
    return level


def normal_values(rng, extent, scale, most, split=(), kind=jnp.bfloat16):
    level = block_levels(rng, extent, split, -0.22, 0.18) if split else 1.0
    drawn = jax.random.normal(rng, extent, jnp.float32) * scale * level
    return jnp.minimum(jnp.maximum(drawn, -most), most).astype(kind)


def bell_draw_with(stream_key, dims, scale, bound, pieces, heavy, kind=jnp.bfloat16):
    values = scale * jax.random.normal(stream_key, dims, jnp.float32)
    if pieces:
        values = values * block_levels(stream_key, dims, pieces, -0.22, 0.18)
    return jnp.clip(with_spikes(values, jax.random.fold_in(stream_key, 3), *heavy), -bound, bound).astype(kind)


def setup_inputs(seed: int = 0) -> dict:
    splits = jax.random.split(jax.random.key(seed), 10)
    return {
        "tokens": draw_tokens(jax.random.fold_in(splits[9], 71), 0),
        "norm_gain": jnp.clip(1.0 + 0.1 * jax.random.normal(splits[1], (D,), jnp.float32), 0.5, 1.5),
        "query_weight": draw_query_weight(jax.random.fold_in(splits[9], 71), 0),
        "kv_weight": draw_kv_weight(jax.random.fold_in(splits[9], 71), 0),
        "out_weight": normal_values(splits[4], (HEADS * HEAD_DIM, D), HEAD_DIM ** -0.5, 0.5, ((0, 16),)),
        "pseudo_grad": bell_draw_with(splits[5], (REPLICAS, D, FRAG), 1.0, 6.0, ((0, 8), (1, 16)), (0, 2, 8, 2.0)),
        "grad_exps": with_ends(jax.random.randint(splits[6], (REPLICAS, D, NBLOCKS), -2, 2), jax.random.fold_in(splits[6], 1), -2, 1).astype(jnp.int32),
        "params": normal_values(splits[7], (D, FRAG), 0.5, 4.0, ((0, 16),)),
        "momentum": normal_values(splits[8], (D, FRAG), 0.5, 4.0, ((0, 16), (1, 8)), jnp.float32),
    }


def hadamard_table(width):
    index = jnp.arange(width, dtype=jnp.int32)
    common = jnp.bitwise_and(index[:, None], index[None, :])
    parity = jnp.zeros((width, width), jnp.int32)
    for bit in range(int(math.log2(width))):
        parity = parity + jnp.bitwise_and(jnp.right_shift(common, bit), 1)
    sign = 1.0 - 2.0 * jnp.bitwise_and(parity, 1).astype(jnp.float32)
    return sign / math.sqrt(width)

def rotate(values, table):
    shaped = values.reshape(-1, table.shape[0])
    return jnp.dot(shaped, table, precision=lax.Precision.HIGHEST).reshape(values.shape)

def normalize(rows, gain):
    values = rows.astype(jnp.float32)
    power = lax.optimization_barrier(jnp.mean(values * values, axis=-1, keepdims=True))
    return (values * lax.rsqrt(power + 1e-05) * gain).astype(jnp.bfloat16)

def attend(query, keys, values):
    count = keys.shape[0]
    scores = jnp.einsum('thd,sd->hts', query.astype(jnp.float32), keys.astype(jnp.float32)) * (1.0 / math.sqrt(keys.shape[1]))
    causal = jnp.arange(count)[:, None] >= jnp.arange(count)[None, :]
    scores = jnp.where(causal[None], scores, -jnp.inf)
    peak = lax.optimization_barrier(jnp.max(scores, axis=-1, keepdims=True))
    expo = jnp.exp(scores - peak)
    probs = (expo / lax.optimization_barrier(jnp.sum(expo, axis=-1, keepdims=True))).astype(jnp.bfloat16)
    mixed = jnp.einsum('hts,sd->thd', probs.astype(jnp.float32), values.astype(jnp.float32))
    return mixed.astype(jnp.bfloat16).reshape(count, -1)

def reference(tokens, norm_gain, query_weight, kv_weight, out_weight, pseudo_grad, grad_exps, params, momentum):
    qcols = HEADS_DEV * HEAD_DIM

    def replica_attention(rows):
        normed = normalize(rows, norm_gain)

        def one_group(total, group):
            start = (group * qcols).astype(jnp.int32)
            head = (group // 2).astype(jnp.int32)
            w_query = lax.dynamic_slice_in_dim(query_weight, start, qcols, 1)
            w_pair = lax.dynamic_slice_in_dim(kv_weight, head * 2 * HEAD_DIM, 2 * HEAD_DIM, 1)
            w_out = lax.dynamic_slice_in_dim(out_weight, start, qcols, 0)
            query = jnp.dot(normed, w_query, preferred_element_type=jnp.float32).astype(jnp.bfloat16)
            keys = jnp.dot(normed, w_pair[:, :HEAD_DIM], preferred_element_type=jnp.float32).astype(jnp.bfloat16)
            values = jnp.dot(normed, w_pair[:, HEAD_DIM:], preferred_element_type=jnp.float32).astype(jnp.bfloat16)
            mixed = attend(query.reshape(TOK, HEADS_DEV, HEAD_DIM), keys, values)
            partial_value = jnp.dot(mixed, w_out, preferred_element_type=jnp.float32).astype(jnp.bfloat16)
            return (total + partial_value.astype(jnp.float32), None)
        total, unused = lax.scan(one_group, jnp.zeros((TOK, D), jnp.float32), jnp.arange(N_TENSOR, dtype=jnp.int32))
        return total.astype(jnp.bfloat16)
    attended = lax.map(replica_attention, tokens.reshape(N_REPLICA, TOK, D)).reshape(TOKENS, D)
    table = hadamard_table(HBLOCK)
    blocks = pseudo_grad.reshape(REPLICAS, D, NBLOCKS, HBLOCK).astype(jnp.float32)
    terms = blocks * jnp.exp2(grad_exps.astype(jnp.float32))[..., None]
    summed = lax.optimization_barrier(jnp.sum(terms, axis=0)).reshape(D, FRAG)
    averaged = rotate(summed / N_REPLICA, table)
    new_momentum = 0.9 * momentum + averaged
    update = 0.7 * (averaged + 0.9 * new_momentum)
    turned = rotate(update, table).reshape(D, NBLOCKS, HBLOCK)
    scales = (lax.optimization_barrier(jnp.max(jnp.abs(turned), axis=-1)) + 1e-06).astype(jnp.bfloat16)
    codes = (turned / scales.astype(jnp.float32)[..., None]).astype(jnp.bfloat16)
    rebuilt = rotate((codes.astype(jnp.float32) * scales.astype(jnp.float32)[..., None]).reshape(D, FRAG), table)
    new_params = (params.astype(jnp.float32) - rebuilt).astype(jnp.bfloat16)
    return (attended, new_params, new_momentum)
```

```python
import functools
import math

import jax
import jax.numpy as jnp
from jax import lax
from jax.experimental import pallas as pl
from jax.experimental.pallas import tpu as pltpu
from jax.sharding import Mesh
from jax.sharding import PartitionSpec as P

HEAD = 128
REPLICA = ("x", "ylo")
TENSOR = ("yhi", "z", "core")
ROWS = 64
RING = (0, 1, -1, 2)
Y = ("ylo", "yhi")
HALVES = 2
MIB = 1024 * 1024


def params(mib=8):
    return pltpu.CompilerParams(vmem_limit_bytes=mib * MIB)


def cost(flops, moved):
    return pl.CostEstimate(flops=int(flops), bytes_accessed=int(moved), transcendentals=0)


def hadamard_table(width):
    index = jnp.arange(width, dtype=jnp.int32)
    common = jnp.bitwise_and(index[:, None], index[None, :])
    parity = jnp.zeros((width, width), jnp.int32)
    for bit in range(int(math.log2(width))):
        parity = parity + jnp.bitwise_and(jnp.right_shift(common, bit), 1)
    sign = 1.0 - 2.0 * jnp.bitwise_and(parity, 1).astype(jnp.float32)
    return sign / math.sqrt(width)


def norm_body(rows_ref, gain_ref, whole_ref, *half_refs):
    values = rows_ref[...].astype(jnp.float32)
    power = jnp.mean(values * values, axis=-1, keepdims=True)
    normed = (values * lax.rsqrt(power + 1e-05) * gain_ref[...]).astype(jnp.bfloat16)
    whole_ref[...] = normed
    count = normed.shape[0] // HALVES
    for at, half_ref in enumerate(half_refs):
        half_ref[...] = normed[at * count : (at + 1) * count]


def normalize(rows, gain):
    count, width = rows.shape
    return pl.pallas_call(
        norm_body,
        out_shape=[
            jax.ShapeDtypeStruct((c, width), jnp.bfloat16)
            for c in [count] + [count // HALVES] * HALVES
        ],
        compiler_params=params(12),
        cost_estimate=cost(4 * rows.size, 6 * rows.size),
        name="normalize",
    )(rows, gain.reshape(1, width))


def project_body(core_ref, *refs):
    blocks, refs = refs[:-7], refs[-7:]
    qa_ref, qb_ref, ka_ref, kb_ref, query_out, pair_out, total = refs
    step, steps = pl.program_id(0), pl.num_programs(0)
    half = qa_ref.shape[1]

    @pl.when(step == 0)
    def _():
        total[...] = jnp.zeros_like(total)

    rows = jnp.concatenate([ref[...] for ref in blocks], axis=0)
    both = jnp.concatenate([ka_ref[...], kb_ref[...]], axis=1)
    for start, weight in ((0, qa_ref[...]), (half, qb_ref[...]), (2 * half, both)):
        total[:, start : start + weight.shape[1]] += jnp.dot(
            rows, weight, preferred_element_type=jnp.float32
        )

    @pl.when(step == steps - 1)
    def _():
        flip = core_ref[0] == 0
        value = total[...].astype(jnp.bfloat16)
        query_out[...] = value[:, : 2 * half]
        left, right = value[:, 2 * half : 2 * half + HEAD], value[:, 2 * half + HEAD :]
        pair_out[:, :HEAD] = jnp.where(flip, left, right)
        pair_out[:, HEAD:] = jnp.where(flip, right, left)


def project(core, blocks, weights):
    width = blocks[0].shape[1]
    tile = 1024
    count = sum(block.shape[0] for block in blocks)
    qcols = 2 * weights[0].shape[1]
    kcols = 2 * weights[2].shape[1]
    smem = pl.BlockSpec(memory_space=pltpu.SMEM)
    whole = lambda cols: pl.BlockSpec((count, cols), lambda i: (0, 0))
    return pl.pallas_call(
        project_body,
        grid=(width // tile,),
        in_specs=[smem]
        + [pl.BlockSpec((block.shape[0], tile), lambda i: (0, i)) for block in blocks]
        + [pl.BlockSpec((tile, w.shape[1]), lambda i: (i, 0)) for w in weights],
        out_specs=[whole(qcols), whole(kcols)],
        out_shape=[
            jax.ShapeDtypeStruct((count, qcols), jnp.bfloat16),
            jax.ShapeDtypeStruct((count, kcols), jnp.bfloat16),
        ],
        scratch_shapes=[pltpu.VMEM((count, qcols + kcols), jnp.float32)],
        compiler_params=params(16),
        cost_estimate=cost(
            2 * 2 * count * width * (qcols + kcols), 2 * width * (count + qcols + kcols)
        ),
        name="project",
    )(core, *blocks, *weights)


def attend_body(core_ref, place_ref, *refs):
    *ins, mixed_ref, query_ref, own_ref, other_ref = refs
    core = core_ref[0]
    parts = len(ins) // 3
    for kind, whole in enumerate((query_ref, own_ref, other_ref)):
        slot = 0
        for part in ins[kind * parts : (kind + 1) * parts]:
            for top in range(0, part.shape[0], ROWS):
                place = pl.ds(pl.multiple_of(place_ref[slot] * ROWS, ROWS), ROWS)
                whole[place, :] = part[top : top + ROWS]
                slot += 1
    count, qcols = query_ref.shape
    heads = qcols // HEAD
    block = 2 * ROWS
    scale = 1.0 / math.sqrt(HEAD)
    shift = ROWS.bit_length() - 1
    for step in range(count // block):
        rows = slice(step * block, (step + 1) * block)
        span = (step + 1) * block
        query = jnp.concatenate(
            [query_ref[rows, h * HEAD : (h + 1) * HEAD] for h in range(heads)], axis=0
        )
        contract = (((1,), (1,)), ((), ()))
        row = lax.broadcasted_iota(jnp.int32, (block, block), 0)
        col = lax.broadcasted_iota(jnp.int32, (block, block), 1)
        own_seen = jnp.concatenate([col <= row] * heads, axis=0)
        other_seen = jnp.concatenate(
            [jnp.right_shift(col, shift) < jnp.right_shift(row, shift) + core] * heads, axis=0
        )

        def scores_of(ref, seen):
            raw = lax.dot_general(
                query, ref[:span, :HEAD], contract, preferred_element_type=jnp.float32
            )
            tail = jnp.where(seen, raw[:, span - block :], -jnp.inf)
            if span == block:
                return tail
            return jnp.concatenate([raw[:, : span - block], tail], axis=1)

        scores = jnp.concatenate(
            [scores_of(own_ref, own_seen), scores_of(other_ref, other_seen)], axis=1
        )
        peak = jnp.max(scores, axis=-1, keepdims=True)
        probs = jnp.exp((scores - peak) * scale).astype(jnp.bfloat16)
        ones = jnp.ones((span, HEAD), jnp.bfloat16)
        total = jnp.zeros((block * heads, 2 * HEAD), jnp.float32)
        for part, ref in enumerate((own_ref, other_ref)):
            values = jnp.concatenate([ref[:span, HEAD:], ones], axis=1)
            total += jnp.dot(
                probs[:, part * span : (part + 1) * span],
                values,
                preferred_element_type=jnp.float32,
            )
        mixed = (total[:, :HEAD] / total[:, HEAD:]).astype(jnp.bfloat16)
        for part in range(block // ROWS):
            slot = place_ref[8 + step * (block // ROWS) + part]
            place = pl.ds(pl.multiple_of(slot * ROWS, ROWS), ROWS)
            for h in range(heads):
                top = h * block + part * ROWS
                mixed_ref[place, h * HEAD : (h + 1) * HEAD] = mixed[top : top + ROWS]


def attend(core, places, queries, own, other):
    count, qcols = sum(q.shape[0] for q in queries), queries[0].shape[1]
    kcols = own[0].shape[1]
    args = [*queries, *own, *other]
    vmem = pl.BlockSpec(memory_space=pltpu.VMEM)
    return pl.pallas_call(
        attend_body,
        in_specs=[pl.BlockSpec(memory_space=pltpu.SMEM)] * 2 + [vmem] * len(args),
        out_specs=vmem,
        out_shape=jax.ShapeDtypeStruct((count, qcols), jnp.bfloat16),
        scratch_shapes=[pltpu.VMEM((count, cols), jnp.bfloat16) for cols in (qcols, kcols, kcols)],
        compiler_params=params(28),
        cost_estimate=cost(8 * count * count * qcols, 4 * count * qcols),
        name="attend",
    )(core, places, *args)


def output_body(first, mixed_ref, mine_ref, theirs_ref, *out_refs):
    half = mine_ref.shape[0]
    rows = mixed_ref[first : first + sum(ref.shape[0] for ref in out_refs)]
    result = (
        jnp.dot(rows[:, :half], mine_ref[...], preferred_element_type=jnp.float32)
        + jnp.dot(rows[:, half:], theirs_ref[...], preferred_element_type=jnp.float32)
    ).astype(jnp.bfloat16)
    top = 0
    for out_ref in out_refs:
        out_ref[...] = result[top : top + out_ref.shape[0]]
        top += out_ref.shape[0]


def output(mixed, mine, theirs, first, counts):
    width = mine.shape[1]
    depth = mixed.shape[1]
    count = sum(counts)
    tile = 1024
    weight = pl.BlockSpec((depth // 2, tile), lambda i: (0, i))
    return pl.pallas_call(
        functools.partial(output_body, first),
        grid=(width // tile,),
        in_specs=[pl.BlockSpec(mixed.shape, lambda i: (0, 0)), weight, weight],
        out_specs=[pl.BlockSpec((c, tile), lambda i: (0, i)) for c in counts],
        out_shape=[jax.ShapeDtypeStruct((c, width), jnp.bfloat16) for c in counts],
        compiler_params=params(16),
        cost_estimate=cost(2 * count * depth * width, 2 * (depth * width + count * width)),
        name="output",
    )(mixed, mine, theirs)


def pick_body(below_ref, above_ref, first_ref, second_ref):
    count = first_ref.shape[0]
    first_ref[...] = below_ref[:count]
    second_ref[...] = above_ref[count:]


def pick(below, above, flops):
    shape = jax.ShapeDtypeStruct((below.shape[0] // HALVES, below.shape[1]), below.dtype)
    return pl.pallas_call(
        pick_body,
        out_shape=[shape, shape],
        compiler_params=params(),
        cost_estimate=cost(flops, 4 * below.size),
        name="pick",
    )(below, above)


def split_body(*refs):
    terms, outs = refs[:-HALVES], refs[-HALVES:]
    count = outs[0].shape[0]
    for at, out_ref in enumerate(outs):
        rows = slice(at * count, (at + 1) * count)
        total = terms[0][rows].astype(jnp.float32)
        for ref in terms[1:]:
            total += ref[rows].astype(jnp.float32)
        out_ref[...] = total.astype(jnp.bfloat16)


def split_sum(*terms):
    shape = jax.ShapeDtypeStruct((terms[0].shape[0] // HALVES, terms[0].shape[1]), terms[0].dtype)
    return pl.pallas_call(
        split_body,
        out_shape=[shape] * HALVES,
        compiler_params=params(),
        cost_estimate=cost(3 * terms[0].size, 8 * terms[0].size),
        name="split",
    )(*terms)


def sums_body(shapes, *refs):
    outs, refs = refs[-len(shapes) :], refs[: -len(shapes)]
    first = 0
    for out_ref, starts in zip(outs, shapes):
        half = out_ref.shape[0] // HALVES
        for top in range(0, out_ref.shape[0], half):
            total = None
            for at, start in enumerate(starts):
                ref = refs[first + at]
                if start <= top < start + ref.shape[0]:
                    term = ref[top - start : top - start + half].astype(jnp.float32)
                    total = term if total is None else total + term
            out_ref[top : top + half] = total.astype(jnp.bfloat16)
        first += len(starts)


def sums(*groups, name="sums"):
    groups = [[t if isinstance(t, tuple) else (t, 0) for t in group] for group in groups]
    args = [array for group in groups for array, _ in group]
    shapes = tuple(tuple(start for _, start in group) for group in groups)
    result = pl.pallas_call(
        functools.partial(sums_body, shapes),
        out_shape=[jax.ShapeDtypeStruct(group[0][0].shape, jnp.bfloat16) for group in groups],
        compiler_params=params(16),
        cost_estimate=cost(sum(a.size for a in args), 3 * sum(a.size for a in args)),
        name=name,
    )(*args)
    return result if len(groups) > 1 else result[0]


def terms_body(block_ref, codes_ref, exps_ref, *out_refs):
    scale = jnp.exp2(exps_ref[...].astype(jnp.float32))
    lane = lax.broadcasted_iota(jnp.int32, scale.shape, 1)
    count = codes_ref.shape[0]
    for at, out_ref in enumerate(out_refs):
        for side in range(2):
            block = block_ref[2 * at + side]
            cols = pl.ds(pl.multiple_of(block * HEAD, HEAD), HEAD)
            mine = jnp.sum(jnp.where(lane == block, scale, 0.0), axis=1, keepdims=True)
            out_ref[side * count : (side + 1) * count] = (
                codes_ref[:, cols].astype(jnp.float32) * mine
            ).astype(jnp.bfloat16)


def terms(blocks, codes, exps):
    count, width = codes.shape
    vmem = pl.BlockSpec(memory_space=pltpu.VMEM)
    return pl.pallas_call(
        terms_body,
        in_specs=[pl.BlockSpec(memory_space=pltpu.SMEM), vmem, vmem],
        out_shape=[jax.ShapeDtypeStruct((2 * count, HEAD), jnp.bfloat16)] * len(RING),
        compiler_params=params(),
        cost_estimate=cost(codes.size, 4 * codes.size),
        name="terms",
    )(blocks, codes, exps)


def outer_body(replicas, *refs):
    mine_refs, theirs_ref, momentum_ref, table_ref, momentum_out, rebuilt_ref = (
        refs[:3],
        *refs[3:],
    )
    table = table_ref[...]

    def rotate(values):
        return jnp.dot(
            values, table, precision=lax.Precision.HIGHEST, preferred_element_type=jnp.float32
        )

    summed = theirs_ref[...].astype(jnp.float32)
    for ref in mine_refs:
        summed += ref[: summed.shape[0]].astype(jnp.float32)
    averaged = rotate(summed / replicas)
    fresh = 0.9 * momentum_ref[...] + averaged
    momentum_out[...] = fresh
    turned = rotate(0.7 * (averaged + 0.9 * fresh))
    scales = (jnp.max(jnp.abs(turned), axis=-1, keepdims=True) + 1e-06).astype(jnp.bfloat16)
    scales = scales.astype(jnp.float32)
    codes = (turned / scales).astype(jnp.bfloat16)
    rebuilt_ref[...] = rotate(codes.astype(jnp.float32) * scales).astype(jnp.bfloat16)


def outer(mine, theirs, momentum, table, replicas):
    return pl.pallas_call(
        functools.partial(outer_body, replicas),
        out_shape=[
            jax.ShapeDtypeStruct(momentum.shape, jnp.float32),
            jax.ShapeDtypeStruct(momentum.shape, jnp.bfloat16),
        ],
        compiler_params=params(),
        cost_estimate=cost(40 * theirs.size * HEAD, 12 * theirs.size),
        name="outer",
    )(*mine, theirs, momentum, table)


def apply_body(block_ref, params_ref, *refs):
    rebuilt_refs, out_ref = refs[:-1], refs[-1]
    count = out_ref.shape[0]
    for at, rebuilt_ref in enumerate(rebuilt_refs):
        for side in range(2):
            cols = pl.ds(pl.multiple_of(block_ref[2 * at + side] * HEAD, HEAD), HEAD)
            rebuilt = rebuilt_ref[side * count : (side + 1) * count].astype(jnp.float32)
            out_ref[:, cols] = (params_ref[:, cols].astype(jnp.float32) - rebuilt).astype(
                jnp.bfloat16
            )


def apply(blocks, old, rebuilt):
    vmem = pl.BlockSpec(memory_space=pltpu.VMEM)
    return pl.pallas_call(
        apply_body,
        in_specs=[pl.BlockSpec(memory_space=pltpu.SMEM)] + [vmem] * (1 + len(rebuilt)),
        out_shape=jax.ShapeDtypeStruct(old.shape, jnp.bfloat16),
        compiler_params=params(),
        cost_estimate=cost(old.size, 6 * old.size),
        name="apply",
    )(blocks, old, *rebuilt)


def swap(block, axis):
    return lax.ppermute(block, axis, [(0, 1), (1, 0)])


def hop(block, axis, way):
    at = (0, 2, 1, 3) if axis == Y else (0, 1, 2, 3)
    return lax.ppermute(block, axis, [(at[i], at[(i + way) % 4]) for i in range(4)])


def add(*blocks):
    total = blocks[0].astype(jnp.float32)
    for block in blocks[1:]:
        total = total + block.astype(jnp.float32)
    return total.astype(jnp.bfloat16)


def wait(*blocks):
    return lax.optimization_barrier(blocks)


def tie(block, *others):
    return lax.optimization_barrier((block, *others))[0]


def local(
    tokens, norm_gain, query_weight, kv_weight, out_weight, pseudo_grad, grad_exps, old, momentum
):
    core, z, yhi = lax.axis_index("core"), lax.axis_index("z"), lax.axis_index("yhi")
    x, ylo = lax.axis_index("x"), lax.axis_index("ylo")
    replicas = lax.axis_size(REPLICA)
    place = jnp.stack([(yhi ^ side) * 4 + (z + r) % 4 for side in range(2) for r in RING])
    chip = jnp.arange(8, dtype=jnp.int32)
    away = (chip % 4 - z) % 4
    slots = ((chip // 4) ^ yhi) * 4 + jnp.where(away < 2, away, 5 - away)
    share = jnp.stack([((x + r) % 4) * 2 + (ylo ^ side) for r in RING for side in range(2)])
    core, place, slots, share = (
        v.astype(jnp.int32).reshape(-1) for v in (core, place, slots, share)
    )
    places = jnp.concatenate([place, slots])

    block, h1, h2 = normalize(tokens, norm_gain)
    relay1, relay2 = hop(h1, Y, 1), hop(h2, Y, -1)
    below, above = hop(block, "z", 1), hop(block, "z", -1)
    kv_theirs = swap(tie(kv_weight, block), "core")
    at0, at1, at3, at2 = terms(share, tie(pseudo_grad[0], block), grad_exps[0])
    relay1, relay2, kv_theirs, at0, at1, at2, at3, query_weight = wait(
        relay1, relay2, kv_theirs, at0, at1, at2, at3, query_weight
    )
    query_theirs = swap(query_weight, "core")
    partner = jnp.concatenate([hop(relay1, Y, 1), hop(relay2, Y, -1)], axis=0)
    far1, far2 = pick(below, above, 1.5e11)
    partner = tie(partner, far1, far2)
    pbelow, pabove = hop(partner, "z", 1), hop(partner, "z", -1)
    far1, far2 = hop(far1, "z", 1), hop(far2, "z", -1)
    weights = [query_weight, query_theirs, kv_weight, kv_theirs]
    query_a, pair_a = project(core, [block, above, below, far1, far2], weights)
    x2 = hop(tie(at2, far1), "x", 1)
    pbelow, pabove, query_a, pair_a, x2, at1, at3, out_weight = wait(
        pbelow, pabove, query_a, pair_a, x2, at1, at3, out_weight
    )
    pfar1, pfar2 = pick(pbelow, pabove, 1e8)
    pfar1, pfar2 = hop(pfar1, "z", 1), hop(pfar2, "z", -1)
    passed, x3 = hop(add(at1, x2), "x", 1), hop(at3, "x", -1)
    query_m, pair_m = project(core, [partner, pabove, pbelow], weights)
    out_theirs = swap(out_weight, "core")
    pfar1, pfar2, query_m, pair_m, passed, x3, at0 = wait(
        pfar1, pfar2, query_m, pair_m, passed, x3, at0
    )
    other_a, other_m = swap(pair_a, "core"), swap(pair_m, "core")
    query_l, pair_l = project(core, [pfar1, pfar2], weights)
    other_l = swap(pair_l, "core")
    mine = (at0, passed, x3)
    count = momentum.shape[0]
    theirs = swap(add(*(part[count:] for part in mine)), "ylo")
    mixed = attend(
        core,
        places,
        (query_a, query_m, query_l),
        (pair_a, pair_m, pair_l),
        (other_a, other_m, other_l),
    )
    mixed, theirs, out_theirs = wait(mixed, theirs, out_theirs)

    half = ROWS // HALVES
    theirs_at = len(RING) * ROWS
    up1, down2 = output(mixed, out_weight, out_theirs, theirs_at + 3 * ROWS, [half] * HALVES)
    up1, down2 = hop(up1, "z", 1), hop(down2, "z", -1)
    new_momentum, rebuilt = outer(mine, theirs, momentum, hadamard_table(HEAD), replicas)
    beside = swap(rebuilt, "ylo")
    q0, qup, qdown = output(mixed, out_weight, out_theirs, theirs_at, [ROWS] * 3)
    up, down = sums((qup, (up1, 0)), (qdown, (down2, half)))
    both = jnp.concatenate([rebuilt, beside], axis=0)
    up, down, both, mixed = wait(up, down, both, mixed)
    up, down = hop(up, "z", 1), hop(down, "z", -1)
    before = hop(both, "x", 1)
    o0, oup, odown, ofar1, ofar2 = output(
        mixed, out_weight, out_theirs, 0, [ROWS] * 3 + [half] * HALVES
    )
    far1, far2 = hop(ofar1, "z", 1), hop(ofar2, "z", -1)
    after = hop(tie(both, before), "x", -1)
    up, down, before, after, oup, odown = wait(up, down, before, after, oup, odown)
    s1, s2 = split_sum(q0, up, down)
    s1, s2 = hop(s1, Y, 1), hop(s2, Y, -1)
    ahead = hop(before, "x", 1)
    oup, odown = sums((oup, (far1, 0)), (odown, (far2, half)))
    up, down = hop(oup, "z", 1), hop(odown, "z", -1)
    s1, s2, ahead = wait(s1, s2, ahead)
    s1, s2 = hop(s1, Y, 1), hop(s2, Y, -1)
    new_params = apply(share, old, [both, after, before, ahead])
    o0, new_params = wait(o0, new_params)
    attended = sums((o0, up, down, (s1, 0), (s2, half)), name="finish")
    return (attended, new_params, new_momentum)


def solution(mesh):
    fine = Mesh(mesh.devices.reshape(4, 2, 2, 4, 2), ("x", "ylo", "yhi", "z", "core"))
    every = REPLICA + TENSOR
    return jax.shard_map(
        local,
        mesh=fine,
        in_specs=(
            P(every, None),
            P(),
            P(None, TENSOR),
            P(None, TENSOR),
            P(TENSOR, None),
            P(REPLICA, TENSOR, None),
            P(REPLICA, TENSOR, None),
            P(TENSOR, None),
            P(TENSOR, REPLICA),
        ),
        out_specs=(P(every, None), P(TENSOR, None), P(TENSOR, REPLICA)),
        check_vma=False,
    )
```

```python
import functools
import math

import jax
import jax.numpy as jnp
from jax import lax
from jax.experimental import pallas as pl
from jax.experimental.pallas import tpu as pltpu
from jax.sharding import Mesh
from jax.sharding import PartitionSpec as P

HEAD = 128
REPLICA = ("x", "ylo")
TENSOR = ("yhi", "z", "core")
ROWS = 64
RING = (0, 1, -1, 2)
Y = ("ylo", "yhi")
HALVES = 2
MIB = 1024 * 1024


def params(mib=8):
    return pltpu.CompilerParams(vmem_limit_bytes=mib * MIB)


def cost(flops, moved):
    return pl.CostEstimate(flops=int(flops), bytes_accessed=int(moved), transcendentals=0)


def hadamard_table(width):
    index = jnp.arange(width, dtype=jnp.int32)
    common = jnp.bitwise_and(index[:, None], index[None, :])
    parity = jnp.zeros((width, width), jnp.int32)
    for bit in range(int(math.log2(width))):
        parity = parity + jnp.bitwise_and(jnp.right_shift(common, bit), 1)
    sign = 1.0 - 2.0 * jnp.bitwise_and(parity, 1).astype(jnp.float32)
    return sign / math.sqrt(width)


def norm_body(rows_ref, gain_ref, whole_ref, *half_refs):
    values = rows_ref[...].astype(jnp.float32)
    power = jnp.mean(values * values, axis=-1, keepdims=True)
    normed = (values * lax.rsqrt(power + 1e-05) * gain_ref[...]).astype(jnp.bfloat16)
    whole_ref[...] = normed
    count = normed.shape[0] // HALVES
    for at, half_ref in enumerate(half_refs):
        half_ref[...] = normed[at * count : (at + 1) * count]


def normalize(rows, gain):
    count, width = rows.shape
    return pl.pallas_call(
        norm_body,
        out_shape=[
            jax.ShapeDtypeStruct((c, width), jnp.bfloat16)
            for c in [count] + [count // HALVES] * HALVES
        ],
        compiler_params=params(12),
        cost_estimate=cost(4 * rows.size, 6 * rows.size),
        name="normalize",
    )(rows, gain.reshape(1, width))


def project_body(tile, core_ref, *refs):
    blocks, refs = refs[:-12], refs[-12:]
    weights, (query_out, pair_out, total), held, arrived = refs[:4], refs[4:7], refs[7:11], refs[11]
    half = weights[0].shape[1]
    depth = weights[0].shape[0]
    chunks = arrived.shape[1]
    chunk = depth // chunks
    copies = [
        [
            pltpu.make_async_copy(
                weight.at[pl.ds(at * chunk, chunk), :],
                place.at[pl.ds(at * chunk, chunk), :],
                arrived.at[kind, at],
            )
            for kind, (weight, place) in enumerate(zip(weights, held))
        ]
        for at in range(chunks)
    ]
    for group in copies:
        for copy in group:
            copy.start()
    total[...] = jnp.zeros_like(total)
    qa_ref, qb_ref, ka_ref, kb_ref = held

    def step(at, carry):
        span = pl.ds(pl.multiple_of(at * tile, tile), tile)
        rows = jnp.concatenate([ref[:, span] for ref in blocks], axis=0)
        both = jnp.concatenate([ka_ref[span, :], kb_ref[span, :]], axis=1)
        for start, weight in ((0, qa_ref[span, :]), (half, qb_ref[span, :]), (2 * half, both)):
            total[:, start : start + weight.shape[1]] += jnp.dot(
                rows, weight, preferred_element_type=jnp.float32
            )
        return carry

    per = chunk // tile
    for at, group in enumerate(copies):
        for copy in group:
            copy.wait()
        lax.fori_loop(at * per, (at + 1) * per, step, 0)
    flip = core_ref[0] == 0
    value = total[...].astype(jnp.bfloat16)
    query_out[...] = value[:, : 2 * half]
    left, right = value[:, 2 * half : 2 * half + HEAD], value[:, 2 * half + HEAD :]
    pair_out[:, :HEAD] = jnp.where(flip, left, right)
    pair_out[:, HEAD:] = jnp.where(flip, right, left)


def project(core, blocks, weights):
    width = blocks[0].shape[1]
    count = sum(block.shape[0] for block in blocks)
    qcols = 2 * weights[0].shape[1]
    kcols = 2 * weights[2].shape[1]
    vmem = pl.BlockSpec(memory_space=pltpu.VMEM)
    return pl.pallas_call(
        functools.partial(project_body, 1024),
        in_specs=[pl.BlockSpec(memory_space=pltpu.SMEM)]
        + [vmem] * len(blocks)
        + [pl.BlockSpec(memory_space=pl.ANY)] * len(weights),
        out_specs=[vmem, vmem],
        out_shape=[
            jax.ShapeDtypeStruct((count, qcols), jnp.bfloat16),
            jax.ShapeDtypeStruct((count, kcols), jnp.bfloat16),
        ],
        scratch_shapes=[pltpu.VMEM((count, qcols + kcols), jnp.float32)]
        + [pltpu.VMEM(weight.shape, jnp.bfloat16) for weight in weights]
        + [pltpu.SemaphoreType.DMA((len(weights), 4))],
        compiler_params=params(32),
        cost_estimate=cost(
            2 * count * width * (qcols + kcols), 2 * width * (count + qcols + kcols)
        ),
        name="project",
    )(core, *blocks, *weights)


def attend_body(order, core_ref, place_ref, *refs):
    ins, refs = refs[:-10], refs[-10:]
    weights, mixed_ref, far_refs = refs[:2], refs[2], refs[3:5]
    query_ref, own_ref, other_ref, held, arrived = refs[5:]
    half, width = weights[0].shape
    chunks = arrived.shape[1]
    chunk = half // chunks
    copies = [
        pltpu.make_async_copy(
            weight.at[pl.ds(at * chunk, chunk), :],
            held.at[pl.ds(kind * half + at * chunk, chunk), :],
            arrived.at[kind, at],
        )
        for kind, weight in enumerate(weights)
        for at in range(chunks)
    ]
    for copy in copies:
        copy.start()
    core = core_ref[0]
    parts = len(ins) // 3
    for kind, whole in enumerate((query_ref, own_ref, other_ref)):
        at = 0
        for part in ins[kind * parts : (kind + 1) * parts]:
            for top in range(0, part.shape[0], ROWS):
                place = pl.ds(pl.multiple_of(place_ref[order[at]] * ROWS, ROWS), ROWS)
                whole[place, :] = part[top : top + ROWS]
                at += 1
    count, qcols = query_ref.shape
    heads = qcols // HEAD
    block = 2 * ROWS
    scale = 1.0 / math.sqrt(HEAD)
    shift = ROWS.bit_length() - 1
    for step in range(count // block):
        rows = slice(step * block, (step + 1) * block)
        span = (step + 1) * block
        query = jnp.concatenate(
            [query_ref[rows, h * HEAD : (h + 1) * HEAD] for h in range(heads)], axis=0
        )
        contract = (((1,), (1,)), ((), ()))
        row = lax.broadcasted_iota(jnp.int32, (block, block), 0)
        col = lax.broadcasted_iota(jnp.int32, (block, block), 1)
        own_seen = jnp.concatenate([col <= row] * heads, axis=0)
        other_seen = jnp.concatenate(
            [jnp.right_shift(col, shift) < jnp.right_shift(row, shift) + core] * heads, axis=0
        )

        def scores_of(ref, seen):
            raw = lax.dot_general(
                query, ref[:span, :HEAD], contract, preferred_element_type=jnp.float32
            )
            tail = jnp.where(seen, raw[:, span - block :], -jnp.inf)
            if span == block:
                return tail
            return jnp.concatenate([raw[:, : span - block], tail], axis=1)

        scores = jnp.concatenate(
            [scores_of(own_ref, own_seen), scores_of(other_ref, other_seen)], axis=1
        )
        peak = jnp.max(scores, axis=-1, keepdims=True)
        probs = jnp.exp((scores - peak) * scale).astype(jnp.bfloat16)
        ones = jnp.ones((span, HEAD), jnp.bfloat16)
        total = jnp.zeros((block * heads, 2 * HEAD), jnp.float32)
        for part, ref in enumerate((own_ref, other_ref)):
            values = jnp.concatenate([ref[:span, HEAD:], ones], axis=1)
            total += jnp.dot(
                probs[:, part * span : (part + 1) * span],
                values,
                preferred_element_type=jnp.float32,
            )
        mixed = (total[:, :HEAD] / total[:, HEAD:]).astype(jnp.bfloat16)
        for part in range(block // ROWS):
            slot = place_ref[8 + step * (block // ROWS) + part]
            place = pl.ds(pl.multiple_of(slot * ROWS, ROWS), ROWS)
            for h in range(heads):
                top = h * block + part * ROWS
                mixed_ref[place, h * HEAD : (h + 1) * HEAD] = mixed[top : top + ROWS]

    for copy in copies:
        copy.wait()
    rows = mixed_ref[count - ROWS :]
    tile = 1024

    def far(at, carry):
        span = pl.ds(pl.multiple_of(at * tile, tile), tile)
        result = jnp.dot(rows, held[:, span], preferred_element_type=jnp.float32)
        result = result.astype(jnp.bfloat16)
        for side, far_ref in enumerate(far_refs):
            far_ref[:, span] = result[side * ROWS // HALVES : (side + 1) * ROWS // HALVES]
        return carry

    lax.fori_loop(0, width // tile, far, 0)


def attend(core, places, order, queries, own, other, weights):
    count, qcols = sum(q.shape[0] for q in queries), queries[0].shape[1]
    kcols = own[0].shape[1]
    args = [*queries, *own, *other]
    vmem = pl.BlockSpec(memory_space=pltpu.VMEM)
    depth, width = weights[0].shape
    return pl.pallas_call(
        functools.partial(attend_body, order),
        in_specs=[pl.BlockSpec(memory_space=pltpu.SMEM)] * 2
        + [vmem] * len(args)
        + [pl.BlockSpec(memory_space=pl.ANY)] * 2,
        out_specs=[vmem] * 3,
        out_shape=[jax.ShapeDtypeStruct((count, qcols), jnp.bfloat16)]
        + [jax.ShapeDtypeStruct((ROWS // HALVES, width), jnp.bfloat16)] * HALVES,
        scratch_shapes=[pltpu.VMEM((count, cols), jnp.bfloat16) for cols in (qcols, kcols, kcols)]
        + [pltpu.VMEM((2 * depth, width), jnp.bfloat16), pltpu.SemaphoreType.DMA((2, 4))],
        compiler_params=params(48),
        cost_estimate=cost(8 * count * count * qcols, 4 * count * qcols + 4 * depth * width),
        name="attend",
    )(core, places, *args, *weights)


def output_body(first, mixed_ref, mine_ref, theirs_ref, *out_refs):
    half = mine_ref.shape[0]
    rows = mixed_ref[first : first + sum(ref.shape[0] for ref in out_refs)]
    result = (
        jnp.dot(rows[:, :half], mine_ref[...], preferred_element_type=jnp.float32)
        + jnp.dot(rows[:, half:], theirs_ref[...], preferred_element_type=jnp.float32)
    ).astype(jnp.bfloat16)
    top = 0
    for out_ref in out_refs:
        out_ref[...] = result[top : top + out_ref.shape[0]]
        top += out_ref.shape[0]


def output(mixed, mine, theirs, first, counts):
    width = mine.shape[1]
    depth = mixed.shape[1]
    count = sum(counts)
    tile = 1024
    weight = pl.BlockSpec((depth // 2, tile), lambda i: (0, i))
    return pl.pallas_call(
        functools.partial(output_body, first),
        grid=(width // tile,),
        in_specs=[pl.BlockSpec(mixed.shape, lambda i: (0, 0)), weight, weight],
        out_specs=[pl.BlockSpec((c, tile), lambda i: (0, i)) for c in counts],
        out_shape=[jax.ShapeDtypeStruct((c, width), jnp.bfloat16) for c in counts],
        compiler_params=params(16),
        cost_estimate=cost(2 * count * depth * width, 2 * (depth * width + count * width)),
        name="output",
    )(mixed, mine, theirs)


def mark_body(*refs):
    del refs


def mark(*blocks):
    anywhere = [pl.BlockSpec(memory_space=pl.ANY)] * len(blocks)
    return pl.pallas_call(
        mark_body,
        in_specs=anywhere,
        out_specs=anywhere,
        out_shape=[jax.ShapeDtypeStruct(block.shape, block.dtype) for block in blocks],
        input_output_aliases={at: at for at in range(len(blocks))},
        compiler_params=params(),
        cost_estimate=cost(1e11, 4096),
        name="mark",
    )(*blocks)


def split_body(*refs):
    terms, outs = refs[:-HALVES], refs[-HALVES:]
    count = outs[0].shape[0]
    for at, out_ref in enumerate(outs):
        rows = slice(at * count, (at + 1) * count)
        total = terms[0][rows].astype(jnp.float32)
        for ref in terms[1:]:
            total += ref[rows].astype(jnp.float32)
        out_ref[...] = total.astype(jnp.bfloat16)


def split_sum(*terms):
    shape = jax.ShapeDtypeStruct((terms[0].shape[0] // HALVES, terms[0].shape[1]), terms[0].dtype)
    return pl.pallas_call(
        split_body,
        out_shape=[shape] * HALVES,
        compiler_params=params(),
        cost_estimate=cost(3 * terms[0].size, 8 * terms[0].size),
        name="split",
    )(*terms)


def sums_body(shapes, *refs):
    outs, refs = refs[-len(shapes) :], refs[: -len(shapes)]
    first = 0
    for out_ref, starts in zip(outs, shapes):
        half = out_ref.shape[0] // HALVES
        for top in range(0, out_ref.shape[0], half):
            total = None
            for at, start in enumerate(starts):
                ref = refs[first + at]
                if start <= top < start + ref.shape[0]:
                    term = ref[top - start : top - start + half].astype(jnp.float32)
                    total = term if total is None else total + term
            out_ref[top : top + half] = total.astype(jnp.bfloat16)
        first += len(starts)


def sums(*groups, name="sums"):
    groups = [[t if isinstance(t, tuple) else (t, 0) for t in group] for group in groups]
    args = [array for group in groups for array, _ in group]
    shapes = tuple(tuple(start for _, start in group) for group in groups)
    result = pl.pallas_call(
        functools.partial(sums_body, shapes),
        out_shape=[jax.ShapeDtypeStruct(group[0][0].shape, jnp.bfloat16) for group in groups],
        compiler_params=params(16),
        cost_estimate=cost(sum(a.size for a in args), 3 * sum(a.size for a in args)),
        name=name,
    )(*args)
    return result if len(groups) > 1 else result[0]


def terms_body(block_ref, codes_ref, exps_ref, *out_refs):
    scale = jnp.exp2(exps_ref[...].astype(jnp.float32))
    lane = lax.broadcasted_iota(jnp.int32, scale.shape, 1)
    count = codes_ref.shape[0]
    for at, out_ref in enumerate(out_refs):
        for side in range(2):
            block = block_ref[2 * at + side]
            cols = pl.ds(pl.multiple_of(block * HEAD, HEAD), HEAD)
            mine = jnp.sum(jnp.where(lane == block, scale, 0.0), axis=1, keepdims=True)
            out_ref[side * count : (side + 1) * count] = (
                codes_ref[:, cols].astype(jnp.float32) * mine
            ).astype(jnp.bfloat16)


def terms(blocks, codes, exps):
    count, width = codes.shape
    vmem = pl.BlockSpec(memory_space=pltpu.VMEM)
    return pl.pallas_call(
        terms_body,
        in_specs=[pl.BlockSpec(memory_space=pltpu.SMEM), vmem, vmem],
        out_shape=[jax.ShapeDtypeStruct((2 * count, HEAD), jnp.bfloat16)] * len(RING),
        compiler_params=params(),
        cost_estimate=cost(codes.size, 4 * codes.size),
        name="terms",
    )(blocks, codes, exps)


def outer_body(replicas, *refs):
    mine_refs, theirs_ref, momentum_ref, table_ref, momentum_out, rebuilt_ref = (
        refs[:3],
        *refs[3:],
    )
    table = table_ref[...]

    def rotate(values):
        return jnp.dot(
            values, table, precision=lax.Precision.HIGHEST, preferred_element_type=jnp.float32
        )

    summed = theirs_ref[...].astype(jnp.float32)
    for ref in mine_refs:
        summed += ref[: summed.shape[0]].astype(jnp.float32)
    averaged = rotate(summed / replicas)
    fresh = 0.9 * momentum_ref[...] + averaged
    momentum_out[...] = fresh
    turned = rotate(0.7 * (averaged + 0.9 * fresh))
    scales = (jnp.max(jnp.abs(turned), axis=-1, keepdims=True) + 1e-06).astype(jnp.bfloat16)
    scales = scales.astype(jnp.float32)
    codes = (turned / scales).astype(jnp.bfloat16)
    rebuilt_ref[...] = rotate(codes.astype(jnp.float32) * scales).astype(jnp.bfloat16)


def outer(mine, theirs, momentum, table, replicas):
    return pl.pallas_call(
        functools.partial(outer_body, replicas),
        out_shape=[
            jax.ShapeDtypeStruct(momentum.shape, jnp.float32),
            jax.ShapeDtypeStruct(momentum.shape, jnp.bfloat16),
        ],
        compiler_params=params(),
        cost_estimate=cost(40 * theirs.size * HEAD, 12 * theirs.size),
        name="outer",
    )(*mine, theirs, momentum, table)


def apply_body(block_ref, params_ref, *refs):
    rebuilt_refs, out_ref = refs[:-1], refs[-1]
    count = out_ref.shape[0]
    for at, rebuilt_ref in enumerate(rebuilt_refs):
        for side in range(2):
            cols = pl.ds(pl.multiple_of(block_ref[2 * at + side] * HEAD, HEAD), HEAD)
            rebuilt = rebuilt_ref[side * count : (side + 1) * count].astype(jnp.float32)
            out_ref[:, cols] = (params_ref[:, cols].astype(jnp.float32) - rebuilt).astype(
                jnp.bfloat16
            )


def apply(blocks, old, rebuilt):
    vmem = pl.BlockSpec(memory_space=pltpu.VMEM)
    return pl.pallas_call(
        apply_body,
        in_specs=[pl.BlockSpec(memory_space=pltpu.SMEM)] + [vmem] * (1 + len(rebuilt)),
        out_shape=jax.ShapeDtypeStruct(old.shape, jnp.bfloat16),
        compiler_params=params(),
        cost_estimate=cost(old.size, 6 * old.size),
        name="apply",
    )(blocks, old, *rebuilt)


def swap(block, axis):
    return lax.ppermute(block, axis, [(0, 1), (1, 0)])


def hop(block, axis, way):
    at = (0, 2, 1, 3) if axis == Y else (0, 1, 2, 3)
    return lax.ppermute(block, axis, [(at[i], at[(i + way) % 4]) for i in range(4)])


def add(*blocks):
    total = blocks[0].astype(jnp.float32)
    for block in blocks[1:]:
        total = total + block.astype(jnp.float32)
    return total.astype(jnp.bfloat16)


def wait(*blocks):
    return lax.optimization_barrier(blocks)


def tie(block, *others):
    return lax.optimization_barrier((block, *others))[0]


def local(
    tokens, norm_gain, query_weight, kv_weight, out_weight, pseudo_grad, grad_exps, old, momentum
):
    core, z, yhi = lax.axis_index("core"), lax.axis_index("z"), lax.axis_index("yhi")
    x, ylo = lax.axis_index("x"), lax.axis_index("ylo")
    replicas = lax.axis_size(REPLICA)
    place = jnp.stack([(yhi ^ side) * 4 + (z + r) % 4 for side in range(2) for r in RING])
    chip = jnp.arange(8, dtype=jnp.int32)
    away = (chip % 4 - z) % 4
    slots = ((chip // 4) ^ yhi) * 4 + jnp.where(away < 2, away, 5 - away)
    share = jnp.stack([((x + r) % 4) * 2 + (ylo ^ side) for r in RING for side in range(2)])
    core, place, slots, share = (
        v.astype(jnp.int32).reshape(-1) for v in (core, place, slots, share)
    )
    places = jnp.concatenate([place, slots])

    block, h1, h2 = normalize(tokens, norm_gain)
    relay1, relay2 = hop(h1, Y, 1), hop(h2, Y, -1)
    below, above = hop(block, "z", 1), hop(block, "z", -1)
    kv_theirs = swap(tie(kv_weight, block), "core")
    at0, at1, at3, at2 = terms(share, tie(pseudo_grad[0], block), grad_exps[0])
    relay1, relay2, kv_theirs, at0, at1, at2, at3, query_weight = wait(
        relay1, relay2, kv_theirs, at0, at1, at2, at3, query_weight
    )
    query_theirs = swap(query_weight, "core")
    partner = jnp.concatenate([hop(relay1, Y, 1), hop(relay2, Y, -1)], axis=0)
    below, above = mark(below, above)
    far = hop(below, "z", 1)
    partner, above, below = wait(partner, above, below)
    pabove, pbelow = hop(partner, "z", -1), hop(partner, "z", 1)
    weights = [query_weight, query_theirs, kv_weight, kv_theirs]
    query_a, pair_a = project(core, [block, above, below, partner], weights)
    at2, at3 = wait(at2, at3, partner)[:2]
    x2, x3 = hop(at2, "x", 1), hop(at3, "x", -1)
    pabove, far, query_a, pair_a, x2, x3, at1, out_weight = wait(
        pabove, far, query_a, pair_a, x2, x3, at1, out_weight
    )
    pfar = hop(pabove, "z", -1)
    out_theirs = swap(out_weight, "core")
    query_m, pair_m = project(core, [far, pabove], weights)
    passed = hop(add(at1, x2), "x", 1)
    other_a, other_m = swap(pair_a, "core"), swap(pair_m, "core")
    pbelow, pfar, passed, query_m = wait(pbelow, pfar, passed, query_m)
    query_l, pair_l = project(core, [pbelow, pfar], weights)
    other_l = swap(pair_l, "core")
    mixed, up1, down2 = attend(
        core,
        places,
        (0, 1, 2, 4, 3, 5, 6, 7),
        (query_a, query_m, query_l),
        (pair_a, pair_m, pair_l),
        (other_a, other_m, other_l),
        (out_weight, out_theirs),
    )

    half = ROWS // HALVES
    theirs_at = len(RING) * ROWS
    up1, down2 = hop(up1, "z", 1), hop(down2, "z", -1)
    mine = (at0, passed, x3)
    count = momentum.shape[0]
    q0, qup, qdown = output(mixed, out_weight, out_theirs, theirs_at, [ROWS] * 3)
    theirs = swap(tie(add(*(part[count:] for part in mine)), q0), "ylo")
    new_momentum, rebuilt = outer(mine, theirs, momentum, hadamard_table(HEAD), replicas)
    beside = swap(rebuilt, "ylo")
    up, down = sums((qup, (up1, 0)), (qdown, (down2, half)))
    both = jnp.concatenate([rebuilt, beside], axis=0)
    up, down, both, mixed = wait(up, down, both, mixed)
    up, down = hop(up, "z", 1), hop(down, "z", -1)
    before = hop(both, "x", 1)
    o0, oup, odown, ofar1, ofar2 = output(
        mixed, out_weight, out_theirs, 0, [ROWS] * 3 + [half] * HALVES
    )
    far1, far2 = hop(ofar1, "z", 1), hop(ofar2, "z", -1)
    after = hop(tie(both, before), "x", -1)
    up, down, before, after, oup, odown = wait(up, down, before, after, oup, odown)
    s1, s2 = split_sum(q0, up, down)
    s1, s2 = hop(s1, Y, 1), hop(s2, Y, -1)
    ahead = hop(before, "x", 1)
    oup, odown = sums((oup, (far1, 0)), (odown, (far2, half)))
    up, down = hop(oup, "z", 1), hop(odown, "z", -1)
    s1, s2, ahead = wait(s1, s2, ahead)
    s1, s2 = hop(s1, Y, 1), hop(s2, Y, -1)
    new_params = apply(share, old, [both, after, before, ahead])
    o0, new_params = wait(o0, new_params)
    attended = sums((o0, up, down, (s1, 0), (s2, half)), name="finish")
    return (attended, new_params, new_momentum)


def solution(mesh):
    fine = Mesh(mesh.devices.reshape(4, 2, 2, 4, 2), ("x", "ylo", "yhi", "z", "core"))
    every = REPLICA + TENSOR
    return jax.shard_map(
        local,
        mesh=fine,
        in_specs=(
            P(every, None),
            P(),
            P(None, TENSOR),
            P(None, TENSOR),
            P(TENSOR, None),
            P(REPLICA, TENSOR, None),
            P(REPLICA, TENSOR, None),
            P(TENSOR, None),
            P(TENSOR, REPLICA),
        ),
        out_specs=(P(every, None), P(TENSOR, None), P(TENSOR, REPLICA)),
        check_vma=False,
    )
```

```python
import functools
import math

import jax
import jax.numpy as jnp
from jax import lax
from jax.experimental import pallas as pl
from jax.experimental.pallas import tpu as pltpu
from jax.sharding import Mesh
from jax.sharding import PartitionSpec as P

HEAD = 128
REPLICA = ("x", "ylo")
TENSOR = ("yhi", "z", "core")
ROWS = 64
RING = (0, 1, -1, 2)
Y = ("ylo", "yhi")
HALVES = 2
TILE = 1024
MIB = 1024 * 1024


def params(mib=8):
    return pltpu.CompilerParams(vmem_limit_bytes=mib * MIB)


def cost(flops, moved):
    return pl.CostEstimate(flops=int(flops), bytes_accessed=int(moved), transcendentals=0)


def hadamard_table(width):
    index = jnp.arange(width, dtype=jnp.int32)
    common = jnp.bitwise_and(index[:, None], index[None, :])
    parity = jnp.zeros((width, width), jnp.int32)
    for bit in range(int(math.log2(width))):
        parity = parity + jnp.bitwise_and(jnp.right_shift(common, bit), 1)
    sign = 1.0 - 2.0 * jnp.bitwise_and(parity, 1).astype(jnp.float32)
    return sign / math.sqrt(width)


def norm_body(rows_ref, gain_ref, whole_ref, *half_refs):
    values = rows_ref[...].astype(jnp.float32)
    power = jnp.mean(values * values, axis=-1, keepdims=True)
    normed = (values * lax.rsqrt(power + 1e-05) * gain_ref[...]).astype(jnp.bfloat16)
    whole_ref[...] = normed
    count = normed.shape[0] // HALVES
    for at, half_ref in enumerate(half_refs):
        half_ref[...] = normed[at * count : (at + 1) * count]


def normalize(rows, gain):
    count, width = rows.shape
    return pl.pallas_call(
        norm_body,
        out_shape=[
            jax.ShapeDtypeStruct((c, width), jnp.bfloat16)
            for c in [count] + [count // HALVES] * HALVES
        ],
        compiler_params=params(12),
        cost_estimate=cost(4 * rows.size, 6 * rows.size),
        name="normalize",
    )(rows, gain.reshape(1, width))


def project_body(tile, core_ref, *refs):
    blocks, refs = refs[:-12], refs[-12:]
    weights, (query_out, pair_out, total), held, arrived = refs[:4], refs[4:7], refs[7:11], refs[11]
    half = weights[0].shape[1]
    depth = weights[0].shape[0]
    chunks = arrived.shape[1]
    chunk = depth // chunks
    copies = [
        [
            pltpu.make_async_copy(
                weight.at[pl.ds(at * chunk, chunk), :],
                place.at[pl.ds(at * chunk, chunk), :],
                arrived.at[kind, at],
            )
            for kind, (weight, place) in enumerate(zip(weights, held))
        ]
        for at in range(chunks)
    ]
    for group in copies:
        for copy in group:
            copy.start()
    total[...] = jnp.zeros_like(total)
    qa_ref, qb_ref, ka_ref, kb_ref = held

    def step(at, carry):
        span = pl.ds(pl.multiple_of(at * tile, tile), tile)
        rows = jnp.concatenate([ref[:, span] for ref in blocks], axis=0)
        both = jnp.concatenate([ka_ref[span, :], kb_ref[span, :]], axis=1)
        for start, weight in ((0, qa_ref[span, :]), (half, qb_ref[span, :]), (2 * half, both)):
            total[:, start : start + weight.shape[1]] += jnp.dot(
                rows, weight, preferred_element_type=jnp.float32
            )
        return carry

    per = chunk // tile
    for at, group in enumerate(copies):
        for copy in group:
            copy.wait()
        lax.fori_loop(at * per, (at + 1) * per, step, 0)
    flip = core_ref[0] == 0
    value = total[...].astype(jnp.bfloat16)
    query_out[...] = value[:, : 2 * half]
    left, right = value[:, 2 * half : 2 * half + HEAD], value[:, 2 * half + HEAD :]
    pair_out[:, :HEAD] = jnp.where(flip, left, right)
    pair_out[:, HEAD:] = jnp.where(flip, right, left)


def project(core, blocks, weights):
    width = blocks[0].shape[1]
    count = sum(block.shape[0] for block in blocks)
    qcols = 2 * weights[0].shape[1]
    kcols = 2 * weights[2].shape[1]
    vmem = pl.BlockSpec(memory_space=pltpu.VMEM)
    return pl.pallas_call(
        functools.partial(project_body, 1024),
        in_specs=[pl.BlockSpec(memory_space=pltpu.SMEM)]
        + [vmem] * len(blocks)
        + [pl.BlockSpec(memory_space=pl.ANY)] * len(weights),
        out_specs=[vmem, vmem],
        out_shape=[
            jax.ShapeDtypeStruct((count, qcols), jnp.bfloat16),
            jax.ShapeDtypeStruct((count, kcols), jnp.bfloat16),
        ],
        scratch_shapes=[pltpu.VMEM((count, qcols + kcols), jnp.float32)]
        + [pltpu.VMEM(weight.shape, jnp.bfloat16) for weight in weights]
        + [pltpu.SemaphoreType.DMA((len(weights), 4))],
        compiler_params=params(32),
        cost_estimate=cost(
            2 * count * width * (qcols + kcols), 2 * width * (count + qcols + kcols)
        ),
        name="project",
    )(core, *blocks, *weights)


def fetch(weights, held, arrived, first):
    half = weights[0].shape[0]
    chunks = arrived.shape[0]
    tile = held.shape[1] // chunks
    copies = [
        [
            pltpu.make_async_copy(
                weight.at[:, pl.ds(first + at * tile, tile)],
                held.at[pl.ds(kind * half, half), pl.ds(at * tile, tile)],
                arrived.at[at, kind],
            )
            for kind, weight in enumerate(weights)
        ]
        for at in range(chunks)
    ]
    for group in copies:
        for copy in group:
            copy.start()
    return copies


def multiply(rows, held, copies, out_refs):
    tile = held.shape[1] // len(copies)
    for at, group in enumerate(copies):
        for copy in group:
            copy.wait()
        result = jnp.dot(
            rows, held[:, at * tile : (at + 1) * tile], preferred_element_type=jnp.float32
        ).astype(jnp.bfloat16)
        for block, pieces in enumerate(out_refs):
            width = pieces[0].shape[1]
            left = at * tile % width
            pieces[at * tile // width][:, left : left + tile] = result[
                block * ROWS : (block + 1) * ROWS
            ]


def attend_body(order, core_ref, place_ref, *refs):
    blocks = len(RING)
    ins, refs = refs[: -8 - blocks], refs[-8 - blocks :]
    weights, mixed_ref, out_refs = refs[:2], refs[2], refs[3 : 3 + blocks]
    query_ref, own_ref, other_ref, held, arrived = refs[3 + blocks :]
    copies = fetch(weights, held, arrived, 0)
    core = core_ref[0]
    parts = len(ins) // 3
    for kind, whole in enumerate((query_ref, own_ref, other_ref)):
        at = 0
        for part in ins[kind * parts : (kind + 1) * parts]:
            for top in range(0, part.shape[0], ROWS):
                place = pl.ds(pl.multiple_of(place_ref[order[at]] * ROWS, ROWS), ROWS)
                whole[place, :] = part[top : top + ROWS]
                at += 1
    count, qcols = query_ref.shape
    heads = qcols // HEAD
    block = 2 * ROWS
    scale = 1.0 / math.sqrt(HEAD)
    shift = ROWS.bit_length() - 1
    for step in range(count // block):
        rows = slice(step * block, (step + 1) * block)
        span = (step + 1) * block
        query = jnp.concatenate(
            [query_ref[rows, h * HEAD : (h + 1) * HEAD] for h in range(heads)], axis=0
        )
        contract = (((1,), (1,)), ((), ()))
        row = lax.broadcasted_iota(jnp.int32, (block, block), 0)
        col = lax.broadcasted_iota(jnp.int32, (block, block), 1)
        own_seen = jnp.concatenate([col <= row] * heads, axis=0)
        other_seen = jnp.concatenate(
            [jnp.right_shift(col, shift) < jnp.right_shift(row, shift) + core] * heads, axis=0
        )

        def scores_of(ref, seen):
            raw = lax.dot_general(
                query, ref[:span, :HEAD], contract, preferred_element_type=jnp.float32
            )
            tail = jnp.where(seen, raw[:, span - block :], -jnp.inf)
            if span == block:
                return tail
            return jnp.concatenate([raw[:, : span - block], tail], axis=1)

        scores = jnp.concatenate(
            [scores_of(own_ref, own_seen), scores_of(other_ref, other_seen)], axis=1
        )
        peak = jnp.max(scores, axis=-1, keepdims=True)
        probs = jnp.exp((scores - peak) * scale).astype(jnp.bfloat16)
        ones = jnp.ones((span, HEAD), jnp.bfloat16)
        total = jnp.zeros((block * heads, 2 * HEAD), jnp.float32)
        for part, ref in enumerate((own_ref, other_ref)):
            values = jnp.concatenate([ref[:span, HEAD:], ones], axis=1)
            total += jnp.dot(
                probs[:, part * span : (part + 1) * span],
                values,
                preferred_element_type=jnp.float32,
            )
        mixed = (total[:, :HEAD] / total[:, HEAD:]).astype(jnp.bfloat16)
        for part in range(block // ROWS):
            slot = place_ref[8 + step * (block // ROWS) + part]
            place = pl.ds(pl.multiple_of(slot * ROWS, ROWS), ROWS)
            for h in range(heads):
                top = h * block + part * ROWS
                mixed_ref[place, h * HEAD : (h + 1) * HEAD] = mixed[top : top + ROWS]

    multiply(mixed_ref[count // 2 :], held, copies, [[ref] for ref in out_refs])


def attend(core, places, order, queries, own, other, weights):
    count, qcols = sum(q.shape[0] for q in queries), queries[0].shape[1]
    kcols = own[0].shape[1]
    args = [*queries, *own, *other]
    vmem = pl.BlockSpec(memory_space=pltpu.VMEM)
    depth, width = weights[0].shape
    return pl.pallas_call(
        functools.partial(attend_body, order),
        in_specs=[pl.BlockSpec(memory_space=pltpu.SMEM)] * 2
        + [vmem] * len(args)
        + [pl.BlockSpec(memory_space=pl.ANY)] * 2,
        out_specs=[vmem] * (1 + len(RING)),
        out_shape=[jax.ShapeDtypeStruct((count, qcols), jnp.bfloat16)]
        + [jax.ShapeDtypeStruct((ROWS, width // HALVES), jnp.bfloat16)] * len(RING),
        scratch_shapes=[pltpu.VMEM((count, cols), jnp.bfloat16) for cols in (qcols, kcols, kcols)]
        + [
            pltpu.VMEM((2 * depth, width // HALVES), jnp.bfloat16),
            pltpu.SemaphoreType.DMA((width // HALVES // TILE, 2)),
        ],
        compiler_params=params(48),
        cost_estimate=cost(8 * count * count * qcols, 4 * count * qcols + 4 * depth * width),
        name="attend",
    )(core, places, *args, *weights)


def output_body(side, first, pieces, mixed_ref, *refs):
    weights, out_refs, (held, arrived) = refs[:2], list(refs[2:-2]), refs[-2:]
    copies = fetch(weights, held, arrived, first)
    count = mixed_ref.shape[0] // 2
    outs = [[out_refs.pop(0) for _ in range(piece)] for piece in pieces]
    multiply(mixed_ref[side * count : (side + 1) * count], held, copies, outs)


def output(mixed, weights, side, first, width, pieces):
    depth = weights[0].shape[0]
    count = mixed.shape[0] // 2
    vmem = pl.BlockSpec(memory_space=pltpu.VMEM)
    widths = [width // piece for piece in pieces for _ in range(piece)]
    result = list(
        pl.pallas_call(
            functools.partial(output_body, side, first, pieces),
            in_specs=[vmem] + [pl.BlockSpec(memory_space=pl.ANY)] * 2,
            out_specs=[vmem] * len(widths),
            out_shape=[jax.ShapeDtypeStruct((ROWS, w), jnp.bfloat16) for w in widths],
            scratch_shapes=[
                pltpu.VMEM((2 * depth, width), jnp.bfloat16),
                pltpu.SemaphoreType.DMA((width // TILE, 2)),
            ],
            compiler_params=params(32),
            cost_estimate=cost(
                4 * count * depth * width, 2 * (2 * depth * width + count * width)
            ),
            name="output",
        )(mixed, *weights)
    )
    return [[result.pop(0) for _ in range(piece)] for piece in pieces]


def mark_body(*refs):
    del refs


def mark(*blocks):
    anywhere = [pl.BlockSpec(memory_space=pl.ANY)] * len(blocks)
    return pl.pallas_call(
        mark_body,
        in_specs=anywhere,
        out_specs=anywhere,
        out_shape=[jax.ShapeDtypeStruct(block.shape, block.dtype) for block in blocks],
        input_output_aliases={at: at for at in range(len(blocks))},
        compiler_params=params(),
        cost_estimate=cost(6.5e10, 4096),
        name="mark",
    )(*blocks)


def sums_body(shapes, *refs):
    outs = refs[-len(shapes) :]
    first = 0
    for out_ref, (offset, starts) in zip(outs, shapes):
        step = min(ref.shape[1] for ref in refs[first : first + len(starts)])
        for left in range(0, out_ref.shape[1], step):
            total = None
            for at, start in enumerate(starts):
                ref = refs[first + at]
                col = offset + left - start
                if 0 <= col < ref.shape[1]:
                    term = ref[:, col : col + step].astype(jnp.float32)
                    total = term if total is None else total + term
            out_ref[:, left : left + step] = total.astype(jnp.bfloat16)
        first += len(starts)


def sums(*groups, name="sums", after=()):
    args = [array for _, terms in groups for array, _ in terms]
    shapes = tuple((first, tuple(start for _, start in terms)) for (first, _), terms in groups)
    result = pl.pallas_call(
        functools.partial(sums_body, shapes),
        in_specs=[pl.BlockSpec(memory_space=pltpu.VMEM)] * len(args)
        + [pl.BlockSpec(memory_space=pl.ANY)] * len(after),
        out_shape=[
            jax.ShapeDtypeStruct((terms[0][0].shape[0], width), jnp.bfloat16)
            for (_, width), terms in groups
        ],
        compiler_params=params(16),
        cost_estimate=cost(sum(a.size for a in args), 3 * sum(a.size for a in args)),
        name=name,
    )(*args, *after)
    return result if len(groups) > 1 else result[0]


def terms_body(block_ref, codes_ref, exps_ref, *out_refs):
    scale = jnp.exp2(exps_ref[...].astype(jnp.float32))
    lane = lax.broadcasted_iota(jnp.int32, scale.shape, 1)
    count = codes_ref.shape[0]
    for at, out_ref in enumerate(out_refs):
        for side in range(2):
            block = block_ref[2 * at + side]
            cols = pl.ds(pl.multiple_of(block * HEAD, HEAD), HEAD)
            mine = jnp.sum(jnp.where(lane == block, scale, 0.0), axis=1, keepdims=True)
            out_ref[side * count : (side + 1) * count] = (
                codes_ref[:, cols].astype(jnp.float32) * mine
            ).astype(jnp.bfloat16)


def terms(blocks, codes, exps):
    count, width = codes.shape
    vmem = pl.BlockSpec(memory_space=pltpu.VMEM)
    return pl.pallas_call(
        terms_body,
        in_specs=[pl.BlockSpec(memory_space=pltpu.SMEM), vmem, vmem],
        out_shape=[jax.ShapeDtypeStruct((2 * count, HEAD), jnp.bfloat16)] * len(RING),
        compiler_params=params(),
        cost_estimate=cost(codes.size, 4 * codes.size),
        name="terms",
    )(blocks, codes, exps)


def outer_body(replicas, *refs):
    mine_refs, theirs_ref, momentum_ref, table_ref, momentum_out, rebuilt_ref = (
        refs[:3],
        *refs[3:],
    )
    table = table_ref[...]

    def rotate(values):
        return jnp.dot(
            values, table, precision=lax.Precision.HIGHEST, preferred_element_type=jnp.float32
        )

    summed = theirs_ref[...].astype(jnp.float32)
    for ref in mine_refs:
        summed += ref[: summed.shape[0]].astype(jnp.float32)
    averaged = rotate(summed / replicas)
    fresh = 0.9 * momentum_ref[...] + averaged
    momentum_out[...] = fresh
    turned = rotate(0.7 * (averaged + 0.9 * fresh))
    scales = (jnp.max(jnp.abs(turned), axis=-1, keepdims=True) + 1e-06).astype(jnp.bfloat16)
    scales = scales.astype(jnp.float32)
    codes = (turned / scales).astype(jnp.bfloat16)
    rebuilt_ref[...] = rotate(codes.astype(jnp.float32) * scales).astype(jnp.bfloat16)


def outer(mine, theirs, momentum, table, replicas):
    return pl.pallas_call(
        functools.partial(outer_body, replicas),
        out_shape=[
            jax.ShapeDtypeStruct(momentum.shape, jnp.float32),
            jax.ShapeDtypeStruct(momentum.shape, jnp.bfloat16),
        ],
        compiler_params=params(),
        cost_estimate=cost(40 * theirs.size * HEAD, 12 * theirs.size),
        name="outer",
    )(*mine, theirs, momentum, table)


def apply_body(block_ref, params_ref, *refs):
    rebuilt_refs, out_ref = refs[:-1], refs[-1]
    count = out_ref.shape[0]
    for at, rebuilt_ref in enumerate(rebuilt_refs):
        for side in range(2):
            cols = pl.ds(pl.multiple_of(block_ref[2 * at + side] * HEAD, HEAD), HEAD)
            rebuilt = rebuilt_ref[side * count : (side + 1) * count].astype(jnp.float32)
            out_ref[:, cols] = (params_ref[:, cols].astype(jnp.float32) - rebuilt).astype(
                jnp.bfloat16
            )


def apply(blocks, old, rebuilt):
    vmem = pl.BlockSpec(memory_space=pltpu.VMEM)
    return pl.pallas_call(
        apply_body,
        in_specs=[pl.BlockSpec(memory_space=pltpu.SMEM)] + [vmem] * (1 + len(rebuilt)),
        out_shape=jax.ShapeDtypeStruct(old.shape, jnp.bfloat16),
        compiler_params=params(),
        cost_estimate=cost(old.size, 6 * old.size),
        name="apply",
    )(blocks, old, *rebuilt)


def swap(block, axis):
    return lax.ppermute(block, axis, [(0, 1), (1, 0)])


def hop(block, axis, way):
    at = (0, 2, 1, 3) if axis == Y else (0, 1, 2, 3)
    return lax.ppermute(block, axis, [(at[i], at[(i + way) % 4]) for i in range(4)])


def add(*blocks):
    total = blocks[0].astype(jnp.float32)
    for block in blocks[1:]:
        total = total + block.astype(jnp.float32)
    return total.astype(jnp.bfloat16)


def wait(*blocks):
    return lax.optimization_barrier(blocks)


def tie(block, *others):
    return lax.optimization_barrier((block, *others))[0]


def local(
    tokens, norm_gain, query_weight, kv_weight, out_weight, pseudo_grad, grad_exps, old, momentum
):
    core, z, yhi = lax.axis_index("core"), lax.axis_index("z"), lax.axis_index("yhi")
    x, ylo = lax.axis_index("x"), lax.axis_index("ylo")
    replicas = lax.axis_size(REPLICA)
    place = jnp.stack([(yhi ^ side) * 4 + (z + r) % 4 for side in range(2) for r in RING])
    chip = jnp.arange(8, dtype=jnp.int32)
    away = (chip % 4 - z) % 4
    slots = ((chip // 4) ^ yhi) * 4 + jnp.where(away < 2, away, 5 - away)
    share = jnp.stack([((x + r) % 4) * 2 + (ylo ^ side) for r in RING for side in range(2)])
    core, place, slots, share = (
        v.astype(jnp.int32).reshape(-1) for v in (core, place, slots, share)
    )
    places = jnp.concatenate([place, slots])

    block, h1, h2 = normalize(tokens, norm_gain)
    relay1, relay2 = hop(h1, Y, 1), hop(h2, Y, -1)
    below, above = hop(block, "z", 1), hop(block, "z", -1)
    kv_theirs = swap(tie(kv_weight, block), "core")
    at0, at1, at3, at2 = terms(share, tie(pseudo_grad[0], block), grad_exps[0])
    relay1, relay2, kv_theirs, at0, at1, at2, at3, query_weight = wait(
        relay1, relay2, kv_theirs, at0, at1, at2, at3, query_weight
    )
    query_theirs = swap(query_weight, "core")
    partner = jnp.concatenate([hop(relay1, Y, 1), hop(relay2, Y, -1)], axis=0)
    below, above = mark(below, above)
    far = hop(below, "z", 1)
    partner, above, below = wait(partner, above, below)
    pabove, pbelow = hop(partner, "z", -1), hop(partner, "z", 1)
    weights = [query_weight, query_theirs, kv_weight, kv_theirs]
    query_a, pair_a = project(core, [block, above, below, partner], weights)
    at2, at3 = wait(at2, at3, partner)[:2]
    x2, x3 = hop(at2, "x", 1), hop(at3, "x", -1)
    pabove, far, query_a, pair_a, x2, x3, at1, out_weight = wait(
        pabove, far, query_a, pair_a, x2, x3, at1, out_weight
    )
    pfar = hop(pabove, "z", -1)
    out_theirs = swap(out_weight, "core")
    query_m, pair_m = project(core, [far, pabove], weights)
    passed = hop(add(at1, x2), "x", 1)
    other_a, other_m = swap(pair_a, "core"), swap(pair_m, "core")
    pbelow, pfar, passed, query_m = wait(pbelow, pfar, passed, query_m)
    query_l, pair_l = project(core, [pbelow, pfar], weights)
    other_l = swap(pair_l, "core")
    out_weights = (out_weight, out_theirs)
    mixed, q0a, qupa, qdowna, qfara = attend(
        core,
        places,
        (0, 1, 2, 4, 3, 5, 6, 7),
        (query_a, query_m, query_l),
        (pair_a, pair_m, pair_l),
        (other_a, other_m, other_l),
        out_weights,
    )

    full = out_weight.shape[1]
    half = full // HALVES
    mixed, far_a = wait(mixed, qfara)
    far_a = hop(far_a, "z", 1)
    (q0b,), (qupb,), (qdownb,), (qfarb,) = output(mixed, out_weights, 1, half, half, (1, 1, 1, 1))
    far_b = hop(qfarb, "z", -1)
    mine = (at0, passed, x3)
    count = momentum.shape[0]
    sent, q0b, mixed = wait(add(*(part[count:] for part in mine)), q0b, mixed)
    theirs = swap(sent, "ylo")
    (o0,), (oup,), (odown,), (ofara, ofarb) = output(mixed, out_weights, 0, 0, full, (1, 1, 1, 2))
    far_a, far_b, o0 = wait(far_a, far_b, o0)
    up, down = sums(
        ((0, full), ((qupa, 0), (qupb, half), (far_a, 0))),
        ((0, full), ((qdowna, 0), (qdownb, half), (far_b, half))),
    )
    up, down, theirs, ofara, ofarb = wait(up, down, theirs, ofara, ofarb)
    up, down = hop(up, "z", 1), hop(down, "z", -1)
    ofara, ofarb = hop(ofara, "z", 1), hop(ofarb, "z", -1)
    new_momentum, rebuilt = outer(mine, theirs, momentum, hadamard_table(HEAD), replicas)
    beside = swap(rebuilt, "ylo")
    both = jnp.concatenate([rebuilt, beside], axis=0)
    before = hop(both, "x", 1)
    up, down, before, both = wait(up, down, before, both)
    s1, s2 = sums(
        *(((at, half), ((q0a, 0), (q0b, half), (up, 0), (down, 0))) for at in (0, half))
    )
    oup, odown = sums(
        ((0, full), ((oup, 0), (ofara, 0))),
        ((0, full), ((odown, 0), (ofarb, half))),
        after=(s1,),
    )
    oup, odown = hop(oup, "z", 1), hop(odown, "z", -1)
    s1, s2 = hop(s1, Y, 1), hop(s2, Y, -1)
    after = hop(both, "x", -1)
    s1, s2, before = wait(s1, s2, before)
    s1, s2 = hop(s1, Y, 1), hop(s2, Y, -1)
    ahead = hop(before, "x", 1)
    new_params = apply(share, old, [both, after, before, ahead])
    o0, new_params = wait(o0, new_params)
    attended = sums(
        ((0, full), ((o0, 0), (oup, 0), (odown, 0), (s1, 0), (s2, half))), name="finish"
    )
    return (attended, new_params, new_momentum)


def solution(mesh):
    fine = Mesh(mesh.devices.reshape(4, 2, 2, 4, 2), ("x", "ylo", "yhi", "z", "core"))
    every = REPLICA + TENSOR
    return jax.shard_map(
        local,
        mesh=fine,
        in_specs=(
            P(every, None),
            P(),
            P(None, TENSOR),
            P(None, TENSOR),
            P(TENSOR, None),
            P(REPLICA, TENSOR, None),
            P(REPLICA, TENSOR, None),
            P(TENSOR, None),
            P(TENSOR, REPLICA),
        ),
        out_specs=(P(every, None), P(TENSOR, None), P(TENSOR, REPLICA)),
        check_vma=False,
    )
```

```python
import functools
import math

import jax
import jax.numpy as jnp
from jax import lax
from jax.experimental import pallas as pl
from jax.experimental.pallas import tpu as pltpu
from jax.sharding import Mesh
from jax.sharding import PartitionSpec as P

HEAD = 128
REPLICA = ("x", "ylo")
TENSOR = ("yhi", "z", "core")
ROWS = 64
RING = (0, 1, -1, 2)
Y = ("ylo", "yhi")
HALVES = 2
TILE = 1024
MIB = 1024 * 1024


def params(mib=8):
    return pltpu.CompilerParams(vmem_limit_bytes=mib * MIB)


def cost(flops, moved):
    return pl.CostEstimate(flops=int(flops), bytes_accessed=int(moved), transcendentals=0)


def hadamard_table(width):
    index = jnp.arange(width, dtype=jnp.int32)
    common = jnp.bitwise_and(index[:, None], index[None, :])
    parity = jnp.zeros((width, width), jnp.int32)
    for bit in range(int(math.log2(width))):
        parity = parity + jnp.bitwise_and(jnp.right_shift(common, bit), 1)
    sign = 1.0 - 2.0 * jnp.bitwise_and(parity, 1).astype(jnp.float32)
    return sign / math.sqrt(width)


def norm_body(rows_ref, gain_ref, whole_ref, *half_refs):
    values = rows_ref[...].astype(jnp.float32)
    power = jnp.mean(values * values, axis=-1, keepdims=True)
    normed = (values * lax.rsqrt(power + 1e-05) * gain_ref[...]).astype(jnp.bfloat16)
    whole_ref[...] = normed
    count = normed.shape[0] // HALVES
    for at, half_ref in enumerate(half_refs):
        half_ref[...] = normed[at * count : (at + 1) * count]


def normalize(rows, gain):
    count, width = rows.shape
    return pl.pallas_call(
        norm_body,
        out_shape=[
            jax.ShapeDtypeStruct((c, width), jnp.bfloat16)
            for c in [count] + [count // HALVES] * HALVES
        ],
        compiler_params=params(12),
        cost_estimate=cost(4 * rows.size, 6 * rows.size),
        name="normalize",
    )(rows, gain.reshape(1, width))


def project_body(core_ref, *refs):
    blocks, refs = refs[:-12], refs[-12:]
    weights, (query_out, pair_out, total), held, arrived = refs[:4], refs[4:7], refs[7:11], refs[11]
    half = weights[0].shape[1]
    depth = weights[0].shape[0]
    chunks = arrived.shape[1]
    chunk = depth // chunks

    def copies_of(at):
        span = pl.ds(pl.multiple_of(at * chunk, chunk), chunk)
        return [
            pltpu.make_async_copy(weight.at[span, :], place.at[span, :], arrived.at[kind, at])
            for kind, (weight, place) in enumerate(zip(weights, held))
        ]

    for at in range(chunks):
        for copy in copies_of(at):
            copy.start()
    total[...] = jnp.zeros_like(total)
    qa_ref, qb_ref, ka_ref, kb_ref = held

    def step(at, carry):
        for copy in copies_of(at):
            copy.wait()
        span = pl.ds(pl.multiple_of(at * chunk, chunk), chunk)
        rows = jnp.concatenate([ref[:, span] for ref in blocks], axis=0)
        both = jnp.concatenate([ka_ref[span, :], kb_ref[span, :]], axis=1)
        for start, weight in ((0, qa_ref[span, :]), (half, qb_ref[span, :]), (2 * half, both)):
            total[:, start : start + weight.shape[1]] += jnp.dot(
                rows, weight, preferred_element_type=jnp.float32
            )
        return carry

    lax.fori_loop(0, chunks, step, 0)
    flip = core_ref[0] == 0
    value = total[...].astype(jnp.bfloat16)
    query_out[...] = value[:, : 2 * half]
    left, right = value[:, 2 * half : 2 * half + HEAD], value[:, 2 * half + HEAD :]
    pair_out[:, :HEAD] = jnp.where(flip, left, right)
    pair_out[:, HEAD:] = jnp.where(flip, right, left)


def project(core, blocks, weights):
    width = blocks[0].shape[1]
    count = sum(block.shape[0] for block in blocks)
    qcols = 2 * weights[0].shape[1]
    kcols = 2 * weights[2].shape[1]
    vmem = pl.BlockSpec(memory_space=pltpu.VMEM)
    return pl.pallas_call(
        project_body,
        in_specs=[pl.BlockSpec(memory_space=pltpu.SMEM)]
        + [vmem] * len(blocks)
        + [pl.BlockSpec(memory_space=pl.ANY)] * len(weights),
        out_specs=[vmem, vmem],
        out_shape=[
            jax.ShapeDtypeStruct((count, qcols), jnp.bfloat16),
            jax.ShapeDtypeStruct((count, kcols), jnp.bfloat16),
        ],
        scratch_shapes=[pltpu.VMEM((count, qcols + kcols), jnp.float32)]
        + [pltpu.VMEM(weight.shape, jnp.bfloat16) for weight in weights]
        + [pltpu.SemaphoreType.DMA((len(weights), width // TILE))],
        compiler_params=params(56),
        cost_estimate=cost(
            3 * count * width * (qcols + kcols), 2 * width * (count + qcols + kcols)
        ),
        name="project",
    )(core, *blocks, *weights)


def copies_of(weights, held, arrived, first, at):
    half = weights[0].shape[0]
    span = pl.ds(pl.multiple_of(at * TILE, TILE), TILE)
    return [
        pltpu.make_async_copy(
            weight.at[:, pl.ds(pl.multiple_of(first + at * TILE, TILE), TILE)],
            held.at[pl.ds(kind * half, half), span],
            arrived.at[at, kind],
        )
        for kind, weight in enumerate(weights)
    ]


def fetch(weights, held, arrived, first):
    for at in range(held.shape[1] // TILE):
        for copy in copies_of(weights, held, arrived, first, at):
            copy.start()


def multiply(rows_of, weights, held, arrived, first, out_refs):
    tiles = held.shape[1] // TILE
    parts = max(len(pieces) for pieces in out_refs)
    for part in range(parts):

        def step(at, carry, part=part):
            for copy in copies_of(weights, held, arrived, first, at):
                copy.wait()
            span = pl.ds(pl.multiple_of(at * TILE, TILE), TILE)
            result = jnp.dot(rows_of(), held[:, span], preferred_element_type=jnp.float32)
            result = result.astype(jnp.bfloat16)
            for block, pieces in enumerate(out_refs):
                back = part * (tiles // parts) if len(pieces) == parts else 0
                there = pl.ds(pl.multiple_of((at - back) * TILE, TILE), TILE)
                pieces[part if len(pieces) == parts else 0][:, there] = result[
                    block * ROWS : (block + 1) * ROWS
                ]
            return carry

        lax.fori_loop(part * (tiles // parts), (part + 1) * (tiles // parts), step, 0)


def attend_body(order, core_ref, place_ref, *refs):
    blocks = len(RING)
    ins, refs = refs[: -8 - blocks], refs[-8 - blocks :]
    weights, mixed_ref, out_refs = refs[:2], refs[2], refs[3 : 3 + blocks]
    query_ref, own_ref, other_ref, held, arrived = refs[3 + blocks :]
    fetch(weights, held, arrived, 0)
    core = core_ref[0]
    parts = len(ins) // 3
    for kind, whole in enumerate((query_ref, own_ref, other_ref)):
        at = 0
        for part in ins[kind * parts : (kind + 1) * parts]:
            for top in range(0, part.shape[0], ROWS):
                place = pl.ds(pl.multiple_of(place_ref[order[at]] * ROWS, ROWS), ROWS)
                whole[place, :] = part[top : top + ROWS]
                at += 1
    count, qcols = query_ref.shape
    heads = qcols // HEAD
    block = 2 * ROWS
    scale = 1.0 / math.sqrt(HEAD)
    shift = ROWS.bit_length() - 1
    for step in range(count // block):
        rows = slice(step * block, (step + 1) * block)
        span = (step + 1) * block
        query = jnp.concatenate(
            [query_ref[rows, h * HEAD : (h + 1) * HEAD] for h in range(heads)], axis=0
        )
        contract = (((1,), (1,)), ((), ()))
        row = lax.broadcasted_iota(jnp.int32, (block, block), 0)
        col = lax.broadcasted_iota(jnp.int32, (block, block), 1)
        own_seen = jnp.concatenate([col <= row] * heads, axis=0)
        other_seen = jnp.concatenate(
            [jnp.right_shift(col, shift) < jnp.right_shift(row, shift) + core] * heads, axis=0
        )

        def scores_of(ref, seen):
            raw = lax.dot_general(
                query, ref[:span, :HEAD], contract, preferred_element_type=jnp.float32
            )
            tail = jnp.where(seen, raw[:, span - block :], -jnp.inf)
            if span == block:
                return tail
            return jnp.concatenate([raw[:, : span - block], tail], axis=1)

        scores = jnp.concatenate(
            [scores_of(own_ref, own_seen), scores_of(other_ref, other_seen)], axis=1
        )
        peak = jnp.max(scores, axis=-1, keepdims=True)
        probs = jnp.exp((scores - peak) * scale).astype(jnp.bfloat16)
        ones = jnp.ones((span, HEAD), jnp.bfloat16)
        total = jnp.zeros((block * heads, 2 * HEAD), jnp.float32)
        for part, ref in enumerate((own_ref, other_ref)):
            values = jnp.concatenate([ref[:span, HEAD:], ones], axis=1)
            total += jnp.dot(
                probs[:, part * span : (part + 1) * span],
                values,
                preferred_element_type=jnp.float32,
            )
        mixed = (total[:, :HEAD] / total[:, HEAD:]).astype(jnp.bfloat16)
        for part in range(block // ROWS):
            slot = place_ref[8 + step * (block // ROWS) + part]
            place = pl.ds(pl.multiple_of(slot * ROWS, ROWS), ROWS)
            for h in range(heads):
                top = h * block + part * ROWS
                mixed_ref[place, h * HEAD : (h + 1) * HEAD] = mixed[top : top + ROWS]

    multiply(
        lambda: mixed_ref[count // 2 :], weights, held, arrived, 0, [[ref] for ref in out_refs]
    )


def attend(core, places, order, queries, own, other, weights):
    count, qcols = sum(q.shape[0] for q in queries), queries[0].shape[1]
    kcols = own[0].shape[1]
    args = [*queries, *own, *other]
    vmem = pl.BlockSpec(memory_space=pltpu.VMEM)
    depth, width = weights[0].shape
    return pl.pallas_call(
        functools.partial(attend_body, order),
        in_specs=[pl.BlockSpec(memory_space=pltpu.SMEM)] * 2
        + [vmem] * len(args)
        + [pl.BlockSpec(memory_space=pl.ANY)] * 2,
        out_specs=[vmem] * (1 + len(RING)),
        out_shape=[jax.ShapeDtypeStruct((count, qcols), jnp.bfloat16)]
        + [jax.ShapeDtypeStruct((ROWS, width // HALVES), jnp.bfloat16)] * len(RING),
        scratch_shapes=[pltpu.VMEM((count, cols), jnp.bfloat16) for cols in (qcols, kcols, kcols)]
        + [
            pltpu.VMEM((2 * depth, width // HALVES), jnp.bfloat16),
            pltpu.SemaphoreType.DMA((width // HALVES // TILE, 2)),
        ],
        compiler_params=params(56),
        cost_estimate=cost(8 * count * count * qcols, 4 * count * qcols + 4 * depth * width),
        name="attend",
    )(core, places, *args, *weights)


def output_body(side, first, pieces, mixed_ref, *refs):
    weights, out_refs, (held, arrived) = refs[:2], list(refs[2:-2]), refs[-2:]
    fetch(weights, held, arrived, first)
    count = mixed_ref.shape[0] // 2
    outs = [[out_refs.pop(0) for _ in range(piece)] for piece in pieces]
    rows_of = lambda: mixed_ref[side * count : (side + 1) * count]
    multiply(rows_of, weights, held, arrived, first, outs)


def output(mixed, weights, side, first, width, pieces):
    depth = weights[0].shape[0]
    count = mixed.shape[0] // 2
    vmem = pl.BlockSpec(memory_space=pltpu.VMEM)
    widths = [width // piece for piece in pieces for _ in range(piece)]
    result = list(
        pl.pallas_call(
            functools.partial(output_body, side, first, pieces),
            in_specs=[vmem] + [pl.BlockSpec(memory_space=pl.ANY)] * 2,
            out_specs=[vmem] * len(widths),
            out_shape=[jax.ShapeDtypeStruct((ROWS, w), jnp.bfloat16) for w in widths],
            scratch_shapes=[
                pltpu.VMEM((2 * depth, width), jnp.bfloat16),
                pltpu.SemaphoreType.DMA((width // TILE, 2)),
            ],
            compiler_params=params(56),
            cost_estimate=cost(
                4 * count * depth * width, 2 * (2 * depth * width + count * width)
            ),
            name="output",
        )(mixed, *weights)
    )
    return [[result.pop(0) for _ in range(piece)] for piece in pieces]


def mark_body(*refs):
    del refs


def mark(*blocks):
    anywhere = [pl.BlockSpec(memory_space=pl.ANY)] * len(blocks)
    return pl.pallas_call(
        mark_body,
        in_specs=anywhere,
        out_specs=anywhere,
        out_shape=[jax.ShapeDtypeStruct(block.shape, block.dtype) for block in blocks],
        input_output_aliases={at: at for at in range(len(blocks))},
        compiler_params=params(),
        cost_estimate=cost(7e10, 4096),
        name="mark",
    )(*blocks)


def pick_body(below_ref, above_ref, first_ref, second_ref):
    count = first_ref.shape[0]
    first_ref[...] = below_ref[:count]
    second_ref[...] = above_ref[count:]


def pick(below, above):
    shape = jax.ShapeDtypeStruct((below.shape[0] // HALVES, below.shape[1]), below.dtype)
    return pl.pallas_call(
        pick_body,
        out_shape=[shape, shape],
        compiler_params=params(),
        cost_estimate=cost(1e8, 4 * below.size),
        name="pick",
    )(below, above)


def sums_body(shapes, *refs):
    outs = refs[-len(shapes) :]
    first = 0
    for out_ref, (offset, starts) in zip(outs, shapes):
        step = min(ref.shape[1] for ref in refs[first : first + len(starts)])
        for left in range(0, out_ref.shape[1], step):
            total = None
            for at, start in enumerate(starts):
                ref = refs[first + at]
                col = offset + left - start
                if 0 <= col < ref.shape[1]:
                    term = ref[:, col : col + step].astype(jnp.float32)
                    total = term if total is None else total + term
            out_ref[:, left : left + step] = total.astype(jnp.bfloat16)
        first += len(starts)


def sums(*groups, name="sums", after=()):
    args = [array for _, terms in groups for array, _ in terms]
    shapes = tuple((first, tuple(start for _, start in terms)) for (first, _), terms in groups)
    result = pl.pallas_call(
        functools.partial(sums_body, shapes),
        in_specs=[pl.BlockSpec(memory_space=pltpu.VMEM)] * len(args)
        + [pl.BlockSpec(memory_space=pl.ANY)] * len(after),
        out_shape=[
            jax.ShapeDtypeStruct((terms[0][0].shape[0], width), jnp.bfloat16)
            for (_, width), terms in groups
        ],
        compiler_params=params(16),
        cost_estimate=cost(sum(a.size for a in args), 3 * sum(a.size for a in args)),
        name=name,
    )(*args, *after)
    return result if len(groups) > 1 else result[0]


def terms_body(block_ref, codes_ref, exps_ref, *out_refs):
    scale = jnp.exp2(exps_ref[...].astype(jnp.float32))
    lane = lax.broadcasted_iota(jnp.int32, scale.shape, 1)
    count = codes_ref.shape[0]
    for at, out_ref in enumerate(out_refs):
        for side in range(2):
            block = block_ref[2 * at + side]
            cols = pl.ds(pl.multiple_of(block * HEAD, HEAD), HEAD)
            mine = jnp.sum(jnp.where(lane == block, scale, 0.0), axis=1, keepdims=True)
            out_ref[side * count : (side + 1) * count] = (
                codes_ref[:, cols].astype(jnp.float32) * mine
            ).astype(jnp.bfloat16)


def terms(blocks, codes, exps):
    count, width = codes.shape
    vmem = pl.BlockSpec(memory_space=pltpu.VMEM)
    return pl.pallas_call(
        terms_body,
        in_specs=[pl.BlockSpec(memory_space=pltpu.SMEM), vmem, vmem],
        out_shape=[jax.ShapeDtypeStruct((2 * count, HEAD), jnp.bfloat16)] * len(RING),
        compiler_params=params(),
        cost_estimate=cost(codes.size, 4 * codes.size),
        name="terms",
    )(blocks, codes, exps)


def outer_body(replicas, *refs):
    mine_refs, theirs_ref, momentum_ref, table_ref, momentum_out, rebuilt_ref = (
        refs[:3],
        *refs[3:],
    )
    table = table_ref[...]

    def rotate(values):
        return jnp.dot(
            values, table, precision=lax.Precision.HIGHEST, preferred_element_type=jnp.float32
        )

    summed = theirs_ref[...].astype(jnp.float32)
    for ref in mine_refs:
        summed += ref[: summed.shape[0]].astype(jnp.float32)
    averaged = rotate(summed / replicas)
    fresh = 0.9 * momentum_ref[...] + averaged
    momentum_out[...] = fresh
    turned = rotate(0.7 * (averaged + 0.9 * fresh))
    scales = (jnp.max(jnp.abs(turned), axis=-1, keepdims=True) + 1e-06).astype(jnp.bfloat16)
    scales = scales.astype(jnp.float32)
    codes = (turned / scales).astype(jnp.bfloat16)
    rebuilt_ref[...] = rotate(codes.astype(jnp.float32) * scales).astype(jnp.bfloat16)


def outer(mine, theirs, momentum, table, replicas):
    return pl.pallas_call(
        functools.partial(outer_body, replicas),
        out_shape=[
            jax.ShapeDtypeStruct(momentum.shape, jnp.float32),
            jax.ShapeDtypeStruct(momentum.shape, jnp.bfloat16),
        ],
        compiler_params=params(),
        cost_estimate=cost(40 * theirs.size * HEAD, 12 * theirs.size),
        name="outer",
    )(*mine, theirs, momentum, table)


def apply_body(block_ref, params_ref, *refs):
    rebuilt_refs, out_ref = refs[:-1], refs[-1]
    count = out_ref.shape[0]
    for at, rebuilt_ref in enumerate(rebuilt_refs):
        for side in range(2):
            cols = pl.ds(pl.multiple_of(block_ref[2 * at + side] * HEAD, HEAD), HEAD)
            rebuilt = rebuilt_ref[side * count : (side + 1) * count].astype(jnp.float32)
            out_ref[:, cols] = (params_ref[:, cols].astype(jnp.float32) - rebuilt).astype(
                jnp.bfloat16
            )


def apply(blocks, old, rebuilt):
    vmem = pl.BlockSpec(memory_space=pltpu.VMEM)
    return pl.pallas_call(
        apply_body,
        in_specs=[pl.BlockSpec(memory_space=pltpu.SMEM)] + [vmem] * (1 + len(rebuilt)),
        out_shape=jax.ShapeDtypeStruct(old.shape, jnp.bfloat16),
        compiler_params=params(),
        cost_estimate=cost(old.size, 6 * old.size),
        name="apply",
    )(blocks, old, *rebuilt)


def swap(block, axis):
    return lax.ppermute(block, axis, [(0, 1), (1, 0)])


def hop(block, axis, way):
    at = (0, 2, 1, 3) if axis == Y else (0, 1, 2, 3)
    return lax.ppermute(block, axis, [(at[i], at[(i + way) % 4]) for i in range(4)])


def add(*blocks):
    total = blocks[0].astype(jnp.float32)
    for block in blocks[1:]:
        total = total + block.astype(jnp.float32)
    return total.astype(jnp.bfloat16)


def wait(*blocks):
    return lax.optimization_barrier(blocks)


def tie(block, *others):
    return lax.optimization_barrier((block, *others))[0]


def local(
    tokens, norm_gain, query_weight, kv_weight, out_weight, pseudo_grad, grad_exps, old, momentum
):
    core, z, yhi = lax.axis_index("core"), lax.axis_index("z"), lax.axis_index("yhi")
    x, ylo = lax.axis_index("x"), lax.axis_index("ylo")
    replicas = lax.axis_size(REPLICA)
    place = jnp.stack([(yhi ^ side) * 4 + (z + r) % 4 for side in range(2) for r in RING])
    chip = jnp.arange(8, dtype=jnp.int32)
    away = (chip % 4 - z) % 4
    slots = ((chip // 4) ^ yhi) * 4 + jnp.where(away < 2, away, 5 - away)
    share = jnp.stack([((x + r) % 4) * 2 + (ylo ^ side) for r in RING for side in range(2)])
    core, place, slots, share = (
        v.astype(jnp.int32).reshape(-1) for v in (core, place, slots, share)
    )
    places = jnp.concatenate([place, slots])

    block, h1, h2 = normalize(tokens, norm_gain)
    relay1, relay2 = hop(h1, Y, 1), hop(h2, Y, -1)
    below, above = hop(block, "z", 1), hop(block, "z", -1)
    kv_theirs = swap(tie(kv_weight, block), "core")
    at0, at1, at3, at2 = terms(share, tie(pseudo_grad[0], block), grad_exps[0])
    relay1, relay2, kv_theirs, at0, at1, at2, at3, query_weight = wait(
        relay1, relay2, kv_theirs, at0, at1, at2, at3, query_weight
    )
    query_theirs = swap(query_weight, "core")
    partner = jnp.concatenate([hop(relay1, Y, 1), hop(relay2, Y, -1)], axis=0)
    below, above = mark(below, above)
    far1, far2 = pick(below, above)
    partner, above, below = wait(partner, above, below)
    far1, far2 = hop(far1, "z", 1), hop(far2, "z", -1)
    pbelow, pabove = hop(partner, "z", 1), hop(partner, "z", -1)
    weights = [query_weight, query_theirs, kv_weight, kv_theirs]
    query_a, pair_a = project(core, [block, above, below, far1, far2], weights)
    query_a, far1, far2, at2, at3 = wait(query_a, far1, far2, at2, at3)
    x2, x3 = hop(at2, "x", 1), hop(at3, "x", -1)
    pabove, pbelow, query_a, pair_a, x2, x3, at1, out_weight = wait(
        pabove, pbelow, query_a, pair_a, x2, x3, at1, out_weight
    )
    pfar1, pfar2 = pick(pbelow, pabove)
    pfar1, pfar2 = hop(pfar1, "z", 1), hop(pfar2, "z", -1)
    out_theirs = swap(out_weight, "core")
    query_m, pair_m = project(core, [partner, pabove, pbelow], weights)
    passed = hop(add(at1, x2), "x", 1)
    other_a, other_m = swap(pair_a, "core"), swap(pair_m, "core")
    pfar1, pfar2, passed, query_m = wait(pfar1, pfar2, passed, query_m)
    query_l, pair_l = project(core, [pfar1, pfar2], weights)
    other_l = swap(pair_l, "core")
    out_weights = (out_weight, out_theirs)
    mixed, q0a, qupa, qdowna, qfara = attend(
        core,
        places,
        tuple(range(8)),
        (query_a, query_m, query_l),
        (pair_a, pair_m, pair_l),
        (other_a, other_m, other_l),
        out_weights,
    )

    full = out_weight.shape[1]
    half = full // HALVES
    mixed, far_a = wait(mixed, qfara)
    far_a = hop(far_a, "z", 1)
    (q0b,), (qupb,), (qdownb,), (qfarb,) = output(mixed, out_weights, 1, half, half, (1, 1, 1, 1))
    far_b = hop(qfarb, "z", -1)
    mine = (at0, passed, x3)
    count = momentum.shape[0]
    sent, q0b, mixed = wait(add(*(part[count:] for part in mine)), q0b, mixed)
    theirs = swap(sent, "ylo")
    (o0,), (oup,), (odown,), (ofara, ofarb) = output(mixed, out_weights, 0, 0, full, (1, 1, 1, 2))
    far_a, far_b, o0 = wait(far_a, far_b, o0)
    up, down = sums(
        ((0, full), ((qupa, 0), (qupb, half), (far_a, 0))),
        ((0, full), ((qdowna, 0), (qdownb, half), (far_b, half))),
    )
    up, down, theirs, ofara, ofarb = wait(up, down, theirs, ofara, ofarb)
    up, down = hop(up, "z", 1), hop(down, "z", -1)
    ofara, ofarb = hop(ofara, "z", 1), hop(ofarb, "z", -1)
    new_momentum, rebuilt = outer(mine, theirs, momentum, hadamard_table(HEAD), replicas)
    beside = swap(rebuilt, "ylo")
    both = jnp.concatenate([rebuilt, beside], axis=0)
    before = hop(both, "x", 1)
    up, down, before, both = wait(up, down, before, both)
    s1, s2 = sums(
        *(((at, half), ((q0a, 0), (q0b, half), (up, 0), (down, 0))) for at in (0, half))
    )
    oup, odown = sums(
        ((0, full), ((oup, 0), (ofara, 0))),
        ((0, full), ((odown, 0), (ofarb, half))),
        after=(s1,),
    )
    oup, odown = hop(oup, "z", 1), hop(odown, "z", -1)
    s1, s2 = hop(s1, Y, 1), hop(s2, Y, -1)
    after = hop(both, "x", -1)
    s1, s2, before = wait(s1, s2, before)
    s1, s2 = hop(s1, Y, 1), hop(s2, Y, -1)
    ahead = hop(before, "x", 1)
    new_params = apply(share, old, [both, after, before, ahead])
    o0, new_params = wait(o0, new_params)
    attended = sums(
        ((0, full), ((o0, 0), (oup, 0), (odown, 0), (s1, 0), (s2, half))), name="finish"
    )
    return (attended, new_params, new_momentum)


def solution(mesh):
    fine = Mesh(mesh.devices.reshape(4, 2, 2, 4, 2), ("x", "ylo", "yhi", "z", "core"))
    every = REPLICA + TENSOR
    return jax.shard_map(
        local,
        mesh=fine,
        in_specs=(
            P(every, None),
            P(),
            P(None, TENSOR),
            P(None, TENSOR),
            P(TENSOR, None),
            P(REPLICA, TENSOR, None),
            P(REPLICA, TENSOR, None),
            P(TENSOR, None),
            P(TENSOR, REPLICA),
        ),
        out_specs=(P(every, None), P(TENSOR, None), P(TENSOR, REPLICA)),
        check_vma=False,
    )
```

```python
import functools
import math

import jax
import jax.numpy as jnp
from jax import lax
from jax.experimental import pallas as pl
from jax.experimental.pallas import tpu as pltpu
from jax.sharding import Mesh
from jax.sharding import PartitionSpec as P

HEAD = 128
REPLICA = ("x", "ylo")
TENSOR = ("yhi", "z", "core")
ROWS = 64
RING = (0, 1, -1, 2)
Y = ("ylo", "yhi")
HALVES = 2
TILE = 1024
PIECES = (1, 1, 1, HALVES)
MIB = 1024 * 1024


def params(mib=8):
    return pltpu.CompilerParams(vmem_limit_bytes=mib * MIB)


def cost(flops, moved):
    return pl.CostEstimate(flops=int(flops), bytes_accessed=int(moved), transcendentals=0)


def hadamard_table(width):
    index = jnp.arange(width, dtype=jnp.int32)
    common = jnp.bitwise_and(index[:, None], index[None, :])
    parity = jnp.zeros((width, width), jnp.int32)
    for bit in range(int(math.log2(width))):
        parity = parity + jnp.bitwise_and(jnp.right_shift(common, bit), 1)
    sign = 1.0 - 2.0 * jnp.bitwise_and(parity, 1).astype(jnp.float32)
    return sign / math.sqrt(width)


def norm_body(rows_ref, gain_ref, whole_ref, *half_refs):
    values = rows_ref[...].astype(jnp.float32)
    power = jnp.mean(values * values, axis=-1, keepdims=True)
    normed = (values * lax.rsqrt(power + 1e-05) * gain_ref[...]).astype(jnp.bfloat16)
    whole_ref[...] = normed
    count = normed.shape[0] // HALVES
    for at, half_ref in enumerate(half_refs):
        half_ref[...] = normed[at * count : (at + 1) * count]


def normalize(rows, gain):
    count, width = rows.shape
    return pl.pallas_call(
        norm_body,
        out_shape=[
            jax.ShapeDtypeStruct((c, width), jnp.bfloat16)
            for c in [count] + [count // HALVES] * HALVES
        ],
        compiler_params=params(56),
        cost_estimate=cost(4 * rows.size, 6 * rows.size),
        name="normalize",
    )(rows, gain.reshape(1, width))


def project_body(core_ref, *refs):
    blocks, refs = refs[:-12], refs[-12:]
    weights, (query_out, pair_out, total), held, arrived = refs[:4], refs[4:7], refs[7:11], refs[11]
    half = weights[0].shape[1]
    depth = weights[0].shape[0]
    chunks = arrived.shape[1]
    chunk = depth // chunks

    def copies_of(at):
        span = pl.ds(pl.multiple_of(at * chunk, chunk), chunk)
        return [
            pltpu.make_async_copy(weight.at[span, :], place.at[span, :], arrived.at[kind, at])
            for kind, (weight, place) in enumerate(zip(weights, held))
        ]

    for at in range(chunks):
        for copy in copies_of(at):
            copy.start()
    total[...] = jnp.zeros_like(total)
    qa_ref, qb_ref, ka_ref, kb_ref = held

    def step(at, carry):
        for copy in copies_of(at):
            copy.wait()
        span = pl.ds(pl.multiple_of(at * chunk, chunk), chunk)
        rows = jnp.concatenate([ref[:, span] for ref in blocks], axis=0)
        both = jnp.concatenate([ka_ref[span, :], kb_ref[span, :]], axis=1)
        for start, weight in ((0, qa_ref[span, :]), (half, qb_ref[span, :]), (2 * half, both)):
            total[:, start : start + weight.shape[1]] += jnp.dot(
                rows, weight, preferred_element_type=jnp.float32
            )
        return carry

    lax.fori_loop(0, chunks, step, 0)
    flip = core_ref[0] == 0
    value = total[...].astype(jnp.bfloat16)
    query_out[...] = value[:, : 2 * half]
    left, right = value[:, 2 * half : 2 * half + HEAD], value[:, 2 * half + HEAD :]
    pair_out[:, :HEAD] = jnp.where(flip, left, right)
    pair_out[:, HEAD:] = jnp.where(flip, right, left)


def project(core, blocks, weights):
    width = blocks[0].shape[1]
    count = sum(block.shape[0] for block in blocks)
    qcols = 2 * weights[0].shape[1]
    kcols = 2 * weights[2].shape[1]
    vmem = pl.BlockSpec(memory_space=pltpu.VMEM)
    return pl.pallas_call(
        project_body,
        in_specs=[pl.BlockSpec(memory_space=pltpu.SMEM)]
        + [vmem] * len(blocks)
        + [pl.BlockSpec(memory_space=pl.ANY)] * len(weights),
        out_specs=[vmem, vmem],
        out_shape=[
            jax.ShapeDtypeStruct((count, qcols), jnp.bfloat16),
            jax.ShapeDtypeStruct((count, kcols), jnp.bfloat16),
        ],
        scratch_shapes=[pltpu.VMEM((count, qcols + kcols), jnp.float32)]
        + [pltpu.VMEM(weight.shape, jnp.bfloat16) for weight in weights]
        + [pltpu.SemaphoreType.DMA((len(weights), width // TILE))],
        compiler_params=params(56),
        cost_estimate=cost(
            3 * count * width * (qcols + kcols), 2 * width * (count + qcols + kcols)
        ),
        name="project",
    )(core, *blocks, *weights)


def copies_of(weights, held, arrived, first, at):
    half = weights[0].shape[0]
    span = pl.ds(pl.multiple_of(at * TILE, TILE), TILE)
    return [
        pltpu.make_async_copy(
            weight.at[:, pl.ds(pl.multiple_of(first + at * TILE, TILE), TILE)],
            held.at[pl.ds(kind * half, half), span],
            arrived.at[at, kind],
        )
        for kind, weight in enumerate(weights)
    ]


def fetch(weights, held, arrived, first):
    for at in range(held.shape[1] // TILE):
        for copy in copies_of(weights, held, arrived, first, at):
            copy.start()


def multiply(rows_of, weights, held, arrived, first, out_refs):
    tiles = held.shape[1] // TILE
    parts = max(len(pieces) for pieces in out_refs)
    for part in range(parts):

        def step(at, carry, part=part):
            for copy in copies_of(weights, held, arrived, first, at):
                copy.wait()
            span = pl.ds(pl.multiple_of(at * TILE, TILE), TILE)
            result = jnp.dot(rows_of(), held[:, span], preferred_element_type=jnp.float32)
            result = result.astype(jnp.bfloat16)
            for block, pieces in enumerate(out_refs):
                back = part * (tiles // parts) if len(pieces) == parts else 0
                there = pl.ds(pl.multiple_of((at - back) * TILE, TILE), TILE)
                pieces[part if len(pieces) == parts else 0][:, there] = result[
                    block * ROWS : (block + 1) * ROWS
                ]
            return carry

        lax.fori_loop(part * (tiles // parts), (part + 1) * (tiles // parts), step, 0)


def attend_body(order, core_ref, place_ref, *refs):
    ins, refs = refs[: -8 - sum(PIECES)], refs[-8 - sum(PIECES) :]
    weights, mixed_ref, out_refs = refs[:2], refs[2], list(refs[3 : 3 + sum(PIECES)])
    query_ref, own_ref, other_ref, held, arrived = refs[3 + sum(PIECES) :]
    fetch(weights, held, arrived, 0)
    core = core_ref[0]
    parts = len(ins) // 3
    for kind, whole in enumerate((query_ref, own_ref, other_ref)):
        at = 0
        for part in ins[kind * parts : (kind + 1) * parts]:
            for top in range(0, part.shape[0], ROWS):
                place = pl.ds(pl.multiple_of(place_ref[order[at]] * ROWS, ROWS), ROWS)
                whole[place, :] = part[top : top + ROWS]
                at += 1
    count, qcols = query_ref.shape
    heads = qcols // HEAD
    block = 2 * ROWS
    scale = 1.0 / math.sqrt(HEAD)
    shift = ROWS.bit_length() - 1
    for step in range(count // block):
        rows = slice(step * block, (step + 1) * block)
        span = (step + 1) * block
        query = jnp.concatenate(
            [query_ref[rows, h * HEAD : (h + 1) * HEAD] for h in range(heads)], axis=0
        )
        contract = (((1,), (1,)), ((), ()))
        row = lax.broadcasted_iota(jnp.int32, (block, block), 0)
        col = lax.broadcasted_iota(jnp.int32, (block, block), 1)
        own_seen = jnp.concatenate([col <= row] * heads, axis=0)
        other_seen = jnp.concatenate(
            [jnp.right_shift(col, shift) < jnp.right_shift(row, shift) + core] * heads, axis=0
        )

        def scores_of(ref, seen):
            raw = lax.dot_general(
                query, ref[:span, :HEAD], contract, preferred_element_type=jnp.float32
            )
            tail = jnp.where(seen, raw[:, span - block :], -jnp.inf)
            if span == block:
                return tail
            return jnp.concatenate([raw[:, : span - block], tail], axis=1)

        scores = jnp.concatenate(
            [scores_of(own_ref, own_seen), scores_of(other_ref, other_seen)], axis=1
        )
        peak = jnp.max(scores, axis=-1, keepdims=True)
        probs = jnp.exp((scores - peak) * scale).astype(jnp.bfloat16)
        ones = jnp.ones((span, HEAD), jnp.bfloat16)
        total = jnp.zeros((block * heads, 2 * HEAD), jnp.float32)
        for part, ref in enumerate((own_ref, other_ref)):
            values = jnp.concatenate([ref[:span, HEAD:], ones], axis=1)
            total += jnp.dot(
                probs[:, part * span : (part + 1) * span],
                values,
                preferred_element_type=jnp.float32,
            )
        mixed = (total[:, :HEAD] / total[:, HEAD:]).astype(jnp.bfloat16)
        for part in range(block // ROWS):
            slot = place_ref[8 + step * (block // ROWS) + part]
            place = pl.ds(pl.multiple_of(slot * ROWS, ROWS), ROWS)
            for h in range(heads):
                top = h * block + part * ROWS
                mixed_ref[place, h * HEAD : (h + 1) * HEAD] = mixed[top : top + ROWS]

    outs = [[out_refs.pop(0) for _ in range(piece)] for piece in PIECES]
    multiply(lambda: mixed_ref[count // 2 :], weights, held, arrived, 0, outs)


def attend(core, places, order, queries, own, other, weights):
    count, qcols = sum(q.shape[0] for q in queries), queries[0].shape[1]
    kcols = own[0].shape[1]
    args = [*queries, *own, *other]
    vmem = pl.BlockSpec(memory_space=pltpu.VMEM)
    depth, width = weights[0].shape
    return pl.pallas_call(
        functools.partial(attend_body, order),
        in_specs=[pl.BlockSpec(memory_space=pltpu.SMEM)] * 2
        + [vmem] * len(args)
        + [pl.BlockSpec(memory_space=pl.ANY)] * 2,
        out_specs=[vmem] * (1 + sum(PIECES)),
        out_shape=[jax.ShapeDtypeStruct((count, qcols), jnp.bfloat16)]
        + [
            jax.ShapeDtypeStruct((ROWS, width // piece), jnp.bfloat16)
            for piece in PIECES
            for _ in range(piece)
        ],
        scratch_shapes=[pltpu.VMEM((count, cols), jnp.bfloat16) for cols in (qcols, kcols, kcols)]
        + [
            pltpu.VMEM((2 * depth, width), jnp.bfloat16),
            pltpu.SemaphoreType.DMA((width // TILE, 2)),
        ],
        compiler_params=params(56),
        cost_estimate=cost(8 * count * count * qcols, 4 * count * qcols + 4 * depth * width),
        name="attend",
    )(core, places, *args, *weights)


def output_body(mixed_ref, *refs):
    weights, out_refs, (held, arrived) = refs[:2], list(refs[2:-2]), refs[-2:]
    fetch(weights, held, arrived, 0)
    count = mixed_ref.shape[0] // 2
    outs = [[out_refs.pop(0) for _ in range(piece)] for piece in PIECES]
    multiply(lambda: mixed_ref[:count], weights, held, arrived, 0, outs)


def output(mixed, weights):
    depth, width = weights[0].shape
    count = mixed.shape[0] // 2
    vmem = pl.BlockSpec(memory_space=pltpu.VMEM)
    widths = [width // piece for piece in PIECES for _ in range(piece)]
    return list(
        pl.pallas_call(
            output_body,
            in_specs=[vmem] + [pl.BlockSpec(memory_space=pl.ANY)] * 2,
            out_specs=[vmem] * len(widths),
            out_shape=[jax.ShapeDtypeStruct((ROWS, w), jnp.bfloat16) for w in widths],
            scratch_shapes=[
                pltpu.VMEM((2 * depth, width), jnp.bfloat16),
                pltpu.SemaphoreType.DMA((width // TILE, 2)),
            ],
            compiler_params=params(56),
            cost_estimate=cost(
                4 * count * depth * width, 2 * (2 * depth * width + count * width)
            ),
            name="output",
        )(mixed, *weights)
    )


def mark_body(*refs):
    del refs


def mark(*blocks):
    anywhere = [pl.BlockSpec(memory_space=pl.ANY)] * len(blocks)
    return pl.pallas_call(
        mark_body,
        in_specs=anywhere,
        out_specs=anywhere,
        out_shape=[jax.ShapeDtypeStruct(block.shape, block.dtype) for block in blocks],
        input_output_aliases={at: at for at in range(len(blocks))},
        compiler_params=params(),
        cost_estimate=cost(7e10, 4096),
        name="mark",
    )(*blocks)


def pick_body(below_ref, above_ref, first_ref, second_ref):
    count = first_ref.shape[0]
    first_ref[...] = below_ref[:count]
    second_ref[...] = above_ref[count:]


def pick(below, above):
    shape = jax.ShapeDtypeStruct((below.shape[0] // HALVES, below.shape[1]), below.dtype)
    return pl.pallas_call(
        pick_body,
        out_shape=[shape, shape],
        compiler_params=params(),
        cost_estimate=cost(1e8, 4 * below.size),
        name="pick",
    )(below, above)


def sums_body(shapes, *refs):
    outs = refs[-len(shapes) :]
    first = 0
    for out_ref, (offset, starts) in zip(outs, shapes):
        step = min(ref.shape[1] for ref in (out_ref, *refs[first : first + len(starts)]))
        for left in range(0, out_ref.shape[1], step):
            total = None
            for at, start in enumerate(starts):
                ref = refs[first + at]
                col = offset + left - start
                if 0 <= col < ref.shape[1]:
                    term = ref[:, col : col + step].astype(jnp.float32)
                    total = term if total is None else total + term
            out_ref[:, left : left + step] = total.astype(jnp.bfloat16)
        first += len(starts)


def sums(*groups, name="sums", after=()):
    args = [array for _, terms in groups for array, _ in terms]
    shapes = tuple((first, tuple(start for _, start in terms)) for (first, _), terms in groups)
    result = pl.pallas_call(
        functools.partial(sums_body, shapes),
        in_specs=[pl.BlockSpec(memory_space=pltpu.VMEM)] * len(args)
        + [pl.BlockSpec(memory_space=pl.ANY)] * len(after),
        out_shape=[
            jax.ShapeDtypeStruct((terms[0][0].shape[0], width), jnp.bfloat16)
            for (_, width), terms in groups
        ],
        compiler_params=params(16),
        cost_estimate=cost(sum(a.size for a in args), 3 * sum(a.size for a in args)),
        name=name,
    )(*args, *after)
    return result if len(groups) > 1 else result[0]


def terms_body(block_ref, codes_ref, exps_ref, *out_refs):
    scale = jnp.exp2(exps_ref[...].astype(jnp.float32))
    lane = lax.broadcasted_iota(jnp.int32, scale.shape, 1)
    count = codes_ref.shape[0]
    for at, out_ref in enumerate(out_refs):
        for side in range(2):
            block = block_ref[2 * at + side]
            cols = pl.ds(pl.multiple_of(block * HEAD, HEAD), HEAD)
            mine = jnp.sum(jnp.where(lane == block, scale, 0.0), axis=1, keepdims=True)
            out_ref[side * count : (side + 1) * count] = (
                codes_ref[:, cols].astype(jnp.float32) * mine
            ).astype(jnp.bfloat16)


def terms(blocks, codes, exps):
    count, width = codes.shape
    vmem = pl.BlockSpec(memory_space=pltpu.VMEM)
    return pl.pallas_call(
        terms_body,
        in_specs=[pl.BlockSpec(memory_space=pltpu.SMEM), vmem, vmem],
        out_shape=[jax.ShapeDtypeStruct((2 * count, HEAD), jnp.bfloat16)] * len(RING),
        compiler_params=params(),
        cost_estimate=cost(codes.size, 4 * codes.size),
        name="terms",
    )(blocks, codes, exps)


def outer_body(replicas, *refs):
    mine_refs, theirs_ref, momentum_ref, table_ref, momentum_out, rebuilt_ref = (
        refs[:3],
        *refs[3:],
    )
    table = table_ref[...]

    def rotate(values):
        return jnp.dot(
            values, table, precision=lax.Precision.HIGHEST, preferred_element_type=jnp.float32
        )

    summed = theirs_ref[...].astype(jnp.float32)
    for ref in mine_refs:
        summed += ref[: summed.shape[0]].astype(jnp.float32)
    averaged = rotate(summed / replicas)
    fresh = 0.9 * momentum_ref[...] + averaged
    momentum_out[...] = fresh
    turned = rotate(0.7 * (averaged + 0.9 * fresh))
    scales = (jnp.max(jnp.abs(turned), axis=-1, keepdims=True) + 1e-06).astype(jnp.bfloat16)
    scales = scales.astype(jnp.float32)
    codes = (turned / scales).astype(jnp.bfloat16)
    rebuilt_ref[...] = rotate(codes.astype(jnp.float32) * scales).astype(jnp.bfloat16)


def outer(mine, theirs, momentum, table, replicas):
    return pl.pallas_call(
        functools.partial(outer_body, replicas),
        out_shape=[
            jax.ShapeDtypeStruct(momentum.shape, jnp.float32),
            jax.ShapeDtypeStruct(momentum.shape, jnp.bfloat16),
        ],
        compiler_params=params(),
        cost_estimate=cost(40 * theirs.size * HEAD, 12 * theirs.size),
        name="outer",
    )(*mine, theirs, momentum, table)


def apply_body(block_ref, params_ref, *refs):
    rebuilt_refs, out_ref = refs[:-1], refs[-1]
    count = out_ref.shape[0]
    for at, rebuilt_ref in enumerate(rebuilt_refs):
        for side in range(2):
            cols = pl.ds(pl.multiple_of(block_ref[2 * at + side] * HEAD, HEAD), HEAD)
            rebuilt = rebuilt_ref[side * count : (side + 1) * count].astype(jnp.float32)
            out_ref[:, cols] = (params_ref[:, cols].astype(jnp.float32) - rebuilt).astype(
                jnp.bfloat16
            )


def apply(blocks, old, rebuilt):
    vmem = pl.BlockSpec(memory_space=pltpu.VMEM)
    return pl.pallas_call(
        apply_body,
        in_specs=[pl.BlockSpec(memory_space=pltpu.SMEM)] + [vmem] * (1 + len(rebuilt)),
        out_shape=jax.ShapeDtypeStruct(old.shape, jnp.bfloat16),
        compiler_params=params(),
        cost_estimate=cost(old.size, 6 * old.size),
        name="apply",
    )(blocks, old, *rebuilt)


def swap(block, axis):
    return lax.ppermute(block, axis, [(0, 1), (1, 0)])


def hop(block, axis, way):
    at = (0, 2, 1, 3) if axis == Y else (0, 1, 2, 3)
    return lax.ppermute(block, axis, [(at[i], at[(i + way) % 4]) for i in range(4)])


def add(*blocks):
    total = blocks[0].astype(jnp.float32)
    for block in blocks[1:]:
        total = total + block.astype(jnp.float32)
    return total.astype(jnp.bfloat16)


def wait(*blocks):
    return lax.optimization_barrier(blocks)


def tie(block, *others):
    return lax.optimization_barrier((block, *others))[0]


def local(
    tokens, norm_gain, query_weight, kv_weight, out_weight, pseudo_grad, grad_exps, old, momentum
):
    core, z, yhi = lax.axis_index("core"), lax.axis_index("z"), lax.axis_index("yhi")
    x, ylo = lax.axis_index("x"), lax.axis_index("ylo")
    replicas = lax.axis_size(REPLICA)
    place = jnp.stack([(yhi ^ side) * 4 + (z + r) % 4 for side in range(2) for r in RING])
    chip = jnp.arange(8, dtype=jnp.int32)
    away = (chip % 4 - z) % 4
    slots = ((chip // 4) ^ yhi) * 4 + jnp.where(away < 2, away, 5 - away)
    share = jnp.stack([((x + r) % 4) * 2 + (ylo ^ side) for r in RING for side in range(2)])
    core, place, slots, share = (
        v.astype(jnp.int32).reshape(-1) for v in (core, place, slots, share)
    )
    places = jnp.concatenate([place, slots])

    block, h1, h2 = normalize(tokens, norm_gain)
    relay1, relay2 = hop(h1, Y, 1), hop(h2, Y, -1)
    below, above = hop(block, "z", 1), hop(block, "z", -1)
    kv_theirs = swap(tie(kv_weight, block), "core")
    at0, at1, at3, at2 = terms(share, tie(pseudo_grad[0], block), grad_exps[0])
    relay1, relay2, kv_theirs, at0, at1, at2, at3, query_weight = wait(
        relay1, relay2, kv_theirs, at0, at1, at2, at3, query_weight
    )
    query_theirs = swap(query_weight, "core")
    partner = jnp.concatenate([hop(relay1, Y, 1), hop(relay2, Y, -1)], axis=0)
    below, above = mark(below, above)
    far1, far2 = pick(below, above)
    partner, above, below = wait(partner, above, below)
    far1, far2 = hop(far1, "z", 1), hop(far2, "z", -1)
    pbelow, pabove = hop(partner, "z", 1), hop(partner, "z", -1)
    weights = [query_weight, query_theirs, kv_weight, kv_theirs]
    query_a, pair_a = project(core, [block, above, below, far1, far2], weights)
    query_a, far1, far2, at2, at3 = wait(query_a, far1, far2, at2, at3)
    x2, x3 = hop(at2, "x", 1), hop(at3, "x", -1)
    pabove, pbelow, query_a, pair_a, x2, x3, at1, out_weight = wait(
        pabove, pbelow, query_a, pair_a, x2, x3, at1, out_weight
    )
    pfar1, pfar2 = pick(pbelow, pabove)
    pfar1, pfar2 = hop(pfar1, "z", 1), hop(pfar2, "z", -1)
    out_theirs = swap(out_weight, "core")
    query_m, pair_m = project(core, [partner, pabove, pbelow], weights)
    passed = hop(add(at1, x2), "x", 1)
    other_a, other_m = swap(pair_a, "core"), swap(pair_m, "core")
    pfar1, pfar2, passed, query_m = wait(pfar1, pfar2, passed, query_m)
    query_l, pair_l = project(core, [pfar1, pfar2], weights)
    other_l = swap(pair_l, "core")
    out_weights = (out_weight, out_theirs)
    mixed, q0, qup, qdown, far_a, far_b = attend(
        core,
        places,
        tuple(range(8)),
        (query_a, query_m, query_l),
        (pair_a, pair_m, pair_l),
        (other_a, other_m, other_l),
        out_weights,
    )

    full = out_weight.shape[1]
    half = full // HALVES
    mixed, far_a, far_b = wait(mixed, far_a, far_b)
    far_a, far_b = hop(far_a, "z", 1), hop(far_b, "z", -1)
    mine = (at0, passed, x3)
    count = momentum.shape[0]
    sent, q0, mixed = wait(add(*(part[count:] for part in mine)), q0, mixed)
    theirs = swap(sent, "ylo")
    o0, oup, odown, ofara, ofarb = output(mixed, out_weights)
    far_a, far_b, o0 = wait(far_a, far_b, o0)
    up, down = sums(
        ((0, full), ((qup, 0), (far_a, 0))), ((0, full), ((qdown, 0), (far_b, half)))
    )
    up, down, theirs, ofara, ofarb = wait(up, down, theirs, ofara, ofarb)
    up, down = hop(up, "z", 1), hop(down, "z", -1)
    ofara, ofarb = hop(ofara, "z", 1), hop(ofarb, "z", -1)
    new_momentum, rebuilt = outer(mine, theirs, momentum, hadamard_table(HEAD), replicas)
    beside = swap(rebuilt, "ylo")
    both = jnp.concatenate([rebuilt, beside], axis=0)
    before = hop(both, "x", 1)
    up, down, before, both = wait(up, down, before, both)
    s1, s2 = sums(
        *(((at, half), ((q0, 0), (up, 0), (down, 0))) for at in (0, half))
    )
    oup, odown = sums(
        ((0, full), ((oup, 0), (ofara, 0))),
        ((0, full), ((odown, 0), (ofarb, half))),
        after=(s1,),
    )
    oup, odown = hop(oup, "z", 1), hop(odown, "z", -1)
    s1, s2 = hop(s1, Y, 1), hop(s2, Y, -1)
    after = hop(both, "x", -1)
    s1, s2, before = wait(s1, s2, before)
    s1, s2 = hop(s1, Y, 1), hop(s2, Y, -1)
    ahead = hop(before, "x", 1)
    new_params = apply(share, old, [both, after, before, ahead])
    o0, new_params = wait(o0, new_params)
    attended = sums(
        ((0, full), ((o0, 0), (oup, 0), (odown, 0), (s1, 0), (s2, half))), name="finish"
    )
    return (attended, new_params, new_momentum)


def solution(mesh):
    fine = Mesh(mesh.devices.reshape(4, 2, 2, 4, 2), ("x", "ylo", "yhi", "z", "core"))
    every = REPLICA + TENSOR
    return jax.shard_map(
        local,
        mesh=fine,
        in_specs=(
            P(every, None),
            P(),
            P(None, TENSOR),
            P(None, TENSOR),
            P(TENSOR, None),
            P(REPLICA, TENSOR, None),
            P(REPLICA, TENSOR, None),
            P(TENSOR, None),
            P(TENSOR, REPLICA),
        ),
        out_specs=(P(every, None), P(TENSOR, None), P(TENSOR, REPLICA)),
        check_vma=False,
    )
```

```python
import functools
import math

import jax
import jax.numpy as jnp
from jax import lax
from jax.experimental import pallas as pl
from jax.experimental.pallas import tpu as pltpu
from jax.sharding import Mesh
from jax.sharding import PartitionSpec as P

HEAD = 128
REPLICA = ("x", "ylo")
TENSOR = ("yhi", "z", "core")
ROWS = 64
RING = (0, 1, -1, 2)
Y = ("ylo", "yhi")
HALVES = 2
TILE = 1024
PIECES = (1, 1, 1, HALVES)
MIB = 1024 * 1024


def params(mib=8):
    return pltpu.CompilerParams(vmem_limit_bytes=mib * MIB)


def cost(flops, moved):
    return pl.CostEstimate(flops=int(flops), bytes_accessed=int(moved), transcendentals=0)


def hadamard_table(width):
    index = jnp.arange(width, dtype=jnp.int32)
    common = jnp.bitwise_and(index[:, None], index[None, :])
    parity = jnp.zeros((width, width), jnp.int32)
    for bit in range(int(math.log2(width))):
        parity = parity + jnp.bitwise_and(jnp.right_shift(common, bit), 1)
    sign = 1.0 - 2.0 * jnp.bitwise_and(parity, 1).astype(jnp.float32)
    return sign / math.sqrt(width)


def norm_body(rows_ref, gain_ref, whole_ref, *half_refs):
    values = rows_ref[...].astype(jnp.float32)
    power = jnp.mean(values * values, axis=-1, keepdims=True)
    normed = (values * lax.rsqrt(power + 1e-05) * gain_ref[...]).astype(jnp.bfloat16)
    whole_ref[...] = normed
    count = normed.shape[0] // HALVES
    for at, half_ref in enumerate(half_refs):
        half_ref[...] = normed[at * count : (at + 1) * count]


def normalize(rows, gain):
    count, width = rows.shape
    return pl.pallas_call(
        norm_body,
        out_shape=[
            jax.ShapeDtypeStruct((c, width), jnp.bfloat16)
            for c in [count] + [count // HALVES] * HALVES
        ],
        compiler_params=params(56),
        cost_estimate=cost(4 * rows.size, 6 * rows.size),
        name="normalize",
    )(rows, gain.reshape(1, width))


def project_body(core_ref, *refs):
    blocks, refs = refs[:-12], refs[-12:]
    weights, (query_out, pair_out, total), held, arrived = refs[:4], refs[4:7], refs[7:11], refs[11]
    half = weights[0].shape[1]
    depth = weights[0].shape[0]
    chunks = arrived.shape[1]
    chunk = depth // chunks

    def copies_of(at):
        span = pl.ds(pl.multiple_of(at * chunk, chunk), chunk)
        return [
            pltpu.make_async_copy(weight.at[span, :], place.at[span, :], arrived.at[kind, at])
            for kind, (weight, place) in enumerate(zip(weights, held))
        ]

    for at in range(chunks):
        for copy in copies_of(at):
            copy.start()
    total[...] = jnp.zeros_like(total)
    qa_ref, qb_ref, ka_ref, kb_ref = held

    def step(at, carry):
        for copy in copies_of(at):
            copy.wait()
        span = pl.ds(pl.multiple_of(at * chunk, chunk), chunk)
        rows = jnp.concatenate([ref[:, span] for ref in blocks], axis=0)
        both = jnp.concatenate([ka_ref[span, :], kb_ref[span, :]], axis=1)
        for start, weight in ((0, qa_ref[span, :]), (half, qb_ref[span, :]), (2 * half, both)):
            total[:, start : start + weight.shape[1]] += jnp.dot(
                rows, weight, preferred_element_type=jnp.float32
            )
        return carry

    lax.fori_loop(0, chunks, step, 0)
    flip = core_ref[0] == 0
    value = total[...].astype(jnp.bfloat16)
    query_out[...] = value[:, : 2 * half]
    left, right = value[:, 2 * half : 2 * half + HEAD], value[:, 2 * half + HEAD :]
    pair_out[:, :HEAD] = jnp.where(flip, left, right)
    pair_out[:, HEAD:] = jnp.where(flip, right, left)


def project(core, blocks, weights):
    width = blocks[0].shape[1]
    count = sum(block.shape[0] for block in blocks)
    qcols = 2 * weights[0].shape[1]
    kcols = 2 * weights[2].shape[1]
    vmem = pl.BlockSpec(memory_space=pltpu.VMEM)
    return pl.pallas_call(
        project_body,
        in_specs=[pl.BlockSpec(memory_space=pltpu.SMEM)]
        + [vmem] * len(blocks)
        + [pl.BlockSpec(memory_space=pl.ANY)] * len(weights),
        out_specs=[vmem, vmem],
        out_shape=[
            jax.ShapeDtypeStruct((count, qcols), jnp.bfloat16),
            jax.ShapeDtypeStruct((count, kcols), jnp.bfloat16),
        ],
        scratch_shapes=[pltpu.VMEM((count, qcols + kcols), jnp.float32)]
        + [pltpu.VMEM(weight.shape, jnp.bfloat16) for weight in weights]
        + [pltpu.SemaphoreType.DMA((len(weights), width // TILE))],
        compiler_params=params(56),
        cost_estimate=cost(
            3 * count * width * (qcols + kcols), 2 * width * (count + qcols + kcols)
        ),
        name="project",
    )(core, *blocks, *weights)


def copies_of(weights, held, arrived, first, at):
    half = weights[0].shape[0]
    span = pl.ds(pl.multiple_of(at * TILE, TILE), TILE)
    return [
        pltpu.make_async_copy(
            weight.at[:, pl.ds(pl.multiple_of(first + at * TILE, TILE), TILE)],
            held.at[pl.ds(kind * half, half), span],
            arrived.at[at, kind],
        )
        for kind, weight in enumerate(weights)
    ]


def fetch(weights, held, arrived, first):
    for at in range(held.shape[1] // TILE):
        for copy in copies_of(weights, held, arrived, first, at):
            copy.start()


def multiply(rows_of, weights, held, arrived, first, out_refs):
    tiles = held.shape[1] // TILE
    parts = max(len(pieces) for pieces in out_refs)
    for part in range(parts):

        def step(at, carry, part=part):
            for copy in copies_of(weights, held, arrived, first, at):
                copy.wait()
            span = pl.ds(pl.multiple_of(at * TILE, TILE), TILE)
            result = jnp.dot(rows_of(), held[:, span], preferred_element_type=jnp.float32)
            result = result.astype(jnp.bfloat16)
            for block, pieces in enumerate(out_refs):
                back = part * (tiles // parts) if len(pieces) == parts else 0
                there = pl.ds(pl.multiple_of((at - back) * TILE, TILE), TILE)
                pieces[part if len(pieces) == parts else 0][:, there] = result[
                    block * ROWS : (block + 1) * ROWS
                ]
            return carry

        lax.fori_loop(part * (tiles // parts), (part + 1) * (tiles // parts), step, 0)


def attend_body(order, core_ref, place_ref, *refs):
    ins, refs = refs[: -8 - sum(PIECES)], refs[-8 - sum(PIECES) :]
    weights, mixed_ref, out_refs = refs[:2], refs[2], list(refs[3 : 3 + sum(PIECES)])
    query_ref, own_ref, other_ref, held, arrived = refs[3 + sum(PIECES) :]
    fetch(weights, held, arrived, 0)
    core = core_ref[0]
    parts = len(ins) // 3
    for kind, whole in enumerate((query_ref, own_ref, other_ref)):
        at = 0
        for part in ins[kind * parts : (kind + 1) * parts]:
            for top in range(0, part.shape[0], ROWS):
                place = pl.ds(pl.multiple_of(place_ref[order[at]] * ROWS, ROWS), ROWS)
                whole[place, :] = part[top : top + ROWS]
                at += 1
    count, qcols = query_ref.shape
    heads = qcols // HEAD
    block = 2 * ROWS
    scale = 1.0 / math.sqrt(HEAD)
    shift = ROWS.bit_length() - 1
    for step in range(count // block):
        rows = slice(step * block, (step + 1) * block)
        span = (step + 1) * block
        query = jnp.concatenate(
            [query_ref[rows, h * HEAD : (h + 1) * HEAD] for h in range(heads)], axis=0
        )
        contract = (((1,), (1,)), ((), ()))
        row = lax.broadcasted_iota(jnp.int32, (block, block), 0)
        col = lax.broadcasted_iota(jnp.int32, (block, block), 1)
        own_seen = jnp.concatenate([col <= row] * heads, axis=0)
        other_seen = jnp.concatenate(
            [jnp.right_shift(col, shift) < jnp.right_shift(row, shift) + core] * heads, axis=0
        )

        def scores_of(ref, seen):
            raw = lax.dot_general(
                query, ref[:span, :HEAD], contract, preferred_element_type=jnp.float32
            )
            tail = jnp.where(seen, raw[:, span - block :], -jnp.inf)
            if span == block:
                return tail
            return jnp.concatenate([raw[:, : span - block], tail], axis=1)

        scores = jnp.concatenate(
            [scores_of(own_ref, own_seen), scores_of(other_ref, other_seen)], axis=1
        )
        peak = jnp.max(scores, axis=-1, keepdims=True)
        probs = jnp.exp((scores - peak) * scale).astype(jnp.bfloat16)
        ones = jnp.ones((span, HEAD), jnp.bfloat16)
        total = jnp.zeros((block * heads, 2 * HEAD), jnp.float32)
        for part, ref in enumerate((own_ref, other_ref)):
            values = jnp.concatenate([ref[:span, HEAD:], ones], axis=1)
            total += jnp.dot(
                probs[:, part * span : (part + 1) * span],
                values,
                preferred_element_type=jnp.float32,
            )
        mixed = (total[:, :HEAD] / total[:, HEAD:]).astype(jnp.bfloat16)
        for part in range(block // ROWS):
            slot = place_ref[8 + step * (block // ROWS) + part]
            place = pl.ds(pl.multiple_of(slot * ROWS, ROWS), ROWS)
            for h in range(heads):
                top = h * block + part * ROWS
                mixed_ref[place, h * HEAD : (h + 1) * HEAD] = mixed[top : top + ROWS]

    outs = [[out_refs.pop(0) for _ in range(piece)] for piece in PIECES]
    multiply(lambda: mixed_ref[count // 2 :], weights, held, arrived, 0, outs)


def attend(core, places, order, queries, own, other, weights):
    count, qcols = sum(q.shape[0] for q in queries), queries[0].shape[1]
    kcols = own[0].shape[1]
    args = [*queries, *own, *other]
    vmem = pl.BlockSpec(memory_space=pltpu.VMEM)
    depth, width = weights[0].shape
    return pl.pallas_call(
        functools.partial(attend_body, order),
        in_specs=[pl.BlockSpec(memory_space=pltpu.SMEM)] * 2
        + [vmem] * len(args)
        + [pl.BlockSpec(memory_space=pl.ANY)] * 2,
        out_specs=[vmem] * (1 + sum(PIECES)),
        out_shape=[jax.ShapeDtypeStruct((count, qcols), jnp.bfloat16)]
        + [
            jax.ShapeDtypeStruct((ROWS, width // piece), jnp.bfloat16)
            for piece in PIECES
            for _ in range(piece)
        ],
        scratch_shapes=[pltpu.VMEM((count, cols), jnp.bfloat16) for cols in (qcols, kcols, kcols)]
        + [
            pltpu.VMEM((2 * depth, width), jnp.bfloat16),
            pltpu.SemaphoreType.DMA((width // TILE, 2)),
        ],
        compiler_params=params(56),
        cost_estimate=cost(8 * count * count * qcols, 4 * count * qcols + 4 * depth * width),
        name="attend",
    )(core, places, *args, *weights)


def output_body(mixed_ref, *refs):
    weights, out_refs, (held, arrived) = refs[:2], list(refs[2:-2]), refs[-2:]
    fetch(weights, held, arrived, 0)
    count = mixed_ref.shape[0] // 2
    outs = [[out_refs.pop(0) for _ in range(piece)] for piece in PIECES]
    multiply(lambda: mixed_ref[:count], weights, held, arrived, 0, outs)


def output(mixed, weights):
    depth, width = weights[0].shape
    count = mixed.shape[0] // 2
    vmem = pl.BlockSpec(memory_space=pltpu.VMEM)
    widths = [width // piece for piece in PIECES for _ in range(piece)]
    return list(
        pl.pallas_call(
            output_body,
            in_specs=[vmem] + [pl.BlockSpec(memory_space=pl.ANY)] * 2,
            out_specs=[vmem] * len(widths),
            out_shape=[jax.ShapeDtypeStruct((ROWS, w), jnp.bfloat16) for w in widths],
            scratch_shapes=[
                pltpu.VMEM((2 * depth, width), jnp.bfloat16),
                pltpu.SemaphoreType.DMA((width // TILE, 2)),
            ],
            compiler_params=params(56),
            cost_estimate=cost(
                4 * count * depth * width, 2 * (2 * depth * width + count * width)
            ),
            name="output",
        )(mixed, *weights)
    )


def mark_body(*refs):
    del refs


def mark(*blocks):
    anywhere = [pl.BlockSpec(memory_space=pl.ANY)] * len(blocks)
    return pl.pallas_call(
        mark_body,
        in_specs=anywhere,
        out_specs=anywhere,
        out_shape=[jax.ShapeDtypeStruct(block.shape, block.dtype) for block in blocks],
        input_output_aliases={at: at for at in range(len(blocks))},
        compiler_params=params(),
        cost_estimate=cost(7e10, 4096),
        name="mark",
    )(*blocks)


def pick_body(below_ref, above_ref, first_ref, second_ref):
    first_ref[...] = below_ref[...]
    second_ref[...] = above_ref[...]


def pick(below, above):
    shape = jax.ShapeDtypeStruct((below.shape[0] // HALVES, below.shape[1]), below.dtype)
    return pl.pallas_call(
        pick_body,
        grid=(1,),
        in_specs=[pl.BlockSpec(shape.shape, lambda i, at=at: (at, 0)) for at in range(HALVES)],
        out_specs=[pl.BlockSpec(shape.shape, lambda i: (0, 0))] * HALVES,
        out_shape=[shape, shape],
        compiler_params=params(),
        cost_estimate=cost(1e8, 4 * below.size),
        name="pick",
    )(below, above)


def sums_body(shapes, *refs):
    outs = refs[-len(shapes) :]
    first = 0
    for out_ref, (offset, starts) in zip(outs, shapes):
        step = min(ref.shape[1] for ref in (out_ref, *refs[first : first + len(starts)]))
        for left in range(0, out_ref.shape[1], step):
            total = None
            for at, start in enumerate(starts):
                ref = refs[first + at]
                col = offset + left - start
                if 0 <= col < ref.shape[1]:
                    term = ref[:, col : col + step].astype(jnp.float32)
                    total = term if total is None else total + term
            out_ref[:, left : left + step] = total.astype(jnp.bfloat16)
        first += len(starts)


def sums(*groups, name="sums", after=()):
    args = [array for _, terms in groups for array, _ in terms]
    shapes = tuple((first, tuple(start for _, start in terms)) for (first, _), terms in groups)
    result = pl.pallas_call(
        functools.partial(sums_body, shapes),
        in_specs=[pl.BlockSpec(memory_space=pltpu.VMEM)] * len(args)
        + [pl.BlockSpec(memory_space=pl.ANY)] * len(after),
        out_shape=[
            jax.ShapeDtypeStruct((terms[0][0].shape[0], width), jnp.bfloat16)
            for (_, width), terms in groups
        ],
        compiler_params=params(16),
        cost_estimate=cost(sum(a.size for a in args), 3 * sum(a.size for a in args)),
        name=name,
    )(*args, *after)
    return result if len(groups) > 1 else result[0]


def terms_body(block_ref, codes_ref, exps_ref, *out_refs):
    scale = jnp.exp2(exps_ref[...].astype(jnp.float32))
    lane = lax.broadcasted_iota(jnp.int32, scale.shape, 1)
    count = codes_ref.shape[0]
    for at, out_ref in enumerate(out_refs):
        for side in range(2):
            block = block_ref[2 * at + side]
            cols = pl.ds(pl.multiple_of(block * HEAD, HEAD), HEAD)
            mine = jnp.sum(jnp.where(lane == block, scale, 0.0), axis=1, keepdims=True)
            out_ref[side * count : (side + 1) * count] = (
                codes_ref[:, cols].astype(jnp.float32) * mine
            ).astype(jnp.bfloat16)


def terms(blocks, codes, exps):
    count, width = codes.shape
    vmem = pl.BlockSpec(memory_space=pltpu.VMEM)
    return pl.pallas_call(
        terms_body,
        in_specs=[pl.BlockSpec(memory_space=pltpu.SMEM), vmem, vmem],
        out_shape=[jax.ShapeDtypeStruct((2 * count, HEAD), jnp.bfloat16)] * len(RING),
        compiler_params=params(),
        cost_estimate=cost(codes.size, 4 * codes.size),
        name="terms",
    )(blocks, codes, exps)


def outer_body(replicas, *refs):
    mine_refs, theirs_ref, momentum_ref, table_ref, momentum_out, rebuilt_ref = (
        refs[:3],
        *refs[3:],
    )
    table = table_ref[...]

    def rotate(values):
        return jnp.dot(
            values, table, precision=lax.Precision.HIGHEST, preferred_element_type=jnp.float32
        )

    summed = theirs_ref[...].astype(jnp.float32)
    for ref in mine_refs:
        summed += ref[: summed.shape[0]].astype(jnp.float32)
    averaged = rotate(summed / replicas)
    fresh = 0.9 * momentum_ref[...] + averaged
    momentum_out[...] = fresh
    turned = rotate(0.7 * (averaged + 0.9 * fresh))
    scales = (jnp.max(jnp.abs(turned), axis=-1, keepdims=True) + 1e-06).astype(jnp.bfloat16)
    scales = scales.astype(jnp.float32)
    codes = (turned / scales).astype(jnp.bfloat16)
    rebuilt_ref[...] = rotate(codes.astype(jnp.float32) * scales).astype(jnp.bfloat16)


def outer(mine, theirs, momentum, table, replicas):
    return pl.pallas_call(
        functools.partial(outer_body, replicas),
        out_shape=[
            jax.ShapeDtypeStruct(momentum.shape, jnp.float32),
            jax.ShapeDtypeStruct(momentum.shape, jnp.bfloat16),
        ],
        compiler_params=params(),
        cost_estimate=cost(40 * theirs.size * HEAD, 12 * theirs.size),
        name="outer",
    )(*mine, theirs, momentum, table)


def apply_body(block_ref, params_ref, *refs):
    rebuilt_refs, out_ref = refs[:-1], refs[-1]
    count = out_ref.shape[0]
    for at, rebuilt_ref in enumerate(rebuilt_refs):
        for side in range(2):
            cols = pl.ds(pl.multiple_of(block_ref[2 * at + side] * HEAD, HEAD), HEAD)
            rebuilt = rebuilt_ref[side * count : (side + 1) * count].astype(jnp.float32)
            out_ref[:, cols] = (params_ref[:, cols].astype(jnp.float32) - rebuilt).astype(
                jnp.bfloat16
            )


def apply(blocks, old, rebuilt):
    vmem = pl.BlockSpec(memory_space=pltpu.VMEM)
    return pl.pallas_call(
        apply_body,
        in_specs=[pl.BlockSpec(memory_space=pltpu.SMEM)] + [vmem] * (1 + len(rebuilt)),
        out_shape=jax.ShapeDtypeStruct(old.shape, jnp.bfloat16),
        compiler_params=params(),
        cost_estimate=cost(old.size, 6 * old.size),
        name="apply",
    )(blocks, old, *rebuilt)


def swap(block, axis):
    return lax.ppermute(block, axis, [(0, 1), (1, 0)])


def hop(block, axis, way):
    at = (0, 2, 1, 3) if axis == Y else (0, 1, 2, 3)
    return lax.ppermute(block, axis, [(at[i], at[(i + way) % 4]) for i in range(4)])


def add(*blocks):
    total = blocks[0].astype(jnp.float32)
    for block in blocks[1:]:
        total = total + block.astype(jnp.float32)
    return total.astype(jnp.bfloat16)


def wait(*blocks):
    return lax.optimization_barrier(blocks)


def tie(block, *others):
    return lax.optimization_barrier((block, *others))[0]


def local(
    tokens, norm_gain, query_weight, kv_weight, out_weight, pseudo_grad, grad_exps, old, momentum
):
    core, z, yhi = lax.axis_index("core"), lax.axis_index("z"), lax.axis_index("yhi")
    x, ylo = lax.axis_index("x"), lax.axis_index("ylo")
    replicas = lax.axis_size(REPLICA)
    place = jnp.stack([(yhi ^ side) * 4 + (z + r) % 4 for side in range(2) for r in RING])
    chip = jnp.arange(8, dtype=jnp.int32)
    away = (chip % 4 - z) % 4
    slots = ((chip // 4) ^ yhi) * 4 + jnp.where(away < 2, away, 5 - away)
    share = jnp.stack([((x + r) % 4) * 2 + (ylo ^ side) for r in RING for side in range(2)])
    core, place, slots, share = (
        v.astype(jnp.int32).reshape(-1) for v in (core, place, slots, share)
    )
    places = jnp.concatenate([place, slots])

    block, h1, h2 = normalize(tokens, norm_gain)
    relay1, relay2 = hop(h1, Y, 1), hop(h2, Y, -1)
    below, above = hop(block, "z", 1), hop(block, "z", -1)
    kv_theirs = swap(tie(kv_weight, block), "core")
    at0, at1, at3, at2 = terms(share, tie(pseudo_grad[0], block), grad_exps[0])
    relay1, relay2, kv_theirs, at0, at1, at2, at3, query_weight = wait(
        relay1, relay2, kv_theirs, at0, at1, at2, at3, query_weight
    )
    query_theirs = swap(query_weight, "core")
    partner = jnp.concatenate([hop(relay1, Y, 1), hop(relay2, Y, -1)], axis=0)
    below, above = mark(below, above)
    far1, far2 = pick(below, above)
    partner, above, below = wait(partner, above, below)
    far1, far2 = hop(far1, "z", 1), hop(far2, "z", -1)
    pbelow, pabove = hop(partner, "z", 1), hop(partner, "z", -1)
    weights = [query_weight, query_theirs, kv_weight, kv_theirs]
    query_a, pair_a = project(core, [block, above, below, far1, far2, partner], weights)
    query_a, far1, far2, at2, at3 = wait(query_a, far1, far2, at2, at3)
    x2, x3 = hop(at2, "x", 1), hop(at3, "x", -1)
    pabove, pbelow, query_a, pair_a, x2, x3, at1, out_weight, places = wait(
        pabove, pbelow, query_a, pair_a, x2, x3, at1, out_weight, places
    )
    pfar1, pfar2 = pick(pbelow, pabove)
    pfar1, pfar2 = hop(pfar1, "z", 1), hop(pfar2, "z", -1)
    out_theirs = swap(out_weight, "core")
    passed = hop(add(at1, x2), "x", 1)
    other_a = swap(pair_a, "core")
    pfar1, pfar2, passed, other_a = wait(pfar1, pfar2, passed, other_a)
    query_l, pair_l = project(core, [pabove, pbelow, pfar1, pfar2], weights)
    other_l = swap(pair_l, "core")
    out_weights = (out_weight, out_theirs)
    mixed, q0, qup, qdown, far_a, far_b = attend(
        core,
        places,
        tuple(range(8)),
        (query_a, query_l),
        (pair_a, pair_l),
        (other_a, other_l),
        out_weights,
    )

    full = out_weight.shape[1]
    half = full // HALVES
    mixed, far_a, far_b = wait(mixed, far_a, far_b)
    far_a, far_b = hop(far_a, "z", 1), hop(far_b, "z", -1)
    mine = (at0, passed, x3)
    count = momentum.shape[0]
    sent, q0, mixed = wait(add(*(part[count:] for part in mine)), q0, mixed)
    theirs = swap(sent, "ylo")
    o0, oup, odown, ofara, ofarb = output(mixed, out_weights)
    far_a, far_b, o0 = wait(far_a, far_b, o0)
    up, down = sums(
        ((0, full), ((qup, 0), (far_a, 0))), ((0, full), ((qdown, 0), (far_b, half)))
    )
    up, down, theirs, ofara, ofarb = wait(up, down, theirs, ofara, ofarb)
    up, down = hop(up, "z", 1), hop(down, "z", -1)
    ofara, ofarb = hop(ofara, "z", 1), hop(ofarb, "z", -1)
    new_momentum, rebuilt = outer(mine, theirs, momentum, hadamard_table(HEAD), replicas)
    beside = swap(rebuilt, "ylo")
    both = jnp.concatenate([rebuilt, beside], axis=0)
    before = hop(both, "x", 1)
    up, down, before, both = wait(up, down, before, both)
    s1, s2 = sums(
        *(((at, half), ((q0, 0), (up, 0), (down, 0))) for at in (0, half))
    )
    oup, odown = sums(
        ((0, full), ((oup, 0), (ofara, 0))),
        ((0, full), ((odown, 0), (ofarb, half))),
        after=(s1,),
    )
    oup, odown = hop(oup, "z", 1), hop(odown, "z", -1)
    s1, s2 = hop(s1, Y, 1), hop(s2, Y, -1)
    after = hop(both, "x", -1)
    s1, s2, before = wait(s1, s2, before)
    s1, s2 = hop(s1, Y, 1), hop(s2, Y, -1)
    ahead = hop(before, "x", 1)
    new_params = apply(share, old, [both, after, before, ahead])
    o0, new_params = wait(o0, new_params)
    attended = sums(
        ((0, full), ((o0, 0), (oup, 0), (odown, 0), (s1, 0), (s2, half))), name="finish"
    )
    return (attended, new_params, new_momentum)


def solution(mesh):
    fine = Mesh(mesh.devices.reshape(4, 2, 2, 4, 2), ("x", "ylo", "yhi", "z", "core"))
    every = REPLICA + TENSOR
    return jax.shard_map(
        local,
        mesh=fine,
        in_specs=(
            P(every, None),
            P(),
            P(None, TENSOR),
            P(None, TENSOR),
            P(TENSOR, None),
            P(REPLICA, TENSOR, None),
            P(REPLICA, TENSOR, None),
            P(TENSOR, None),
            P(TENSOR, REPLICA),
        ),
        out_specs=(P(every, None), P(TENSOR, None), P(TENSOR, REPLICA)),
        check_vma=False,
    )
```

```python
import functools
import math

import jax
import jax.numpy as jnp
from jax import lax
from jax.experimental import pallas as pl
from jax.experimental.pallas import tpu as pltpu
from jax.sharding import Mesh
from jax.sharding import PartitionSpec as P

HEAD = 128
REPLICA = ("x", "ylo")
TENSOR = ("yhi", "z", "core")
ROWS = 64
RING = (0, 1, -1, 2)
Y = ("ylo", "yhi")
HALVES = 2
TILE = 1024
PIECES = (1, 1, 1, HALVES)
MIB = 1024 * 1024


def params(mib=8):
    return pltpu.CompilerParams(vmem_limit_bytes=mib * MIB)


def cost(flops, moved):
    return pl.CostEstimate(flops=int(flops), bytes_accessed=int(moved), transcendentals=0)


def hadamard_table(width):
    index = jnp.arange(width, dtype=jnp.int32)
    common = jnp.bitwise_and(index[:, None], index[None, :])
    parity = jnp.zeros((width, width), jnp.int32)
    for bit in range(int(math.log2(width))):
        parity = parity + jnp.bitwise_and(jnp.right_shift(common, bit), 1)
    sign = 1.0 - 2.0 * jnp.bitwise_and(parity, 1).astype(jnp.float32)
    return sign / math.sqrt(width)


def norm_body(rows_ref, gain_ref, whole_ref, *half_refs):
    values = rows_ref[...].astype(jnp.float32)
    power = jnp.mean(values * values, axis=-1, keepdims=True)
    normed = (values * lax.rsqrt(power + 1e-05) * gain_ref[...]).astype(jnp.bfloat16)
    whole_ref[...] = normed
    count = normed.shape[0] // HALVES
    for at, half_ref in enumerate(half_refs):
        half_ref[...] = normed[at * count : (at + 1) * count]


def normalize(rows, gain):
    count, width = rows.shape
    return pl.pallas_call(
        norm_body,
        out_shape=[
            jax.ShapeDtypeStruct((c, width), jnp.bfloat16)
            for c in [count] + [count // HALVES] * HALVES
        ],
        compiler_params=params(56),
        cost_estimate=cost(4 * rows.size, 6 * rows.size),
        name="normalize",
    )(rows, gain.reshape(1, width))


def project_body(core_ref, *refs):
    blocks, refs = refs[:-12], refs[-12:]
    weights, (query_out, pair_out, total), held, arrived = refs[:4], refs[4:7], refs[7:11], refs[11]
    half = weights[0].shape[1]
    depth = weights[0].shape[0]
    chunks = arrived.shape[1]
    chunk = depth // chunks

    def copies_of(at):
        span = pl.ds(pl.multiple_of(at * chunk, chunk), chunk)
        return [
            pltpu.make_async_copy(weight.at[span, :], place.at[span, :], arrived.at[kind, at])
            for kind, (weight, place) in enumerate(zip(weights, held))
        ]

    for at in range(chunks):
        for copy in copies_of(at):
            copy.start()
    total[...] = jnp.zeros_like(total)
    qa_ref, qb_ref, ka_ref, kb_ref = held

    def step(at, carry):
        for copy in copies_of(at):
            copy.wait()
        span = pl.ds(pl.multiple_of(at * chunk, chunk), chunk)
        rows = jnp.concatenate([ref[:, span] for ref in blocks], axis=0)
        both = jnp.concatenate([ka_ref[span, :], kb_ref[span, :]], axis=1)
        for start, weight in ((0, qa_ref[span, :]), (half, qb_ref[span, :]), (2 * half, both)):
            total[:, start : start + weight.shape[1]] += jnp.dot(
                rows, weight, preferred_element_type=jnp.float32
            )
        return carry

    lax.fori_loop(0, chunks, step, 0)
    flip = core_ref[0] == 0
    value = total[...].astype(jnp.bfloat16)
    query_out[...] = value[:, : 2 * half]
    left, right = value[:, 2 * half : 2 * half + HEAD], value[:, 2 * half + HEAD :]
    pair_out[:, :HEAD] = jnp.where(flip, left, right)
    pair_out[:, HEAD:] = jnp.where(flip, right, left)


def project(core, blocks, weights):
    width = blocks[0].shape[1]
    count = sum(block.shape[0] for block in blocks)
    qcols = 2 * weights[0].shape[1]
    kcols = 2 * weights[2].shape[1]
    vmem = pl.BlockSpec(memory_space=pltpu.VMEM)
    return pl.pallas_call(
        project_body,
        in_specs=[pl.BlockSpec(memory_space=pltpu.SMEM)]
        + [vmem] * len(blocks)
        + [pl.BlockSpec(memory_space=pl.ANY)] * len(weights),
        out_specs=[vmem, vmem],
        out_shape=[
            jax.ShapeDtypeStruct((count, qcols), jnp.bfloat16),
            jax.ShapeDtypeStruct((count, kcols), jnp.bfloat16),
        ],
        scratch_shapes=[pltpu.VMEM((count, qcols + kcols), jnp.float32)]
        + [pltpu.VMEM(weight.shape, jnp.bfloat16) for weight in weights]
        + [pltpu.SemaphoreType.DMA((len(weights), width // TILE))],
        compiler_params=params(56),
        cost_estimate=cost(
            3 * count * width * (qcols + kcols), 2 * width * (count + qcols + kcols)
        ),
        name="project",
    )(core, *blocks, *weights)


def copies_of(weights, held, arrived, first, at):
    half = weights[0].shape[0]
    span = pl.ds(pl.multiple_of(at * TILE, TILE), TILE)
    return [
        pltpu.make_async_copy(
            weight.at[:, pl.ds(pl.multiple_of(first + at * TILE, TILE), TILE)],
            held.at[pl.ds(kind * half, half), span],
            arrived.at[at, kind],
        )
        for kind, weight in enumerate(weights)
    ]


def fetch(weights, held, arrived, first):
    for at in range(held.shape[1] // TILE):
        for copy in copies_of(weights, held, arrived, first, at):
            copy.start()


def multiply(rows_of, weights, held, arrived, first, out_refs):
    tiles = held.shape[1] // TILE
    parts = max(len(pieces) for pieces in out_refs)
    for part in range(parts):

        def step(at, carry, part=part):
            for copy in copies_of(weights, held, arrived, first, at):
                copy.wait()
            span = pl.ds(pl.multiple_of(at * TILE, TILE), TILE)
            result = jnp.dot(rows_of(), held[:, span], preferred_element_type=jnp.float32)
            result = result.astype(jnp.bfloat16)
            for block, pieces in enumerate(out_refs):
                back = part * (tiles // parts) if len(pieces) == parts else 0
                there = pl.ds(pl.multiple_of((at - back) * TILE, TILE), TILE)
                pieces[part if len(pieces) == parts else 0][:, there] = result[
                    block * ROWS : (block + 1) * ROWS
                ]
            return carry

        lax.fori_loop(part * (tiles // parts), (part + 1) * (tiles // parts), step, 0)


def attend_body(order, core_ref, place_ref, *refs):
    ins, refs = refs[: -8 - sum(PIECES)], refs[-8 - sum(PIECES) :]
    weights, mixed_ref, out_refs = refs[:2], refs[2], list(refs[3 : 3 + sum(PIECES)])
    query_ref, own_ref, other_ref, held, arrived = refs[3 + sum(PIECES) :]
    fetch(weights, held, arrived, 0)
    core = core_ref[0]
    parts = len(ins) // 3
    for kind, whole in enumerate((query_ref, own_ref, other_ref)):
        at = 0
        for part in ins[kind * parts : (kind + 1) * parts]:
            for top in range(0, part.shape[0], ROWS):
                place = pl.ds(pl.multiple_of(place_ref[order[at]] * ROWS, ROWS), ROWS)
                whole[place, :] = part[top : top + ROWS]
                at += 1
    count, qcols = query_ref.shape
    heads = qcols // HEAD
    block = 2 * ROWS
    scale = 1.0 / math.sqrt(HEAD)
    shift = ROWS.bit_length() - 1
    for step in range(count // block):
        rows = slice(step * block, (step + 1) * block)
        span = (step + 1) * block
        query = jnp.concatenate(
            [query_ref[rows, h * HEAD : (h + 1) * HEAD] for h in range(heads)], axis=0
        )
        contract = (((1,), (1,)), ((), ()))
        row = lax.broadcasted_iota(jnp.int32, (block, block), 0)
        col = lax.broadcasted_iota(jnp.int32, (block, block), 1)
        own_seen = jnp.concatenate([col <= row] * heads, axis=0)
        other_seen = jnp.concatenate(
            [jnp.right_shift(col, shift) < jnp.right_shift(row, shift) + core] * heads, axis=0
        )

        def scores_of(ref, seen):
            raw = lax.dot_general(
                query, ref[:span, :HEAD], contract, preferred_element_type=jnp.float32
            )
            tail = jnp.where(seen, raw[:, span - block :], -jnp.inf)
            if span == block:
                return tail
            return jnp.concatenate([raw[:, : span - block], tail], axis=1)

        scores = jnp.concatenate(
            [scores_of(own_ref, own_seen), scores_of(other_ref, other_seen)], axis=1
        )
        peak = jnp.max(scores, axis=-1, keepdims=True)
        probs = jnp.exp((scores - peak) * scale).astype(jnp.bfloat16)
        ones = jnp.ones((span, HEAD), jnp.bfloat16)
        total = jnp.zeros((block * heads, 2 * HEAD), jnp.float32)
        for part, ref in enumerate((own_ref, other_ref)):
            values = jnp.concatenate([ref[:span, HEAD:], ones], axis=1)
            total += jnp.dot(
                probs[:, part * span : (part + 1) * span],
                values,
                preferred_element_type=jnp.float32,
            )
        mixed = (total[:, :HEAD] / total[:, HEAD:]).astype(jnp.bfloat16)
        for part in range(block // ROWS):
            slot = place_ref[8 + step * (block // ROWS) + part]
            place = pl.ds(pl.multiple_of(slot * ROWS, ROWS), ROWS)
            for h in range(heads):
                top = h * block + part * ROWS
                mixed_ref[place, h * HEAD : (h + 1) * HEAD] = mixed[top : top + ROWS]

    outs = [[out_refs.pop(0) for _ in range(piece)] for piece in PIECES]
    multiply(lambda: mixed_ref[count // 2 :], weights, held, arrived, 0, outs)


def attend(core, places, order, queries, own, other, weights):
    count, qcols = sum(q.shape[0] for q in queries), queries[0].shape[1]
    kcols = own[0].shape[1]
    args = [*queries, *own, *other]
    vmem = pl.BlockSpec(memory_space=pltpu.VMEM)
    depth, width = weights[0].shape
    return pl.pallas_call(
        functools.partial(attend_body, order),
        in_specs=[pl.BlockSpec(memory_space=pltpu.SMEM)] * 2
        + [vmem] * len(args)
        + [pl.BlockSpec(memory_space=pl.ANY)] * 2,
        out_specs=[vmem] * (1 + sum(PIECES)),
        out_shape=[jax.ShapeDtypeStruct((count, qcols), jnp.bfloat16)]
        + [
            jax.ShapeDtypeStruct((ROWS, width // piece), jnp.bfloat16)
            for piece in PIECES
            for _ in range(piece)
        ],
        scratch_shapes=[pltpu.VMEM((count, cols), jnp.bfloat16) for cols in (qcols, kcols, kcols)]
        + [
            pltpu.VMEM((2 * depth, width), jnp.bfloat16),
            pltpu.SemaphoreType.DMA((width // TILE, 2)),
        ],
        compiler_params=params(56),
        cost_estimate=cost(8 * count * count * qcols, 4 * count * qcols + 4 * depth * width),
        name="attend",
    )(core, places, *args, *weights)


def output_body(mixed_ref, *refs):
    weights, out_refs, (held, arrived) = refs[:2], list(refs[2:-2]), refs[-2:]
    fetch(weights, held, arrived, 0)
    count = mixed_ref.shape[0] // 2
    outs = [[out_refs.pop(0) for _ in range(piece)] for piece in PIECES]
    multiply(lambda: mixed_ref[:count], weights, held, arrived, 0, outs)


def output(mixed, weights):
    depth, width = weights[0].shape
    count = mixed.shape[0] // 2
    vmem = pl.BlockSpec(memory_space=pltpu.VMEM)
    widths = [width // piece for piece in PIECES for _ in range(piece)]
    return list(
        pl.pallas_call(
            output_body,
            in_specs=[vmem] + [pl.BlockSpec(memory_space=pl.ANY)] * 2,
            out_specs=[vmem] * len(widths),
            out_shape=[jax.ShapeDtypeStruct((ROWS, w), jnp.bfloat16) for w in widths],
            scratch_shapes=[
                pltpu.VMEM((2 * depth, width), jnp.bfloat16),
                pltpu.SemaphoreType.DMA((width // TILE, 2)),
            ],
            compiler_params=params(56),
            cost_estimate=cost(
                4 * count * depth * width, 2 * (2 * depth * width + count * width)
            ),
            name="output",
        )(mixed, *weights)
    )


def mark_body(*refs):
    del refs


def mark(*blocks):
    anywhere = [pl.BlockSpec(memory_space=pl.ANY)] * len(blocks)
    return pl.pallas_call(
        mark_body,
        in_specs=anywhere,
        out_specs=anywhere,
        out_shape=[jax.ShapeDtypeStruct(block.shape, block.dtype) for block in blocks],
        input_output_aliases={at: at for at in range(len(blocks))},
        compiler_params=params(),
        cost_estimate=cost(7e10, 4096),
        name="mark",
    )(*blocks)


def pick_body(below_ref, above_ref, first_ref, second_ref):
    first_ref[...] = below_ref[...]
    second_ref[...] = above_ref[...]


def pick(below, above):
    shape = jax.ShapeDtypeStruct((below.shape[0] // HALVES, below.shape[1]), below.dtype)
    return pl.pallas_call(
        pick_body,
        grid=(1,),
        in_specs=[pl.BlockSpec(shape.shape, lambda i, at=at: (at, 0)) for at in range(HALVES)],
        out_specs=[pl.BlockSpec(shape.shape, lambda i: (0, 0))] * HALVES,
        out_shape=[shape, shape],
        compiler_params=params(),
        cost_estimate=cost(1e8, 4 * below.size),
        name="pick",
    )(below, above)


def sums_body(shapes, *refs):
    outs = refs[-len(shapes) :]
    first = 0
    for out_ref, (offset, starts) in zip(outs, shapes):
        step = min(ref.shape[1] for ref in (out_ref, *refs[first : first + len(starts)]))
        for left in range(0, out_ref.shape[1], step):
            total = None
            for at, start in enumerate(starts):
                ref = refs[first + at]
                col = offset + left - start
                if 0 <= col < ref.shape[1]:
                    term = ref[:, col : col + step].astype(jnp.float32)
                    total = term if total is None else total + term
            out_ref[:, left : left + step] = total.astype(jnp.bfloat16)
        first += len(starts)


def sums(*groups, name="sums", after=()):
    args = [array for _, terms in groups for array, _ in terms]
    shapes = tuple((first, tuple(start for _, start in terms)) for (first, _), terms in groups)
    result = pl.pallas_call(
        functools.partial(sums_body, shapes),
        in_specs=[pl.BlockSpec(memory_space=pltpu.VMEM)] * len(args)
        + [pl.BlockSpec(memory_space=pl.ANY)] * len(after),
        out_shape=[
            jax.ShapeDtypeStruct((terms[0][0].shape[0], width), jnp.bfloat16)
            for (_, width), terms in groups
        ],
        compiler_params=params(16),
        cost_estimate=cost(sum(a.size for a in args), 3 * sum(a.size for a in args)),
        name=name,
    )(*args, *after)
    return result if len(groups) > 1 else result[0]


def terms_body(block_ref, codes_ref, exps_ref, *out_refs):
    scale = jnp.exp2(exps_ref[...].astype(jnp.float32))
    lane = lax.broadcasted_iota(jnp.int32, scale.shape, 1)
    count = codes_ref.shape[0]
    for at, out_ref in enumerate(out_refs):
        for side in range(2):
            block = block_ref[2 * at + side]
            cols = pl.ds(pl.multiple_of(block * HEAD, HEAD), HEAD)
            mine = jnp.sum(jnp.where(lane == block, scale, 0.0), axis=1, keepdims=True)
            out_ref[side * count : (side + 1) * count] = (
                codes_ref[:, cols].astype(jnp.float32) * mine
            ).astype(jnp.bfloat16)


def terms(blocks, codes, exps):
    count, width = codes.shape
    vmem = pl.BlockSpec(memory_space=pltpu.VMEM)
    return pl.pallas_call(
        terms_body,
        in_specs=[pl.BlockSpec(memory_space=pltpu.SMEM), vmem, vmem],
        out_shape=[jax.ShapeDtypeStruct((2 * count, HEAD), jnp.bfloat16)] * len(RING),
        compiler_params=params(),
        cost_estimate=cost(codes.size, 4 * codes.size),
        name="terms",
    )(blocks, codes, exps)


def outer_body(replicas, *refs):
    mine_refs, theirs_ref, momentum_ref, table_ref, momentum_out, rebuilt_ref = (
        refs[:3],
        *refs[3:],
    )
    table = table_ref[...]

    def rotate(values):
        return jnp.dot(
            values, table, precision=lax.Precision.HIGHEST, preferred_element_type=jnp.float32
        )

    summed = theirs_ref[...].astype(jnp.float32)
    for ref in mine_refs:
        summed += ref[: summed.shape[0]].astype(jnp.float32)
    averaged = rotate(summed / replicas)
    fresh = 0.9 * momentum_ref[...] + averaged
    momentum_out[...] = fresh
    turned = rotate(0.7 * (averaged + 0.9 * fresh))
    scales = (jnp.max(jnp.abs(turned), axis=-1, keepdims=True) + 1e-06).astype(jnp.bfloat16)
    scales = scales.astype(jnp.float32)
    codes = (turned / scales).astype(jnp.bfloat16)
    rebuilt_ref[...] = rotate(codes.astype(jnp.float32) * scales).astype(jnp.bfloat16)


def outer(mine, theirs, momentum, table, replicas):
    return pl.pallas_call(
        functools.partial(outer_body, replicas),
        out_shape=[
            jax.ShapeDtypeStruct(momentum.shape, jnp.float32),
            jax.ShapeDtypeStruct(momentum.shape, jnp.bfloat16),
        ],
        compiler_params=params(),
        cost_estimate=cost(40 * theirs.size * HEAD, 12 * theirs.size),
        name="outer",
    )(*mine, theirs, momentum, table)


def apply_body(block_ref, params_ref, *refs):
    rebuilt_refs, out_ref = refs[:-1], refs[-1]
    count = out_ref.shape[0]
    for at, rebuilt_ref in enumerate(rebuilt_refs):
        for side in range(2):
            cols = pl.ds(pl.multiple_of(block_ref[2 * at + side] * HEAD, HEAD), HEAD)
            rebuilt = rebuilt_ref[side * count : (side + 1) * count].astype(jnp.float32)
            out_ref[:, cols] = (params_ref[:, cols].astype(jnp.float32) - rebuilt).astype(
                jnp.bfloat16
            )


def apply(blocks, old, rebuilt):
    vmem = pl.BlockSpec(memory_space=pltpu.VMEM)
    return pl.pallas_call(
        apply_body,
        in_specs=[pl.BlockSpec(memory_space=pltpu.SMEM)] + [vmem] * (1 + len(rebuilt)),
        out_shape=jax.ShapeDtypeStruct(old.shape, jnp.bfloat16),
        compiler_params=params(),
        cost_estimate=cost(old.size, 6 * old.size),
        name="apply",
    )(blocks, old, *rebuilt)


def swap(block, axis):
    return lax.ppermute(block, axis, [(0, 1), (1, 0)])


def hop(block, axis, way):
    at = (0, 2, 1, 3) if axis == Y else (0, 1, 2, 3)
    return lax.ppermute(block, axis, [(at[i], at[(i + way) % 4]) for i in range(4)])


def add(*blocks):
    total = blocks[0].astype(jnp.float32)
    for block in blocks[1:]:
        total = total + block.astype(jnp.float32)
    return total.astype(jnp.bfloat16)


def wait(*blocks):
    return lax.optimization_barrier(blocks)


def tie(block, *others):
    return lax.optimization_barrier((block, *others))[0]


def local(
    tokens, norm_gain, query_weight, kv_weight, out_weight, pseudo_grad, grad_exps, old, momentum
):
    core, z, yhi = lax.axis_index("core"), lax.axis_index("z"), lax.axis_index("yhi")
    x, ylo = lax.axis_index("x"), lax.axis_index("ylo")
    replicas = lax.axis_size(REPLICA)
    place = jnp.stack([(yhi ^ side) * 4 + (z + r) % 4 for side in range(2) for r in RING])
    chip = jnp.arange(8, dtype=jnp.int32)
    away = (chip % 4 - z) % 4
    slots = ((chip // 4) ^ yhi) * 4 + jnp.where(away < 2, away, 5 - away)
    share = jnp.stack([((x + r) % 4) * 2 + (ylo ^ side) for r in RING for side in range(2)])
    core, place, slots, share = (
        v.astype(jnp.int32).reshape(-1) for v in (core, place, slots, share)
    )
    places = jnp.concatenate([place, slots])

    block, h1, h2 = normalize(tokens, norm_gain)
    relay1, relay2 = hop(h1, Y, 1), hop(h2, Y, -1)
    below, above = hop(block, "z", 1), hop(block, "z", -1)
    kv_theirs = swap(tie(kv_weight, block), "core")
    at0, at1, at3, at2 = terms(share, tie(pseudo_grad[0], block), grad_exps[0])
    relay1, relay2, kv_theirs, at0, at1, at2, at3, query_weight = wait(
        relay1, relay2, kv_theirs, at0, at1, at2, at3, query_weight
    )
    query_theirs = swap(query_weight, "core")
    partner = jnp.concatenate([hop(relay1, Y, 1), hop(relay2, Y, -1)], axis=0)
    below, above = mark(below, above)
    far1, far2 = pick(below, above)
    partner, above, below = wait(partner, above, below)
    far1, far2 = hop(far1, "z", 1), hop(far2, "z", -1)
    pbelow, pabove = hop(partner, "z", 1), hop(partner, "z", -1)
    weights = [query_weight, query_theirs, kv_weight, kv_theirs]
    query_a, pair_a = project(core, [block, above, below, far1, far2], weights)
    query_a, far1, far2, at2, at3 = wait(query_a, far1, far2, at2, at3)
    x2, x3 = hop(at2, "x", 1), hop(at3, "x", -1)
    pabove, pbelow, query_a, pair_a, x2, x3, at1, out_weight, places = wait(
        pabove, pbelow, query_a, pair_a, x2, x3, at1, out_weight, places
    )
    pfar1, pfar2 = pick(pbelow, pabove)
    pfar1, pfar2 = hop(pfar1, "z", 1), hop(pfar2, "z", -1)
    out_theirs = swap(out_weight, "core")
    query_m, pair_m = project(core, [partner, pabove, pbelow], weights)
    query_m, pair_m, x2, at1 = wait(query_m, pair_m, x2, at1)
    passed = hop(add(at1, x2), "x", 1)
    other_a, other_m = swap(pair_a, "core"), swap(pair_m, "core")
    pfar1, pfar2, query_m = wait(pfar1, pfar2, query_m)
    query_l, pair_l = project(core, [pfar1, pfar2], weights)
    query_l, pair_l, passed = wait(query_l, pair_l, passed)
    other_l = swap(pair_l, "core")
    out_weights = (out_weight, out_theirs)
    mixed, q0, qup, qdown, far_a, far_b = attend(
        core,
        places,
        tuple(range(8)),
        (query_a, query_m, query_l),
        (pair_a, pair_m, pair_l),
        (other_a, other_m, other_l),
        out_weights,
    )

    full = out_weight.shape[1]
    half = full // HALVES
    mixed, far_a, far_b = wait(mixed, far_a, far_b)
    far_a, far_b = hop(far_a, "z", 1), hop(far_b, "z", -1)
    mine = (at0, passed, x3)
    count = momentum.shape[0]
    sent, q0, mixed = wait(add(*(part[count:] for part in mine)), q0, mixed)
    theirs = swap(sent, "ylo")
    o0, oup, odown, ofara, ofarb = output(mixed, out_weights)
    far_a, far_b, o0 = wait(far_a, far_b, o0)
    up, down = sums(
        ((0, full), ((qup, 0), (far_a, 0))), ((0, full), ((qdown, 0), (far_b, half)))
    )
    up, down, theirs, ofara, ofarb = wait(up, down, theirs, ofara, ofarb)
    up, down = hop(up, "z", 1), hop(down, "z", -1)
    ofara, ofarb = hop(ofara, "z", 1), hop(ofarb, "z", -1)
    new_momentum, rebuilt = outer(mine, theirs, momentum, hadamard_table(HEAD), replicas)
    beside = swap(rebuilt, "ylo")
    both = jnp.concatenate([rebuilt, beside], axis=0)
    before = hop(both, "x", 1)
    up, down, before, both = wait(up, down, before, both)
    s1, s2 = sums(
        *(((at, half), ((q0, 0), (up, 0), (down, 0))) for at in (0, half))
    )
    oup, odown = sums(
        ((0, full), ((oup, 0), (ofara, 0))),
        ((0, full), ((odown, 0), (ofarb, half))),
        after=(s1,),
    )
    oup, odown = hop(oup, "z", 1), hop(odown, "z", -1)
    s1, s2 = hop(s1, Y, 1), hop(s2, Y, -1)
    after = hop(both, "x", -1)
    s1, s2, before = wait(s1, s2, before)
    s1, s2 = hop(s1, Y, 1), hop(s2, Y, -1)
    ahead = hop(before, "x", 1)
    new_params = apply(share, old, [both, after, before, ahead])
    o0, new_params = wait(o0, new_params)
    attended = sums(
        ((0, full), ((o0, 0), (oup, 0), (odown, 0), (s1, 0), (s2, half))), name="finish"
    )
    return (attended, new_params, new_momentum)


def solution(mesh):
    fine = Mesh(mesh.devices.reshape(4, 2, 2, 4, 2), ("x", "ylo", "yhi", "z", "core"))
    every = REPLICA + TENSOR
    return jax.shard_map(
        local,
        mesh=fine,
        in_specs=(
            P(every, None),
            P(),
            P(None, TENSOR),
            P(None, TENSOR),
            P(TENSOR, None),
            P(REPLICA, TENSOR, None),
            P(REPLICA, TENSOR, None),
            P(TENSOR, None),
            P(TENSOR, REPLICA),
        ),
        out_specs=(P(every, None), P(TENSOR, None), P(TENSOR, REPLICA)),
        check_vma=False,
    )
```

```python
import functools
import math

import jax
import jax.numpy as jnp
from jax import lax
from jax.experimental import pallas as pl
from jax.experimental.pallas import tpu as pltpu
from jax.sharding import Mesh
from jax.sharding import PartitionSpec as P

HEAD = 128
REPLICA = ("x", "ylo")
TENSOR = ("yhi", "z", "core")
ROWS = 64
RING = (0, 1, -1, 2)
Y = ("ylo", "yhi")
HALVES = 2
TILE = 1024
STRIP = 256
PIECES = (1, 1, 1, HALVES)
MIB = 1024 * 1024


def params(mib=8):
    return pltpu.CompilerParams(vmem_limit_bytes=mib * MIB)


def cost(flops, moved):
    return pl.CostEstimate(flops=int(flops), bytes_accessed=int(moved), transcendentals=0)


def hadamard_table(width):
    index = jnp.arange(width, dtype=jnp.int32)
    common = jnp.bitwise_and(index[:, None], index[None, :])
    parity = jnp.zeros((width, width), jnp.int32)
    for bit in range(int(math.log2(width))):
        parity = parity + jnp.bitwise_and(jnp.right_shift(common, bit), 1)
    sign = 1.0 - 2.0 * jnp.bitwise_and(parity, 1).astype(jnp.float32)
    return sign / math.sqrt(width)


def norm_body(rows_ref, gain_ref, whole_ref, *half_refs):
    values = rows_ref[...].astype(jnp.float32)
    power = jnp.mean(values * values, axis=-1, keepdims=True)
    normed = (values * lax.rsqrt(power + 1e-05) * gain_ref[...]).astype(jnp.bfloat16)
    whole_ref[...] = normed
    count = normed.shape[0] // HALVES
    for at, half_ref in enumerate(half_refs):
        half_ref[...] = normed[at * count : (at + 1) * count]


def normalize(rows, gain):
    count, width = rows.shape
    return pl.pallas_call(
        norm_body,
        out_shape=[
            jax.ShapeDtypeStruct((c, width), jnp.bfloat16)
            for c in [count] + [count // HALVES] * HALVES
        ],
        compiler_params=params(56),
        cost_estimate=cost(4 * rows.size, 6 * rows.size),
        name="normalize",
    )(rows, gain.reshape(1, width))


def project_body(core_ref, *refs):
    blocks, refs = refs[:-12], refs[-12:]
    weights, (query_out, pair_out, total), held, arrived = refs[:4], refs[4:7], refs[7:11], refs[11]
    half = weights[0].shape[1]
    depth = weights[0].shape[0]
    chunks = arrived.shape[1]
    chunk = depth // chunks

    def copies_of(at):
        span = pl.ds(pl.multiple_of(at * chunk, chunk), chunk)
        return [
            pltpu.make_async_copy(weight.at[span, :], place.at[span, :], arrived.at[kind, at])
            for kind, (weight, place) in enumerate(zip(weights, held))
        ]

    for at in range(chunks):
        for copy in copies_of(at):
            copy.start()
    total[...] = jnp.zeros_like(total)
    qa_ref, qb_ref, ka_ref, kb_ref = held

    def step(at, carry):
        for copy in copies_of(at):
            copy.wait()
        span = pl.ds(pl.multiple_of(at * chunk, chunk), chunk)
        rows = jnp.concatenate([ref[:, span] for ref in blocks], axis=0)
        both = jnp.concatenate([ka_ref[span, :], kb_ref[span, :]], axis=1)
        for start, weight in ((0, qa_ref[span, :]), (half, qb_ref[span, :]), (2 * half, both)):
            total[:, start : start + weight.shape[1]] += jnp.dot(
                rows, weight, preferred_element_type=jnp.float32
            )
        return carry

    lax.fori_loop(0, chunks, step, 0)
    flip = core_ref[0] == 0
    value = total[...].astype(jnp.bfloat16)
    query_out[...] = value[:, : 2 * half]
    left, right = value[:, 2 * half : 2 * half + HEAD], value[:, 2 * half + HEAD :]
    pair_out[:, :HEAD] = jnp.where(flip, left, right)
    pair_out[:, HEAD:] = jnp.where(flip, right, left)


def project(core, blocks, weights):
    width = blocks[0].shape[1]
    count = sum(block.shape[0] for block in blocks)
    qcols = 2 * weights[0].shape[1]
    kcols = 2 * weights[2].shape[1]
    vmem = pl.BlockSpec(memory_space=pltpu.VMEM)
    return pl.pallas_call(
        project_body,
        in_specs=[pl.BlockSpec(memory_space=pltpu.SMEM)]
        + [vmem] * len(blocks)
        + [pl.BlockSpec(memory_space=pl.ANY)] * len(weights),
        out_specs=[vmem, vmem],
        out_shape=[
            jax.ShapeDtypeStruct((count, qcols), jnp.bfloat16),
            jax.ShapeDtypeStruct((count, kcols), jnp.bfloat16),
        ],
        scratch_shapes=[pltpu.VMEM((count, qcols + kcols), jnp.float32)]
        + [pltpu.VMEM(weight.shape, jnp.bfloat16) for weight in weights]
        + [pltpu.SemaphoreType.DMA((len(weights), width // TILE))],
        compiler_params=params(56),
        cost_estimate=cost(
            3 * count * width * (qcols + kcols), 2 * width * (count + qcols + kcols)
        ),
        name="project",
    )(core, *blocks, *weights)


def copies_of(weights, held, arrived, first, at):
    half = weights[0].shape[0]
    span = pl.ds(pl.multiple_of(at * TILE, TILE), TILE)
    return [
        pltpu.make_async_copy(
            weight.at[:, pl.ds(pl.multiple_of(first + at * TILE, TILE), TILE)],
            held.at[pl.ds(kind * half, half), span],
            arrived.at[at, kind],
        )
        for kind, weight in enumerate(weights)
    ]


def fetch(weights, held, arrived, first):
    for at in range(held.shape[1] // TILE):
        for copy in copies_of(weights, held, arrived, first, at):
            copy.start()


def multiply(rows_of, weights, held, arrived, first, out_refs):
    tiles = held.shape[1] // TILE
    parts = max(len(pieces) for pieces in out_refs)
    for part in range(parts):

        def step(at, carry, part=part):
            for copy in copies_of(weights, held, arrived, first, at):
                copy.wait()
            rows = rows_of()
            for left in range(0, TILE, STRIP):
                strip = pl.ds(pl.multiple_of(at * TILE + left, STRIP), STRIP)
                result = jnp.dot(rows, held[:, strip], preferred_element_type=jnp.float32)
                result = result.astype(jnp.bfloat16)
                for block, pieces in enumerate(out_refs):
                    back = part * (tiles // parts) if len(pieces) == parts else 0
                    there = pl.ds(pl.multiple_of((at - back) * TILE + left, STRIP), STRIP)
                    pieces[part if len(pieces) == parts else 0][:, there] = result[
                        block * ROWS : (block + 1) * ROWS
                    ]
            return carry

        lax.fori_loop(part * (tiles // parts), (part + 1) * (tiles // parts), step, 0)


def attend_body(order, core_ref, place_ref, *refs):
    ins, refs = refs[: -8 - sum(PIECES)], refs[-8 - sum(PIECES) :]
    weights, mixed_ref, out_refs = refs[:2], refs[2], list(refs[3 : 3 + sum(PIECES)])
    query_ref, own_ref, other_ref, held, arrived = refs[3 + sum(PIECES) :]
    fetch(weights, held, arrived, 0)
    core = core_ref[0]
    parts = len(ins) // 3
    for kind, whole in enumerate((query_ref, own_ref, other_ref)):
        at = 0
        for part in ins[kind * parts : (kind + 1) * parts]:
            for top in range(0, part.shape[0], ROWS):
                place = pl.ds(pl.multiple_of(place_ref[order[at]] * ROWS, ROWS), ROWS)
                whole[place, :] = part[top : top + ROWS]
                at += 1
    count, qcols = query_ref.shape
    heads = qcols // HEAD
    block = 2 * ROWS
    scale = 1.0 / math.sqrt(HEAD)
    shift = ROWS.bit_length() - 1
    for step in range(count // block):
        rows = slice(step * block, (step + 1) * block)
        span = (step + 1) * block
        query = jnp.concatenate(
            [query_ref[rows, h * HEAD : (h + 1) * HEAD] for h in range(heads)], axis=0
        )
        contract = (((1,), (1,)), ((), ()))
        row = lax.broadcasted_iota(jnp.int32, (block, block), 0)
        col = lax.broadcasted_iota(jnp.int32, (block, block), 1)
        own_seen = jnp.concatenate([col <= row] * heads, axis=0)
        other_seen = jnp.concatenate(
            [jnp.right_shift(col, shift) < jnp.right_shift(row, shift) + core] * heads, axis=0
        )

        def scores_of(ref, seen):
            raw = lax.dot_general(
                query, ref[:span, :HEAD], contract, preferred_element_type=jnp.float32
            )
            tail = jnp.where(seen, raw[:, span - block :], -jnp.inf)
            if span == block:
                return tail
            return jnp.concatenate([raw[:, : span - block], tail], axis=1)

        scores = jnp.concatenate(
            [scores_of(own_ref, own_seen), scores_of(other_ref, other_seen)], axis=1
        )
        peak = jnp.max(scores, axis=-1, keepdims=True)
        probs = jnp.exp((scores - peak) * scale).astype(jnp.bfloat16)
        ones = jnp.ones((span, HEAD), jnp.bfloat16)
        total = jnp.zeros((block * heads, 2 * HEAD), jnp.float32)
        for part, ref in enumerate((own_ref, other_ref)):
            values = jnp.concatenate([ref[:span, HEAD:], ones], axis=1)
            total += jnp.dot(
                probs[:, part * span : (part + 1) * span],
                values,
                preferred_element_type=jnp.float32,
            )
        mixed = (total[:, :HEAD] / total[:, HEAD:]).astype(jnp.bfloat16)
        for part in range(block // ROWS):
            slot = place_ref[8 + step * (block // ROWS) + part]
            place = pl.ds(pl.multiple_of(slot * ROWS, ROWS), ROWS)
            for h in range(heads):
                top = h * block + part * ROWS
                mixed_ref[place, h * HEAD : (h + 1) * HEAD] = mixed[top : top + ROWS]

    outs = [[out_refs.pop(0) for _ in range(piece)] for piece in PIECES]
    multiply(lambda: mixed_ref[count // 2 :], weights, held, arrived, 0, outs)


def attend(core, places, order, queries, own, other, weights):
    count, qcols = sum(q.shape[0] for q in queries), queries[0].shape[1]
    kcols = own[0].shape[1]
    args = [*queries, *own, *other]
    vmem = pl.BlockSpec(memory_space=pltpu.VMEM)
    depth, width = weights[0].shape
    return pl.pallas_call(
        functools.partial(attend_body, order),
        in_specs=[pl.BlockSpec(memory_space=pltpu.SMEM)] * 2
        + [vmem] * len(args)
        + [pl.BlockSpec(memory_space=pl.ANY)] * 2,
        out_specs=[vmem] * (1 + sum(PIECES)),
        out_shape=[jax.ShapeDtypeStruct((count, qcols), jnp.bfloat16)]
        + [
            jax.ShapeDtypeStruct((ROWS, width // piece), jnp.bfloat16)
            for piece in PIECES
            for _ in range(piece)
        ],
        scratch_shapes=[pltpu.VMEM((count, cols), jnp.bfloat16) for cols in (qcols, kcols, kcols)]
        + [
            pltpu.VMEM((2 * depth, width), jnp.bfloat16),
            pltpu.SemaphoreType.DMA((width // TILE, 2)),
        ],
        compiler_params=params(56),
        cost_estimate=cost(8 * count * count * qcols, 4 * count * qcols + 4 * depth * width),
        name="attend",
    )(core, places, *args, *weights)


def output_body(mixed_ref, *refs):
    weights, out_refs, (held, arrived) = refs[:2], list(refs[2:-2]), refs[-2:]
    fetch(weights, held, arrived, 0)
    count = mixed_ref.shape[0] // 2
    outs = [[out_refs.pop(0) for _ in range(piece)] for piece in PIECES]
    multiply(lambda: mixed_ref[:count], weights, held, arrived, 0, outs)


def output(mixed, weights):
    depth, width = weights[0].shape
    count = mixed.shape[0] // 2
    vmem = pl.BlockSpec(memory_space=pltpu.VMEM)
    widths = [width // piece for piece in PIECES for _ in range(piece)]
    return list(
        pl.pallas_call(
            output_body,
            in_specs=[vmem] + [pl.BlockSpec(memory_space=pl.ANY)] * 2,
            out_specs=[vmem] * len(widths),
            out_shape=[jax.ShapeDtypeStruct((ROWS, w), jnp.bfloat16) for w in widths],
            scratch_shapes=[
                pltpu.VMEM((2 * depth, width), jnp.bfloat16),
                pltpu.SemaphoreType.DMA((width // TILE, 2)),
            ],
            compiler_params=params(56),
            cost_estimate=cost(
                4 * count * depth * width, 2 * (2 * depth * width + count * width)
            ),
            name="output",
        )(mixed, *weights)
    )


def mark_body(*refs):
    del refs


def mark(*blocks):
    anywhere = [pl.BlockSpec(memory_space=pl.ANY)] * len(blocks)
    return pl.pallas_call(
        mark_body,
        in_specs=anywhere,
        out_specs=anywhere,
        out_shape=[jax.ShapeDtypeStruct(block.shape, block.dtype) for block in blocks],
        input_output_aliases={at: at for at in range(len(blocks))},
        compiler_params=params(),
        cost_estimate=cost(7e10, 4096),
        name="mark",
    )(*blocks)


def pick_body(below_ref, above_ref, first_ref, second_ref):
    count = first_ref.shape[0]
    first_ref[...] = below_ref[:count]
    second_ref[...] = above_ref[count:]


def pick(below, above):
    shape = jax.ShapeDtypeStruct((below.shape[0] // HALVES, below.shape[1]), below.dtype)
    return pl.pallas_call(
        pick_body,
        out_shape=[shape, shape],
        compiler_params=params(),
        cost_estimate=cost(1e8, 4 * below.size),
        name="pick",
    )(below, above)


def sums_body(shapes, *refs):
    outs = refs[-len(shapes) :]
    first = 0
    for out_ref, (offset, starts) in zip(outs, shapes):
        step = min(ref.shape[1] for ref in (out_ref, *refs[first : first + len(starts)]))
        for left in range(0, out_ref.shape[1], step):
            total = None
            for at, start in enumerate(starts):
                ref = refs[first + at]
                col = offset + left - start
                if 0 <= col < ref.shape[1]:
                    term = ref[:, col : col + step].astype(jnp.float32)
                    total = term if total is None else total + term
            out_ref[:, left : left + step] = total.astype(jnp.bfloat16)
        first += len(starts)


def sums(*groups, name="sums", after=()):
    args = [array for _, terms in groups for array, _ in terms]
    shapes = tuple((first, tuple(start for _, start in terms)) for (first, _), terms in groups)
    result = pl.pallas_call(
        functools.partial(sums_body, shapes),
        in_specs=[pl.BlockSpec(memory_space=pltpu.VMEM)] * len(args)
        + [pl.BlockSpec(memory_space=pl.ANY)] * len(after),
        out_shape=[
            jax.ShapeDtypeStruct((terms[0][0].shape[0], width), jnp.bfloat16)
            for (_, width), terms in groups
        ],
        compiler_params=params(16),
        cost_estimate=cost(sum(a.size for a in args), 3 * sum(a.size for a in args)),
        name=name,
    )(*args, *after)
    return result if len(groups) > 1 else result[0]


def terms_body(block_ref, codes_ref, exps_ref, *out_refs):
    scale = jnp.exp2(exps_ref[...].astype(jnp.float32))
    lane = lax.broadcasted_iota(jnp.int32, scale.shape, 1)
    count = codes_ref.shape[0]
    for at, out_ref in enumerate(out_refs):
        for side in range(2):
            block = block_ref[2 * at + side]
            cols = pl.ds(pl.multiple_of(block * HEAD, HEAD), HEAD)
            mine = jnp.sum(jnp.where(lane == block, scale, 0.0), axis=1, keepdims=True)
            out_ref[side * count : (side + 1) * count] = (
                codes_ref[:, cols].astype(jnp.float32) * mine
            ).astype(jnp.bfloat16)


def terms(blocks, codes, exps):
    count, width = codes.shape
    vmem = pl.BlockSpec(memory_space=pltpu.VMEM)
    return pl.pallas_call(
        terms_body,
        in_specs=[pl.BlockSpec(memory_space=pltpu.SMEM), vmem, vmem],
        out_shape=[jax.ShapeDtypeStruct((2 * count, HEAD), jnp.bfloat16)] * len(RING),
        compiler_params=params(),
        cost_estimate=cost(codes.size, 4 * codes.size),
        name="terms",
    )(blocks, codes, exps)


def outer_body(replicas, *refs):
    mine_refs, theirs_ref, momentum_ref, table_ref, momentum_out, rebuilt_ref = (
        refs[:3],
        *refs[3:],
    )
    table = table_ref[...]

    def rotate(values):
        return jnp.dot(
            values, table, precision=lax.Precision.HIGHEST, preferred_element_type=jnp.float32
        )

    summed = theirs_ref[...].astype(jnp.float32)
    for ref in mine_refs:
        summed += ref[: summed.shape[0]].astype(jnp.float32)
    averaged = rotate(summed / replicas)
    fresh = 0.9 * momentum_ref[...] + averaged
    momentum_out[...] = fresh
    turned = rotate(0.7 * (averaged + 0.9 * fresh))
    scales = (jnp.max(jnp.abs(turned), axis=-1, keepdims=True) + 1e-06).astype(jnp.bfloat16)
    scales = scales.astype(jnp.float32)
    codes = (turned / scales).astype(jnp.bfloat16)
    rebuilt_ref[...] = rotate(codes.astype(jnp.float32) * scales).astype(jnp.bfloat16)


def outer(mine, theirs, momentum, table, replicas):
    return pl.pallas_call(
        functools.partial(outer_body, replicas),
        out_shape=[
            jax.ShapeDtypeStruct(momentum.shape, jnp.float32),
            jax.ShapeDtypeStruct(momentum.shape, jnp.bfloat16),
        ],
        compiler_params=params(),
        cost_estimate=cost(40 * theirs.size * HEAD, 12 * theirs.size),
        name="outer",
    )(*mine, theirs, momentum, table)


def apply_body(block_ref, params_ref, *refs):
    rebuilt_refs, out_ref = refs[:-1], refs[-1]
    count = out_ref.shape[0]
    for at, rebuilt_ref in enumerate(rebuilt_refs):
        for side in range(2):
            cols = pl.ds(pl.multiple_of(block_ref[2 * at + side] * HEAD, HEAD), HEAD)
            rebuilt = rebuilt_ref[side * count : (side + 1) * count].astype(jnp.float32)
            out_ref[:, cols] = (params_ref[:, cols].astype(jnp.float32) - rebuilt).astype(
                jnp.bfloat16
            )


def apply(blocks, old, rebuilt):
    vmem = pl.BlockSpec(memory_space=pltpu.VMEM)
    return pl.pallas_call(
        apply_body,
        in_specs=[pl.BlockSpec(memory_space=pltpu.SMEM)] + [vmem] * (1 + len(rebuilt)),
        out_shape=jax.ShapeDtypeStruct(old.shape, jnp.bfloat16),
        compiler_params=params(),
        cost_estimate=cost(old.size, 6 * old.size),
        name="apply",
    )(blocks, old, *rebuilt)


def swap(block, axis):
    return lax.ppermute(block, axis, [(0, 1), (1, 0)])


def hop(block, axis, way):
    at = (0, 2, 1, 3) if axis == Y else (0, 1, 2, 3)
    return lax.ppermute(block, axis, [(at[i], at[(i + way) % 4]) for i in range(4)])


def add(*blocks):
    total = blocks[0].astype(jnp.float32)
    for block in blocks[1:]:
        total = total + block.astype(jnp.float32)
    return total.astype(jnp.bfloat16)


def wait(*blocks):
    return lax.optimization_barrier(blocks)


def tie(block, *others):
    return lax.optimization_barrier((block, *others))[0]


def local(
    tokens, norm_gain, query_weight, kv_weight, out_weight, pseudo_grad, grad_exps, old, momentum
):
    core, z, yhi = lax.axis_index("core"), lax.axis_index("z"), lax.axis_index("yhi")
    x, ylo = lax.axis_index("x"), lax.axis_index("ylo")
    replicas = lax.axis_size(REPLICA)
    place = jnp.stack([(yhi ^ side) * 4 + (z + r) % 4 for side in range(2) for r in RING])
    chip = jnp.arange(8, dtype=jnp.int32)
    away = (chip % 4 - z) % 4
    slots = ((chip // 4) ^ yhi) * 4 + jnp.where(away < 2, away, 5 - away)
    share = jnp.stack([((x + r) % 4) * 2 + (ylo ^ side) for r in RING for side in range(2)])
    core, place, slots, share = (
        v.astype(jnp.int32).reshape(-1) for v in (core, place, slots, share)
    )
    places = jnp.concatenate([place, slots])

    block, h1, h2 = normalize(tokens, norm_gain)
    relay1, relay2 = hop(h1, Y, 1), hop(h2, Y, -1)
    below, above = hop(block, "z", 1), hop(block, "z", -1)
    kv_theirs = swap(tie(kv_weight, block), "core")
    at0, at1, at3, at2 = terms(share, tie(pseudo_grad[0], block), grad_exps[0])
    relay1, relay2, kv_theirs, at0, at1, at2, at3, query_weight = wait(
        relay1, relay2, kv_theirs, at0, at1, at2, at3, query_weight
    )
    query_theirs = swap(query_weight, "core")
    partner = jnp.concatenate([hop(relay1, Y, 1), hop(relay2, Y, -1)], axis=0)
    below, above = mark(below, above)
    far1, far2 = pick(below, above)
    partner, above, below = wait(partner, above, below)
    far1, far2 = hop(far1, "z", 1), hop(far2, "z", -1)
    pbelow, pabove = hop(partner, "z", 1), hop(partner, "z", -1)
    weights = [query_weight, query_theirs, kv_weight, kv_theirs]
    query_a, pair_a = project(core, [block, above, below, far1, far2], weights)
    query_a, far1, far2, at2, at3 = wait(query_a, far1, far2, at2, at3)
    x2, x3 = hop(at2, "x", 1), hop(at3, "x", -1)
    pabove, pbelow, query_a, pair_a, x2, x3, at1, out_weight = wait(
        pabove, pbelow, query_a, pair_a, x2, x3, at1, out_weight
    )
    pfar1, pfar2 = pick(pbelow, pabove)
    pfar1, pfar2 = hop(pfar1, "z", 1), hop(pfar2, "z", -1)
    out_theirs = swap(out_weight, "core")
    query_m, pair_m = project(core, [partner, pabove, pbelow], weights)
    passed = hop(add(at1, x2), "x", 1)
    other_a, other_m = swap(pair_a, "core"), swap(pair_m, "core")
    pfar1, pfar2, passed, query_m = wait(pfar1, pfar2, passed, query_m)
    query_l, pair_l = project(core, [pfar1, pfar2], weights)
    other_l = swap(pair_l, "core")
    out_weights = (out_weight, out_theirs)
    mixed, q0, qup, qdown, far_a, far_b = attend(
        core,
        places,
        tuple(range(8)),
        (query_a, query_m, query_l),
        (pair_a, pair_m, pair_l),
        (other_a, other_m, other_l),
        out_weights,
    )

    full = out_weight.shape[1]
    half = full // HALVES
    mixed, far_a, far_b = wait(mixed, far_a, far_b)
    far_a, far_b = hop(far_a, "z", 1), hop(far_b, "z", -1)
    mine = (at0, passed, x3)
    count = momentum.shape[0]
    sent, q0, mixed = wait(add(*(part[count:] for part in mine)), q0, mixed)
    theirs = swap(sent, "ylo")
    o0, oup, odown, ofara, ofarb = output(mixed, out_weights)
    far_a, far_b, o0 = wait(far_a, far_b, o0)
    up, down = sums(
        ((0, full), ((qup, 0), (far_a, 0))), ((0, full), ((qdown, 0), (far_b, half)))
    )
    up, down, theirs, ofara, ofarb = wait(up, down, theirs, ofara, ofarb)
    up, down = hop(up, "z", 1), hop(down, "z", -1)
    ofara, ofarb = hop(ofara, "z", 1), hop(ofarb, "z", -1)
    new_momentum, rebuilt = outer(mine, theirs, momentum, hadamard_table(HEAD), replicas)
    beside = swap(rebuilt, "ylo")
    both = jnp.concatenate([rebuilt, beside], axis=0)
    before = hop(both, "x", 1)
    up, down, before, both = wait(up, down, before, both)
    s1, s2 = sums(
        *(((at, half), ((q0, 0), (up, 0), (down, 0))) for at in (0, half))
    )
    oup, odown = sums(
        ((0, full), ((oup, 0), (ofara, 0))),
        ((0, full), ((odown, 0), (ofarb, half))),
        after=(s1,),
    )
    oup, odown = hop(oup, "z", 1), hop(odown, "z", -1)
    s1, s2 = hop(s1, Y, 1), hop(s2, Y, -1)
    after = hop(both, "x", -1)
    s1, s2, before = wait(s1, s2, before)
    s1, s2 = hop(s1, Y, 1), hop(s2, Y, -1)
    ahead = hop(before, "x", 1)
    new_params = apply(share, old, [both, after, before, ahead])
    o0, new_params = wait(o0, new_params)
    attended = sums(
        ((0, full), ((o0, 0), (oup, 0), (odown, 0), (s1, 0), (s2, half))), name="finish"
    )
    return (attended, new_params, new_momentum)


def solution(mesh):
    fine = Mesh(mesh.devices.reshape(4, 2, 2, 4, 2), ("x", "ylo", "yhi", "z", "core"))
    every = REPLICA + TENSOR
    return jax.shard_map(
        local,
        mesh=fine,
        in_specs=(
            P(every, None),
            P(),
            P(None, TENSOR),
            P(None, TENSOR),
            P(TENSOR, None),
            P(REPLICA, TENSOR, None),
            P(REPLICA, TENSOR, None),
            P(TENSOR, None),
            P(TENSOR, REPLICA),
        ),
        out_specs=(P(every, None), P(TENSOR, None), P(TENSOR, REPLICA)),
        check_vma=False,
    )
```
